256 devices in a mesh: dp: 32 (over z_hi, x, y), graph: 8 (over z_lo, core).
Axes of the slice: x: 4, y: 4, z: 8 (z_hi: 2, z_lo: 4; z = z_hi * 4 + z_lo), core: 2. Of those that a mesh axis runs over, the one named last changes fastest.
Arguments:
- node_feats: bfloat16 [32, 512, 512], P('dp', 'graph'), may hold values from -6 to 6
- positions: float32 [32, 3, 512], P('dp', None, 'graph'), may hold values from -8 to 8
- edge_src: int32 [32, 2048], P('dp', 'graph'), may hold values from 0 to 511
- edge_dst: int32 [32, 2048], P('dp', 'graph'), may hold values from 0 to 511
- edge_count: int32 [32, 8], P('dp', 'graph'), may hold values from 64 to 256, as said below
- trip_in: int32 [32, 8192], P('dp', 'graph'), may hold values from 0 to 127
- trip_out: int32 [32, 8192], P('dp', 'graph'), may hold values from 0 to 127
- trip_count: int32 [32, 8], P('dp', 'graph'), may hold values from 256 to 1024, as said below
- graph_ids: int32 [32, 512], P('dp', 'graph'), may hold values from 0 to 15, never falling along the last dimension, each value on 1 to 64 neighbouring positions
- w_src: bfloat16 [512, 512], replicated, may hold values from -0.25 to 0.25
- w_dst: bfloat16 [512, 512], replicated, may hold values from -0.25 to 0.25
- w_radial: bfloat16 [128, 512], replicated, may hold values from -1 to 1
- w_trip: bfloat16 [512, 512], replicated, may hold values from -0.25 to 0.25
- w_out: bfloat16 [512, 512], replicated, may hold values from -0.25 to 0.25
- w_energy: bfloat16 [512], replicated, may hold values from -0.25 to 0.25
- energy_cot: float32 [32, 16], P('dp'), may hold values from -6 to 6
Outputs:
- energy: float32 [32, 16], P('dp')
- position_grad: float32 [32, 3, 512], P('dp', None, 'graph')
- node_grad: float32 [32, 512, 512], P('dp', 'graph')
- grad_src: float32 [512, 512], replicated
- grad_dst: float32 [512, 512], replicated
- grad_radial: float32 [128, 512], replicated
- grad_trip: float32 [512, 512], replicated
- grad_out: float32 [512, 512], replicated
- grad_energy: float32 [512], replicated
The draws below stay inside these ranges and needn't reach their ends.
Inputs may be any that keep to these rules, and one draw needn't show every extreme that they name: `edge_count`: the live slots of a device are the first ones of its shard; in every draw one device holds 256 live edges and one holds 64. `trip_count`: in every draw one device holds 1024 live triplets and one holds 256.
All inputs are finite; a program needn't handle non-finite values.
Results may differ from the reference program's by a relative error of at most 0.02.
Values may be sent and summed in bfloat16 or wider, within the bound.
No kernel may reach another device: no remote copies, remote signals or barrier semaphores. Data moves between devices by JAX's collectives and lax.ppermute only.
A program may use at most 64 MiB of HBM per device.

```python
import math
import jax
import jax.numpy as jnp
import numpy as np
from jax import lax

D = 512
K = 128
EBLK = 128
TPB = 512
NGRAPH = 16
AT_DEV = 64
E_DEV = 256
TR_DEV = 1024
BATCHES = 32
ATOMS = 512
EDGES = 2048
TRIPS = 8192
N_GRAPH = 8


def spread_counts(key, most):
    total = BATCHES * N_GRAPH
    base = jax.random.randint(key, (total,), most // 4, most + 1)
    order = jax.random.permutation(jax.random.fold_in(key, 7), total)
    base = jnp.where(order == 0, most, base)
    base = jnp.where(order == 1, most // 4, base)
    return base.reshape(BATCHES, N_GRAPH).astype(jnp.int32)


def draw_edge_count(key, part):
    key = jax.random.fold_in(key, 11)
    return spread_counts(key, E_DEV)


def draw_trip_count(key, part):
    key = jax.random.fold_in(key, 13)
    return spread_counts(key, TR_DEV)


def plant(values, rng, smallest, largest):
    longest = values.shape.index(max(values.shape))
    spots = []
    for shift in (0, 1):
        where = [jax.random.randint(jax.random.fold_in(rng, axis), (), 0, length) for axis, length in enumerate(values.shape)]
        where[longest] = (where[longest] + shift) % values.shape[longest]
        spots.append(tuple(where))
    return values.at[spots[0]].set(smallest).at[spots[1]].set(largest)


def level_of(own_key, dims, split, low, high):
    def one(position, blocks):
        heights = jax.random.uniform(jax.random.fold_in(jax.random.fold_in(own_key, 6), position), (blocks,), jnp.float32, low / len(split), high / len(split))
        return jnp.repeat(jnp.exp(heights), dims[position] // blocks).reshape((-1,) + (1,) * (len(dims) - position - 1))

    level = one(*split[0])
    for cut in split[1:]:
        level = level * one(*cut)
    return level


def length_profile(number_of, total, most, slope):
    weights = [(1 << 20) // math.isqrt(standing ** slope) + 1 for standing in range(2, number_of + 1)]
    rest, counts = total - most - (number_of - 1), [1] * (number_of - 1)
    while rest > 0:
        candidates = [i for i in range(number_of - 1) if counts[i] < most]
        mass, budget = sum([weights[i] for i in candidates]), rest
        for i in candidates:
            extra = min(most - counts[i], max(1, budget * weights[i] // mass), rest)
            counts[i] = counts[i] + extra
            rest = rest - extra
    return np.array([most] + counts)


def uneven_parts(key, count, total, most, lean):
    if count == 2:
        one = jax.random.randint(key, (), max(1, total - most), min(most, total - 1) + 1)
        return jnp.stack([one, total - one])
    lengths = jnp.asarray(length_profile(count, total, most, lean), jnp.int32)
    couples = (count - 1) // 2
    source_of, receiver = lengths[1:1 + 2 * couples:2], lengths[2:2 + 2 * couples:2]
    slack = jnp.minimum(source_of - 1, most - receiver)
    moved = jax.random.randint(jax.random.fold_in(key, 1), (couples,), 0, 1 << 20) % (slack + 1)
    lengths = lengths.at[1:1 + 2 * couples:2].set(source_of - moved).at[2:2 + 2 * couples:2].set(receiver + moved)
    return lengths[jax.random.permutation(jax.random.fold_in(key, 2), count)]


def scatter_about(rng, shape, scale, limit, pieces=(), kind=jnp.bfloat16):
    result = jax.random.normal(rng, shape, jnp.float32) * scale
    if len(pieces) > 0:
        result = level_of(rng, shape, pieces, -0.22, 0.18) * result
    return jnp.clip(result, min=-limit, max=limit).astype(kind)


def setup_inputs(seed: int = 0) -> dict:
    splits = jax.random.split(jax.random.key(seed), 17)
    return {
        "node_feats": scatter_about(splits[0], (BATCHES, ATOMS, D), 1.0, 6.0, ((0, 32), (1, 8))),
        "positions": scatter_about(splits[1], (BATCHES, 3, ATOMS), 2.5, 8.0, ((0, 32), (2, 8)), jnp.float32),
        "edge_src": plant(jax.random.randint(splits[2], (BATCHES, EDGES), 0, ATOMS), jax.random.fold_in(splits[2], 1), 0, ATOMS - 1).astype(jnp.int32),
        "edge_dst": plant(jax.random.randint(splits[3], (BATCHES, EDGES), 0, ATOMS), jax.random.fold_in(splits[3], 1), 0, ATOMS - 1).astype(jnp.int32),
        "edge_count": draw_edge_count(jax.random.fold_in(splits[16], 71), 0),
        "trip_in": plant(jax.random.randint(splits[5], (BATCHES, TRIPS), 0, EBLK), jax.random.fold_in(splits[5], 1), 0, EBLK - 1).astype(jnp.int32),
        "trip_out": plant(jax.random.randint(splits[6], (BATCHES, TRIPS), 0, EBLK), jax.random.fold_in(splits[6], 1), 0, EBLK - 1).astype(jnp.int32),
        "trip_count": draw_trip_count(jax.random.fold_in(splits[16], 71), 0),
        "graph_ids": jax.vmap(lambda own: jnp.searchsorted(jnp.cumsum(uneven_parts(own, NGRAPH, ATOMS, 2 * ATOMS // NGRAPH, 0)), jnp.arange(ATOMS), side="right"))(jax.random.split(splits[8], BATCHES)).reshape((BATCHES, ATOMS)).astype(jnp.int32),
        "w_src": scatter_about(splits[9], (D, D), D ** -0.5, 0.25),
        "w_dst": scatter_about(splits[10], (D, D), D ** -0.5, 0.25),
        "w_radial": scatter_about(splits[11], (K, D), (K // 4) ** -0.5, 1.0),
        "w_trip": scatter_about(splits[12], (D, D), D ** -0.5, 0.25),
        "w_out": scatter_about(splits[13], (D, D), D ** -0.5, 0.25),
        "w_energy": scatter_about(splits[14], (D,), D ** -0.5, 0.25),
        "energy_cot": scatter_about(splits[15], (BATCHES, NGRAPH), 1.0, 6.0, ((0, 32),), jnp.float32),
    }


def edge_forward(trip_in, trip_out, live_e, live_t, rows_src, rows_dst, pos_src, pos_dst, w_src, w_dst, w_radial, w_trip):
    vec = pos_dst - pos_src
    dist = jnp.sqrt(lax.optimization_barrier(jnp.sum(vec * vec, axis=0)) + 0.25)
    count = w_radial.shape[0]
    centers = jnp.arange(count, dtype=jnp.float32) * (16.0 / count)
    basis = jnp.exp(-jnp.square((dist[:, None] - centers[None, :]) * (count / 24.0))).astype(jnp.bfloat16)
    pre = jnp.dot(rows_src, w_src, preferred_element_type=jnp.float32) + jnp.dot(rows_dst, w_dst, preferred_element_type=jnp.float32)
    radial = jnp.dot(basis, w_radial, preferred_element_type=jnp.float32)
    message = (jax.nn.silu(pre) * radial * live_e[:, None]).astype(jnp.bfloat16)
    edges, width = message.shape
    blocks = edges // EBLK
    unit = (vec / dist[None, :]).reshape(3, blocks, EBLK)
    incoming = trip_in.reshape(blocks, TPB)
    outgoing = trip_out.reshape(blocks, TPB)
    slots = jnp.arange(EBLK, dtype=jnp.int32)
    pick_in = (incoming[:, :, None] == slots[None, None, :]).astype(jnp.bfloat16)
    pick_out = (outgoing[:, :, None] == slots[None, None, :]).astype(jnp.bfloat16)
    in_dir = jnp.take_along_axis(unit, jnp.broadcast_to(incoming[None], (3, blocks, TPB)), axis=2)
    out_dir = jnp.take_along_axis(unit, jnp.broadcast_to(outgoing[None], (3, blocks, TPB)), axis=2)
    cosine = lax.optimization_barrier(jnp.sum(in_dir * out_dir, axis=0)).reshape(-1)
    gathered = jnp.einsum('bte,bed->btd', pick_in, message.reshape(blocks, EBLK, width), preferred_element_type=jnp.float32).astype(jnp.bfloat16)
    projected = jnp.dot(gathered.reshape(-1, width), w_trip, preferred_element_type=jnp.float32)
    weighted = (projected * (cosine * live_t)[:, None]).astype(jnp.bfloat16).reshape(blocks, TPB, width)
    triplet = jnp.einsum('bte,btd->bed', pick_out, weighted, preferred_element_type=jnp.float32).reshape(edges, width)
    return (message.astype(jnp.float32) + triplet) * live_e[:, None]

def node_forward(h_float, agg, w_out, w_energy):
    out = jax.nn.silu(jnp.dot(agg.astype(jnp.bfloat16), w_out, preferred_element_type=jnp.float32))
    return lax.optimization_barrier(jnp.sum((h_float + out) * w_energy.astype(jnp.float32)[None, :], axis=1))

def reference(node_feats, positions, edge_src, edge_dst, edge_count, trip_in, trip_out, trip_count, graph_ids, w_src, w_dst, w_radial, w_trip, w_out, w_energy, energy_cot):
    edge_slots = jnp.arange(E_DEV, dtype=jnp.int32)
    trip_slots = jnp.arange(TR_DEV, dtype=jnp.int32)

    def one_batch(item):
        table, pos, src, dst, ecount, tin, tout, tcount, gid, cot = item
        src_s = src.reshape(N_GRAPH, E_DEV)
        dst_s = dst.reshape(N_GRAPH, E_DEV)
        tin_s = tin.reshape(N_GRAPH, TR_DEV)
        tout_s = tout.reshape(N_GRAPH, TR_DEV)
        live_e = (edge_slots[None, :] < ecount[:, None]).astype(jnp.float32)
        live_t = (trip_slots[None, :] < tcount[:, None]).astype(jnp.float32)
        shards = (src_s, dst_s, tin_s, tout_s, live_e, live_t)

        def forward_shard(piece):
            s_src, s_dst, s_tin, s_tout, s_le, s_lt = piece
            update = edge_forward(s_tin, s_tout, s_le, s_lt, table[s_src], table[s_dst], pos[:, s_src], pos[:, s_dst], w_src, w_dst, w_radial, w_trip)
            return jax.ops.segment_sum(update, s_dst, num_segments=ATOMS)
        agg = lax.optimization_barrier(jnp.sum(lax.map(forward_shard, shards), axis=0))
        onehot = (gid[:, None] == jnp.arange(NGRAPH, dtype=jnp.int32)[None, :]).astype(jnp.float32)
        cot_atom = lax.optimization_barrier(jnp.sum(onehot * cot[None, :], axis=1))

        def node_shard(piece):
            h_own, agg_own, cot_own = piece
            atom_energy, back = jax.vjp(node_forward, h_own.astype(jnp.float32), agg_own, w_out, w_energy)
            direct, agg_grad, g_out, g_energy = back(cot_own)
            return (atom_energy, direct, agg_grad, g_out.astype(jnp.float32), g_energy.astype(jnp.float32))
        atom_energy, direct, agg_grad, g_out, g_energy = lax.map(node_shard, (table.reshape(N_GRAPH, AT_DEV, -1), agg.reshape(N_GRAPH, AT_DEV, -1), cot_atom.reshape(N_GRAPH, AT_DEV)))
        energy = lax.optimization_barrier(jnp.sum(onehot * atom_energy.reshape(ATOMS)[:, None], axis=0))
        agg_cot = agg_grad.reshape(ATOMS, -1).astype(jnp.bfloat16)

        def backward_shard(piece):
            s_src, s_dst, s_tin, s_tout, s_le, s_lt = piece

            def local(rows_src, rows_dst, pos_src, pos_dst, a, b, c, d):
                return edge_forward(s_tin, s_tout, s_le, s_lt, rows_src, rows_dst, pos_src, pos_dst, a, b, c, d)
            update, back = jax.vjp(local, table[s_src], table[s_dst], pos[:, s_src], pos[:, s_dst], w_src, w_dst, w_radial, w_trip)
            d_rs, d_rd, d_ps, d_pd, g_s, g_d, g_r, g_t = back(agg_cot[s_dst].astype(jnp.float32))
            node_part = jax.ops.segment_sum(d_rs.astype(jnp.float32), s_src, num_segments=ATOMS) + jax.ops.segment_sum(d_rd.astype(jnp.float32), s_dst, num_segments=ATOMS)
            pos_part = (jax.ops.segment_sum(d_ps.T, s_src, num_segments=ATOMS) + jax.ops.segment_sum(d_pd.T, s_dst, num_segments=ATOMS)).T
            return (node_part, pos_part, g_s.astype(jnp.float32), g_d.astype(jnp.float32), g_r.astype(jnp.float32), g_t.astype(jnp.float32))
        node_part, pos_part, g_s, g_d, g_r, g_t = lax.map(backward_shard, shards)
        node_grad = direct.reshape(ATOMS, -1) + lax.optimization_barrier(jnp.sum(node_part, axis=0))
        pos_grad = lax.optimization_barrier(jnp.sum(pos_part, axis=0))
        return (energy, pos_grad, node_grad, lax.optimization_barrier(jnp.sum(g_s, 0)), lax.optimization_barrier(jnp.sum(g_d, 0)), lax.optimization_barrier(jnp.sum(g_r, 0)), lax.optimization_barrier(jnp.sum(g_t, 0)), lax.optimization_barrier(jnp.sum(g_out, 0)), lax.optimization_barrier(jnp.sum(g_energy, 0)))
    outs = lax.map(one_batch, (node_feats, positions, edge_src, edge_dst, edge_count, trip_in, trip_out, trip_count, graph_ids, energy_cot))
    energy, pos_grad, node_grad, g_s, g_d, g_r, g_t, g_o, g_e = outs
    return (energy, pos_grad, node_grad, lax.optimization_barrier(jnp.sum(g_s, 0)), lax.optimization_barrier(jnp.sum(g_d, 0)), lax.optimization_barrier(jnp.sum(g_r, 0)), lax.optimization_barrier(jnp.sum(g_t, 0)), lax.optimization_barrier(jnp.sum(g_o, 0)), lax.optimization_barrier(jnp.sum(g_e, 0)))
```

```python
import jax
import jax.numpy as jnp
from jax import lax
from jax.experimental import pallas as pl
from jax.experimental.pallas import tpu as pltpu
from jax.sharding import PartitionSpec as P

BF = jnp.bfloat16
F32 = jnp.float32
NG = 8
AT = 64
ATOMS = 512
ES = 256
EDGES = 2048
D = 512
K = 128
BLK = 128
TPB = 512
PIECE = 80
CH = 40
AXES = ("dp", "graph")
HI = lax.Precision.HIGHEST


def nn(a, b):
    return lax.dot_general(a, b, (((1,), (0,)), ((), ())), preferred_element_type=F32)


def nt(a, b):
    return lax.dot_general(a, b, (((1,), (1,)), ((), ())), preferred_element_type=F32)


def tn(a, b):
    return lax.dot_general(a, b, (((0,), (0,)), ((), ())), preferred_element_type=F32)


def pack_kernel(me_ref, h_ref, pos_ref, src_ref, dst_ref, ec_ref, tin_ref, tout_ref, tc_ref, gid_ref, out_ref, meta):
    odd = lax.rem(me_ref[0], 2)
    out_ref[0:AT, :] = h_ref[...]

    def place(row):
        full = jnp.concatenate([row, jnp.zeros_like(row)], axis=1)
        return jnp.where(odd == 1, pltpu.roll(full, AT, 1), full)

    for r, ref in ((0, src_ref), (1, dst_ref)):
        v = ref[...]
        half = lax.shift_right_logical(v, 1)
        meta[r : r + 1, 0:ES] = half.astype(F32)
        meta[r : r + 1, ES : 2 * ES] = (v - 2 * half).astype(F32)
    for r, ref in ((2, tin_ref), (4, tout_ref)):
        v = ref[...].astype(F32)
        meta[r : r + 1, :] = v[:, 0:TPB]
        meta[r + 1 : r + 2, :] = v[:, TPB : 2 * TPB]
    p = pos_ref[...]
    p1 = p.astype(BF).astype(F32)
    p2 = (p - p1).astype(BF).astype(F32)
    p3 = (p - p1) - p2
    meta[6:16, :] = jnp.zeros((10, D), F32)
    meta[6:9, 0:128] = place(p1)
    meta[9:12, 0:128] = place(p2)
    meta[12:15, 0:128] = place(p3)
    meta[15:16, 0:128] = place(gid_ref[...].astype(F32))
    tc = tc_ref[0, 0]
    tc_half = lax.shift_right_logical(tc, 3)
    meta[15:16, 128:256] = jnp.full((1, 128), ec_ref[0, 0].astype(F32))
    meta[15:16, 256:384] = jnp.full((1, 128), tc_half.astype(F32))
    meta[15:16, 384:512] = jnp.full((1, 128), (tc - 8 * tc_half).astype(F32))
    out_ref[AT:PIECE, :] = meta[...].astype(BF)


def pack(me, h, pos, src, dst, ec, tin, tout, tc, gid):
    vm = pl.BlockSpec(memory_space=pltpu.VMEM)
    sm = pl.BlockSpec(memory_space=pltpu.SMEM)
    return pl.pallas_call(
        pack_kernel,
        out_shape=jax.ShapeDtypeStruct((PIECE, D), BF),
        in_specs=[sm, vm, vm, vm, vm, sm, vm, vm, sm, vm],
        out_specs=vm,
        scratch_shapes=[pltpu.VMEM((16, D), F32)],
        name="pack",
    )(me, h, pos, src, dst, ec, tin, tout, tc, gid)


def main_kernel(
    me_ref,
    gat_ref,
    ws_ref,
    wd_ref,
    wr_ref,
    wt_ref,
    wo_ref,
    we_ref,
    ecot_ref,
    energy_ref,
    pos_out_ref,
    node_ref,
    pay_ref,
    h_s,
    ab_s,
    posp_s,
    oht_s,
    ohd_s,
    geo_s,
    msg_s,
    f_s,
    sg_s,
    m2_s,
    n_s,
    tt_s,
    upd_s,
    aggb_s,
    dzb_s,
    ac_s,
    cot_s,
    ge_s,
    bt_s,
    dm2_s,
    dpre_s,
    drad_s,
    dv_s,
    a_s,
    b_s,
    r_s,
):
    me = me_ref[0]
    gid_rows = []
    for j in range(4):
        first, second = gat_ref[2 * j, AT:PIECE, 0:128], gat_ref[2 * j + 1, AT:PIECE, 0:128]
        both = first.astype(F32) + second.astype(F32)
        posp_s[:, 128 * j : 128 * (j + 1)] = both.astype(BF)
        gid_rows.append(both[15:16, :])
    for s in range(NG):
        h_s[AT * s : AT * (s + 1), :] = gat_ref[s, 0:AT, :]
    gid_row = jnp.concatenate(gid_rows, axis=1)
    gid_col = jnp.transpose(jnp.broadcast_to(gid_row, (8, ATOMS)))[:, 0:1]
    h = h_s[...]
    ab_s[0:ATOMS, :] = nn(h, ws_ref[...]).astype(BF)
    ab_s[ATOMS : 2 * ATOMS, :] = nn(h, wd_ref[...]).astype(BF)

    step = 16.0 / K
    inv_width = K / 24.0
    sub_a = lax.broadcasted_iota(jnp.int32, (ATOMS, ES), 0).astype(F32)
    lane_a = lax.broadcasted_iota(jnp.int32, (ES, ATOMS), 1).astype(F32)
    sub_b = lax.broadcasted_iota(jnp.int32, (BLK, TPB), 0).astype(F32)
    lane_e = lax.broadcasted_iota(jnp.int32, (1, ES), 1).astype(F32)
    lane_t = lax.broadcasted_iota(jnp.int32, (1, TPB), 1).astype(F32)
    centers = lax.broadcasted_iota(jnp.int32, (1, K), 1).astype(F32) * step

    def onehot(cond):
        return jnp.where(cond, 1.0, 0.0).astype(BF)

    def forward(s, carry):
        meta = gat_ref[s, AT:PIECE, :].astype(F32)
        src = 2.0 * meta[0:1, 0:ES] + meta[0:1, ES : 2 * ES]
        dst = 2.0 * meta[1:2, 0:ES] + meta[1:2, ES : 2 * ES]
        ec = meta[15:16, 128:256]
        tc = 8.0 * meta[15:16, 256:384] + meta[15:16, 384:512]
        live = jnp.where(lane_e < jnp.concatenate([ec, ec], axis=1), 1.0, 0.0)
        lanes = pl.ds(pl.multiple_of(s * ES, ES), ES)
        ohts = onehot(sub_a == src)
        ohtd = onehot(sub_a == dst)
        oht_s[0:ATOMS, lanes] = ohts
        oht_s[ATOMS : 2 * ATOMS, lanes] = ohtd
        posp = posp_s[...]
        ps = nn(posp, ohts)
        pd = nn(posp, ohtd)
        ps = (ps[6:9] + ps[9:12]) + ps[12:15]
        pd = (pd[6:9] + pd[9:12]) + pd[12:15]
        vec = pd - ps
        sq = vec * vec
        dist = jnp.sqrt(sq[0:1] + sq[1:2] + sq[2:3] + 0.25)
        inv = 1.0 / dist
        unit = vec * inv
        geo = jnp.concatenate([src, dst, live, dist, unit, inv], axis=0)
        geo_s[s] = geo
        cols = jnp.transpose(geo)
        ohs = onehot(lane_a == cols[:, 0:1])
        ohd = onehot(lane_a == cols[:, 1:2])
        ohd_s[s] = ohd
        t = (cols[:, 3:4] - centers) * inv_width
        basis = jnp.exp(-(t * t)).astype(BF)
        bt_s[:, lanes] = jnp.transpose(basis.astype(F32)).astype(BF)
        pre = nn(ohs, ab_s[0:ATOMS, :]) + nn(ohd, ab_s[ATOMS : 2 * ATOMS, :])
        radial = nn(basis, wr_ref[...]) * cols[:, 2:3]
        sig = 0.5 + 0.5 * jnp.tanh(0.5 * pre)
        sil = pre * sig
        msg = (sil * radial).astype(BF)
        msg_s[s] = msg
        f_s[s] = (radial * (sig + sil * (1.0 - sig))).astype(BF)
        sg_s[s] = (sil * cols[:, 2:3]).astype(BF)
        m2 = nn(msg, wt_ref[...]).astype(BF)
        m2_s[s] = m2
        for i in range(2):
            rows = slice(BLK * i, BLK * (i + 1))
            limit = jnp.concatenate([tc] * 4, axis=1) - float(TPB * i)
            tin = meta[2 + i : 3 + i, :]
            tout = jnp.where(lane_t < limit, meta[4 + i : 5 + i, :], -1.0)
            pick_in = onehot(sub_b == tin)
            pick_out = onehot(sub_b == tout)
            count = nt(pick_out, pick_in) * cols[rows, 2:3]
            n_s[2 * s + i] = count
            gram = (
                cols[rows, 4:5] * unit[0:1, rows]
                + cols[rows, 5:6] * unit[1:2, rows]
                + cols[rows, 6:7] * unit[2:3, rows]
            )
            mix = count * gram
            tt_s[2 * s + i] = jnp.transpose(mix).astype(BF)
            upd = msg[rows].astype(F32) + nn(mix.astype(BF), m2[rows])
            upd_s[pl.ds(pl.multiple_of(s * ES + BLK * i, BLK), BLK), :] = upd.astype(BF)
        return carry

    lax.fori_loop(0, NG, forward, 0)

    agg = nn(oht_s[ATOMS : 2 * ATOMS, :], upd_s[...]).astype(BF)
    aggb_s[...] = agg
    z = nn(agg, wo_ref[...])
    sig = 0.5 + 0.5 * jnp.tanh(0.5 * z)
    out = z * sig
    we = we_ref[...].astype(F32)
    x = h_s[...].astype(F32) + out
    atom_energy = jnp.sum(x * we, axis=1, keepdims=True)
    member = jnp.where(
        lax.broadcasted_iota(jnp.int32, (ATOMS, 128), 1).astype(F32) == gid_col, 1.0, 0.0
    )
    energy_ref[...] = jnp.sum(member * atom_energy, axis=0, keepdims=True)
    cot = jnp.sum(member * ecot_ref[...], axis=1, keepdims=True)
    cot_s[...] = jnp.broadcast_to(cot, (ATOMS, 128))
    ge_s[...] = jnp.sum(x * cot, axis=0, keepdims=True)
    dz = (cot * we * (sig + out * (1.0 - sig))).astype(BF)
    dzb_s[...] = dz
    ac_s[...] = nt(dz, wo_ref[...]).astype(BF)

    def backward(s, carry):
        lanes = pl.ds(pl.multiple_of(s * ES, ES), ES)
        edges = pl.ds(pl.multiple_of(s * ES, ES), ES)
        geo = geo_s[s]
        cols = jnp.transpose(geo)
        ug = nn(ohd_s[s], ac_s[...])
        ugb = ug.astype(BF)
        m2 = m2_s[s]
        halves, turns = [], []
        for i in range(2):
            rows = slice(BLK * i, BLK * (i + 1))
            halves.append(nn(tt_s[2 * s + i], ugb[rows]).astype(BF))
            dgram = n_s[2 * s + i] * nt(ugb[rows], m2[rows])
            both = dgram + jnp.transpose(dgram)
            turns.append(
                lax.dot_general(
                    geo[:, rows], both, (((1,), (0,)), ((), ())), precision=HI, preferred_element_type=F32
                )
            )
        dm2 = jnp.concatenate(halves, axis=0)
        dm2_s[edges, :] = dm2
        dmsg = ug + nt(dm2, wt_ref[...])
        dpre_s[edges, :] = (dmsg * f_s[s].astype(F32)).astype(BF)
        drad = (dmsg * sg_s[s].astype(F32)).astype(BF)
        drad_s[edges, :] = drad
        t = (cols[:, 3:4] - centers) * inv_width
        slope = nt(drad, wr_ref[...]) * jnp.exp(-(t * t)) * (t * (-2.0 * inv_width))
        ddist = jnp.sum(jnp.transpose(slope), axis=0, keepdims=True)
        unit = geo[4:7]
        du = jnp.concatenate(turns, axis=1)[4:7]
        along = du * unit
        along = along[0:1] + along[1:2] + along[2:3]
        dv = geo[7:8] * (du - unit * along) + unit * ddist
        top = dv.astype(BF).astype(F32)
        dv_s[:, lanes] = jnp.concatenate(
            [top, dv - top, jnp.zeros((10, ES), F32)], axis=0
        ).astype(BF)
        return carry

    lax.fori_loop(0, NG, backward, 0)

    own = pl.multiple_of(me * AT, AT)
    ohs_own = oht_s[pl.ds(own, AT), :]
    ohd_own = oht_s[pl.ds(ATOMS + own, AT), :]
    dpre = dpre_s[...]
    s_src = nn(ohs_own, dpre).astype(BF)
    s_dst = nn(ohd_own, dpre).astype(BF)
    node_ref[...] = (
        cot_s[pl.ds(own, AT), 0:1] * we + nt(s_src, ws_ref[...]) + nt(s_dst, wd_ref[...])
    )
    pos = nt(dv_s[...], ohd_own) - nt(dv_s[...], ohs_own)
    pos_out_ref[...] = pos[0:3] + pos[3:6]

    group = lax.div(me, 4)
    block = pl.ds(pl.multiple_of(lax.rem(me, 4) * 128, 128), 128)
    side = pl.ds(pl.multiple_of(group * ATOMS, ATOMS), ATOMS)
    rows_t = tn(h_s[:, block], oht_s[side, :]).astype(BF)
    a_s[...] = nn(rows_t, dpre)

    @pl.when(group == 0)
    def _():
        for_trip = [msg_s[s, :, block] for s in range(NG)]
        b_s[...] = tn(jnp.concatenate(for_trip, axis=0), dm2_s[...])

    @pl.when(group == 1)
    def _():
        b_s[...] = tn(aggb_s[:, block], dzb_s[...])

    r_s[...] = nn(bt_s[pl.ds(pl.multiple_of(me * 16, 16), 16), :], drad_s[...])
    ge = ge_s[:, block]
    for d in range(32):
        rows, cols = 16 * (d // 4), slice(128 * (d % 4), 128 * (d % 4) + 128)
        two = 2 * (d // 4)
        pay_ref[d] = jnp.concatenate(
            [
                a_s[rows : rows + 16, cols],
                b_s[rows : rows + 16, cols],
                r_s[two : two + 2, cols],
                ge,
                jnp.zeros((5, 128), F32),
            ],
            axis=0,
        ).astype(BF)


def batch(me, gat, ws, wd, wr, wt, wo, we, ecot):
    vm = pl.BlockSpec(memory_space=pltpu.VMEM)
    sm = pl.BlockSpec(memory_space=pltpu.SMEM)
    V = pltpu.VMEM
    return pl.pallas_call(
        main_kernel,
        out_shape=(
            jax.ShapeDtypeStruct((1, 128), F32),
            jax.ShapeDtypeStruct((3, AT), F32),
            jax.ShapeDtypeStruct((AT, D), F32),
            jax.ShapeDtypeStruct((32, CH, 128), BF),
        ),
        in_specs=[sm] + [vm] * 8,
        out_specs=(vm, vm, vm, vm),
        scratch_shapes=[
            V((ATOMS, D), BF),
            V((2 * ATOMS, D), BF),
            V((16, ATOMS), BF),
            V((2 * ATOMS, EDGES), BF),
            V((NG, ES, ATOMS), BF),
            V((NG, 8, ES), F32),
            V((NG, ES, D), BF),
            V((NG, ES, D), BF),
            V((NG, ES, D), BF),
            V((NG, ES, D), BF),
            V((2 * NG, BLK, BLK), F32),
            V((2 * NG, BLK, BLK), BF),
            V((EDGES, D), BF),
            V((ATOMS, D), BF),
            V((ATOMS, D), BF),
            V((ATOMS, D), BF),
            V((ATOMS, 128), F32),
            V((1, D), F32),
            V((K, EDGES), BF),
            V((EDGES, D), BF),
            V((EDGES, D), BF),
            V((EDGES, D), BF),
            V((16, EDGES), BF),
            V((BLK, D), F32),
            V((BLK, D), F32),
            V((16, D), F32),
        ],
        compiler_params=pltpu.CompilerParams(vmem_limit_bytes=50 * 1024 * 1024),
        name="batch",
    )(me, gat, ws, wd, wr, wt, wo, we, ecot)


def sum_kernel(in_ref, out_ref):
    total = in_ref[0].astype(F32)
    for d in range(1, 32):
        total = total + in_ref[d].astype(F32)
    out_ref[...] = total.astype(BF)


def chunk_sum(x):
    vm = pl.BlockSpec(memory_space=pltpu.VMEM)
    return pl.pallas_call(
        sum_kernel,
        out_shape=jax.ShapeDtypeStruct((CH, 128), BF),
        in_specs=[vm],
        out_specs=vm,
        name="chunk_sum",
    )(x)


def place_kernel(me_ref, own_ref, other_ref, gs_ref, gd_ref, gr_ref, gt_ref, go_ref, ge_ref, pairs):
    z, x, y, core = me_ref[0], me_ref[1], me_ref[2], me_ref[3]

    for c, ref in ((0, own_ref), (1, other_ref)):

        def body(i, carry, c=c, ref=ref):
            kx, ky, kz = lax.div(i, 32), lax.rem(lax.div(i, 8), 4), lax.rem(i, 8)
            px = lax.rem(x - kx + 4, 4)
            py = lax.rem(y - ky + 4, 4)
            pz = lax.rem(z - kz + 8, 8)
            pc = lax.rem(core + c, 2)
            d = lax.div(pz, 4) * 16 + px * 4 + py
            g = lax.rem(pz, 4) * 2 + pc
            tile = ref[i].astype(F32)
            cols = pl.ds(pl.multiple_of(lax.rem(d, 4) * 128, 128), 128)
            high = lax.div(d, 4)
            rows = pl.ds(pl.multiple_of(lax.rem(g, 4) * 128 + high * 16, 16), 16)

            @pl.when(g < 4)
            def _():
                gs_ref[rows, cols] = tile[0:16]
                gt_ref[rows, cols] = tile[16:32]

            @pl.when(g >= 4)
            def _():
                gd_ref[rows, cols] = tile[0:16]
                go_ref[rows, cols] = tile[16:32]

            pairs[g * 8 + high, :, cols] = tile[32:40]

            @pl.when((g < 4) & (d == 0))
            def _():
                ge_ref[:, pl.ds(pl.multiple_of(lax.rem(g, 4) * 128, 128), 128)] = tile[34:35]

            return carry

        lax.fori_loop(0, 128, body, 0)
    for i in range(K // 2):
        gr_ref[2 * i : 2 * i + 2, :] = pairs[i, 0:2, :]


def place(where, own, other):
    vm = pl.BlockSpec(memory_space=pltpu.VMEM)
    sm = pl.BlockSpec(memory_space=pltpu.SMEM)
    big = jax.ShapeDtypeStruct((D, D), F32)
    return pl.pallas_call(
        place_kernel,
        out_shape=(big, big, jax.ShapeDtypeStruct((K, D), F32), big, big, jax.ShapeDtypeStruct((1, D), F32)),
        in_specs=[sm, vm, vm],
        out_specs=(vm,) * 6,
        scratch_shapes=[pltpu.VMEM((K // 2, 8, D), F32)],
        compiler_params=pltpu.CompilerParams(vmem_limit_bytes=40 * 1024 * 1024),
        name="place",
    )(where, own, other)


def moves(fn):
    pairs = []
    for zh in range(2):
        for x in range(4):
            for y in range(4):
                for zl in range(4):
                    for c in range(2):
                        z = zh * 4 + zl
                        z2, x2, y2, c2 = fn(z, x, y, c)
                        here = (zh * 16 + x * 4 + y) * 8 + zl * 2 + c
                        there = ((z2 // 4) * 16 + x2 * 4 + y2) * 8 + (z2 % 4) * 2 + c2
                        pairs.append((here, there))
    return pairs


def rotate(v, axis, k):
    if axis == "z":
        fn = lambda z, x, y, c: ((z + k) % 8, x, y, c)
    elif axis == "x":
        fn = lambda z, x, y, c: (z, (x + k) % 4, y, c)
    elif axis == "y":
        fn = lambda z, x, y, c: (z, x, (y + k) % 4, c)
    else:
        fn = lambda z, x, y, c: (z, x, y, 1 - c)
    return lax.ppermute(v, AXES, moves(fn))


def spread(v, axis, n):
    return jnp.concatenate([v] + [rotate(v, axis, k) for k in range(1, n)], axis=0)


def per_device(
    node_feats,
    positions,
    edge_src,
    edge_dst,
    edge_count,
    trip_in,
    trip_out,
    trip_count,
    graph_ids,
    w_src,
    w_dst,
    w_radial,
    w_trip,
    w_out,
    w_energy,
    energy_cot,
):
    dp, graph = lax.axis_index("dp"), lax.axis_index("graph")
    me = graph.reshape(1).astype(jnp.int32)
    piece = pack(
        me,
        node_feats[0],
        positions[0],
        edge_src,
        edge_dst,
        edge_count,
        trip_in,
        trip_out,
        trip_count,
        graph_ids,
    )
    gathered = lax.all_gather(piece, "graph", axis=0, tiled=False)
    ecot = jnp.pad(energy_cot, ((0, 0), (0, 128 - energy_cot.shape[1])))
    energy, pos_grad, node_grad, payload = batch(
        me, gathered, w_src, w_dst, w_radial, w_trip, w_out, w_energy.reshape(1, D), ecot
    )
    arrived = lax.all_to_all(payload, "dp", 0, 0, tiled=True)
    chunk = chunk_sum(arrived)
    part = spread(chunk[None], "z", 8)
    part = spread(part, "y", 4)
    part = spread(part, "x", 4)
    other = rotate(part, "core", 1)
    where = jnp.stack(
        [
            lax.div(dp, 16) * 4 + lax.div(graph, 2),
            lax.rem(lax.div(dp, 4), 4),
            lax.rem(dp, 4),
            lax.rem(graph, 2),
        ]
    ).astype(jnp.int32)
    gs, gd, gr, gt, go, ge = place(where, part, other)
    return (
        energy[:, 0 : energy_cot.shape[1]],
        pos_grad[None],
        node_grad[None],
        gs,
        gd,
        gr,
        gt,
        go,
        ge.reshape(D),
    )


def solution(mesh):
    placed = (
        P("dp", "graph", None),
        P("dp", None, "graph"),
        P("dp", "graph"),
        P("dp", "graph"),
        P("dp", "graph"),
        P("dp", "graph"),
        P("dp", "graph"),
        P("dp", "graph"),
        P("dp", "graph"),
        P(),
        P(),
        P(),
        P(),
        P(),
        P(),
        P("dp", None),
    )
    return jax.shard_map(
        per_device,
        mesh=mesh,
        in_specs=placed,
        out_specs=(
            P("dp", None),
            P("dp", None, "graph"),
            P("dp", "graph", None),
            P(),
            P(),
            P(),
            P(),
            P(),
            P(),
        ),
        check_vma=False,
    )
```

```python
import jax
import jax.numpy as jnp
from jax import lax
from jax.experimental import pallas as pl
from jax.experimental.pallas import tpu as pltpu
from jax.sharding import PartitionSpec as P

BF = jnp.bfloat16
F32 = jnp.float32
NG = 8
AT = 64
ATOMS = 512
ES = 256
EDGES = 2048
D = 512
K = 128
BLK = 128
TPB = 512
PIECE = 80
CH = 80
AXES = ("dp", "graph")
HI = lax.Precision.HIGHEST


def nn(a, b):
    return lax.dot_general(a, b, (((1,), (0,)), ((), ())), preferred_element_type=F32)


def nt(a, b):
    return lax.dot_general(a, b, (((1,), (1,)), ((), ())), preferred_element_type=F32)


def tn(a, b):
    return lax.dot_general(a, b, (((0,), (0,)), ((), ())), preferred_element_type=F32)


def pack_kernel(me_ref, h_ref, pos_ref, src_ref, dst_ref, ec_ref, tin_ref, tout_ref, tc_ref, gid_ref, out_ref, meta, pos_v, sem):
    fetch = pltpu.make_async_copy(pos_ref, pos_v, sem)
    fetch.start()
    odd = lax.rem(me_ref[0], 2)
    out_ref[0:AT, :] = h_ref[...]

    def place(row):
        full = jnp.concatenate([row, jnp.zeros_like(row)], axis=1)
        return jnp.where(odd == 1, pltpu.roll(full, AT, 1), full)

    for r, ref in ((0, src_ref), (1, dst_ref)):
        v = ref[...]
        half = lax.shift_right_logical(v, 1)
        meta[r : r + 1, 0:ES] = half.astype(F32)
        meta[r : r + 1, ES : 2 * ES] = (v - 2 * half).astype(F32)
    for r, ref in ((2, tin_ref), (4, tout_ref)):
        v = ref[...].astype(F32)
        meta[r : r + 1, :] = v[:, 0:TPB]
        meta[r + 1 : r + 2, :] = v[:, TPB : 2 * TPB]
    fetch.wait()
    p = jnp.concatenate([pos_v[i] for i in range(3)], axis=0)
    p1 = p.astype(BF).astype(F32)
    p2 = (p - p1).astype(BF).astype(F32)
    p3 = (p - p1) - p2
    meta[6:16, :] = jnp.zeros((10, D), F32)
    meta[6:9, 0:128] = place(p1)
    meta[9:12, 0:128] = place(p2)
    meta[12:15, 0:128] = place(p3)
    meta[15:16, 0:128] = place(gid_ref[...].astype(F32))
    tc = tc_ref[0, 0]
    tc_half = lax.shift_right_logical(tc, 3)
    meta[15:16, 128:256] = jnp.full((1, 128), ec_ref[0, 0].astype(F32))
    meta[15:16, 256:384] = jnp.full((1, 128), tc_half.astype(F32))
    meta[15:16, 384:512] = jnp.full((1, 128), (tc - 8 * tc_half).astype(F32))
    out_ref[AT:PIECE, :] = meta[...].astype(BF)


def pack(me, h, pos, src, dst, ec, tin, tout, tc, gid):
    vm = pl.BlockSpec(memory_space=pltpu.VMEM)
    sm = pl.BlockSpec(memory_space=pltpu.SMEM)
    return pl.pallas_call(
        pack_kernel,
        out_shape=jax.ShapeDtypeStruct((PIECE, D), BF),
        in_specs=[sm, vm, pl.BlockSpec(memory_space=pl.ANY), vm, vm, sm, vm, vm, sm, vm],
        out_specs=vm,
        scratch_shapes=[pltpu.VMEM((16, D), F32), pltpu.VMEM((3, 1, AT), F32), pltpu.SemaphoreType.DMA],
        name="pack",
    )(me, h, pos, src, dst, ec, tin, tout, tc, gid)


def main_kernel(
    me_ref,
    gat_ref,
    ws_hbm,
    wd_hbm,
    wr_hbm,
    wt_hbm,
    wo_hbm,
    we_ref,
    ecot_ref,
    energy_ref,
    pos_out_ref,
    node_ref,
    pay_ref,
    h_s,
    ab_s,
    posp_s,
    oht_s,
    ohd_s,
    geo_s,
    msg_s,
    f_s,
    sg_s,
    m2_s,
    n_s,
    tt_s,
    upd_s,
    aggb_s,
    dzb_s,
    ac_s,
    cot_s,
    ge_s,
    bt_s,
    dm2_s,
    dpre_s,
    drad_s,
    dv_s,
    a_s,
    b_s,
    r_s,
    ws_ref,
    wd_ref,
    wr_ref,
    wt_ref,
    wo_ref,
    sems,
):
    loads = [
        pltpu.make_async_copy(far, near, sems.at[i])
        for i, (far, near) in enumerate(
            ((ws_hbm, ws_ref), (wd_hbm, wd_ref), (wr_hbm, wr_ref), (wt_hbm, wt_ref), (wo_hbm, wo_ref))
        )
    ]
    for load in loads:
        load.start()
    me, my_u, my_v = me_ref[0], me_ref[1], me_ref[2]
    gid_rows = []
    for j in range(4):
        first, second = gat_ref[me ^ (2 * j), AT:PIECE, 0:128], gat_ref[me ^ (2 * j + 1), AT:PIECE, 0:128]
        both = first.astype(F32) + second.astype(F32)
        posp_s[:, 128 * j : 128 * (j + 1)] = both.astype(BF)
        gid_rows.append(both[15:16, :])
    for s in range(NG):
        h_s[AT * s : AT * (s + 1), :] = gat_ref[me ^ s, 0:AT, :]
    gid_row = jnp.concatenate(gid_rows, axis=1)
    gid_col = jnp.transpose(jnp.broadcast_to(gid_row, (8, ATOMS)))[:, 0:1]
    h = h_s[...]
    loads[0].wait()
    ab_s[0:ATOMS, :] = nn(h, ws_ref[...]).astype(BF)
    loads[1].wait()
    ab_s[ATOMS : 2 * ATOMS, :] = nn(h, wd_ref[...]).astype(BF)

    for load in loads[2:]:
        load.wait()
    step = 16.0 / K
    inv_width = K / 24.0
    sub_a = lax.broadcasted_iota(jnp.int32, (ATOMS, ES), 0).astype(F32)
    lane_a = lax.broadcasted_iota(jnp.int32, (ES, ATOMS), 1).astype(F32)
    sub_b = lax.broadcasted_iota(jnp.int32, (BLK, TPB), 0).astype(F32)
    lane_e = lax.broadcasted_iota(jnp.int32, (1, ES), 1).astype(F32)
    lane_t = lax.broadcasted_iota(jnp.int32, (1, TPB), 1).astype(F32)
    centers = lax.broadcasted_iota(jnp.int32, (1, K), 1).astype(F32) * step

    def onehot(cond):
        return jnp.where(cond, 1.0, 0.0).astype(BF)

    def forward(s, carry):
        meta = gat_ref[lax.bitwise_xor(me, s), AT:PIECE, :].astype(F32)
        src = 2.0 * meta[0:1, 0:ES] + meta[0:1, ES : 2 * ES]
        dst = 2.0 * meta[1:2, 0:ES] + meta[1:2, ES : 2 * ES]
        ec = meta[15:16, 128:256]
        tc = 8.0 * meta[15:16, 256:384] + meta[15:16, 384:512]
        live = jnp.where(lane_e < jnp.concatenate([ec, ec], axis=1), 1.0, 0.0)
        lanes = pl.ds(pl.multiple_of(s * ES, ES), ES)
        ohts = onehot(sub_a == src)
        ohtd = onehot(sub_a == dst)
        oht_s[0:ATOMS, lanes] = ohts
        oht_s[ATOMS : 2 * ATOMS, lanes] = ohtd
        posp = posp_s[...]
        ps = nn(posp, ohts)
        pd = nn(posp, ohtd)
        ps = (ps[6:9] + ps[9:12]) + ps[12:15]
        pd = (pd[6:9] + pd[9:12]) + pd[12:15]
        vec = pd - ps
        sq = vec * vec
        dist = jnp.sqrt(sq[0:1] + sq[1:2] + sq[2:3] + 0.25)
        inv = 1.0 / dist
        unit = vec * inv
        geo = jnp.concatenate([src, dst, live, dist, unit, inv], axis=0)
        geo_s[s] = geo
        cols = jnp.transpose(geo)
        ohs = onehot(lane_a == cols[:, 0:1])
        ohd = onehot(lane_a == cols[:, 1:2])
        ohd_s[s] = ohd
        t = (cols[:, 3:4] - centers) * inv_width
        basis = jnp.exp(-(t * t)).astype(BF)
        bt_s[:, lanes] = jnp.transpose(basis.astype(F32)).astype(BF)
        pre = nn(ohs, ab_s[0:ATOMS, :]) + nn(ohd, ab_s[ATOMS : 2 * ATOMS, :])
        radial = nn(basis, wr_ref[...]) * cols[:, 2:3]
        sig = 0.5 + 0.5 * jnp.tanh(0.5 * pre)
        sil = pre * sig
        msg = (sil * radial).astype(BF)
        msg_s[s] = msg
        f_s[s] = (radial * (sig + sil * (1.0 - sig))).astype(BF)
        sg_s[s] = (sil * cols[:, 2:3]).astype(BF)
        m2 = nn(msg, wt_ref[...]).astype(BF)
        m2_s[s] = m2
        for i in range(2):
            rows = slice(BLK * i, BLK * (i + 1))
            limit = jnp.concatenate([tc] * 4, axis=1) - float(TPB * i)
            tin = meta[2 + i : 3 + i, :]
            tout = jnp.where(lane_t < limit, meta[4 + i : 5 + i, :], -1.0)
            pick_in = onehot(sub_b == tin)
            pick_out = onehot(sub_b == tout)
            count = nt(pick_out, pick_in) * cols[rows, 2:3]
            n_s[2 * s + i] = count
            gram = (
                cols[rows, 4:5] * unit[0:1, rows]
                + cols[rows, 5:6] * unit[1:2, rows]
                + cols[rows, 6:7] * unit[2:3, rows]
            )
            mix = count * gram
            tt_s[2 * s + i] = jnp.transpose(mix).astype(BF)
            upd = msg[rows].astype(F32) + nn(mix.astype(BF), m2[rows])
            upd_s[pl.ds(pl.multiple_of(s * ES + BLK * i, BLK), BLK), :] = upd.astype(BF)
        return carry

    lax.fori_loop(0, NG, forward, 0)

    agg = nn(oht_s[ATOMS : 2 * ATOMS, :], upd_s[...]).astype(BF)
    aggb_s[...] = agg
    z = nn(agg, wo_ref[...])
    sig = 0.5 + 0.5 * jnp.tanh(0.5 * z)
    out = z * sig
    we = we_ref[...].astype(F32)
    x = h_s[...].astype(F32) + out
    atom_energy = jnp.sum(x * we, axis=1, keepdims=True)
    member = jnp.where(
        lax.broadcasted_iota(jnp.int32, (ATOMS, 16), 1).astype(F32) == gid_col, 1.0, 0.0
    )
    energy_ref[...] = jnp.sum(member * atom_energy, axis=0, keepdims=True)
    cot = jnp.sum(member * ecot_ref[...], axis=1, keepdims=True)
    cot_s[...] = jnp.broadcast_to(cot, (ATOMS, 128))
    ge_s[...] = jnp.sum(x * cot, axis=0, keepdims=True)
    dz = (cot * we * (sig + out * (1.0 - sig))).astype(BF)
    dzb_s[...] = dz
    ac_s[...] = nt(dz, wo_ref[...]).astype(BF)

    def backward(s, carry):
        lanes = pl.ds(pl.multiple_of(s * ES, ES), ES)
        edges = pl.ds(pl.multiple_of(s * ES, ES), ES)
        geo = geo_s[s]
        cols = jnp.transpose(geo)
        ug = nn(ohd_s[s], ac_s[...])
        ugb = ug.astype(BF)
        m2 = m2_s[s]
        halves, turns = [], []
        for i in range(2):
            rows = slice(BLK * i, BLK * (i + 1))
            halves.append(nn(tt_s[2 * s + i], ugb[rows]).astype(BF))
            dgram = n_s[2 * s + i] * nt(ugb[rows], m2[rows])
            both = dgram + jnp.transpose(dgram)
            turns.append(
                lax.dot_general(
                    geo[:, rows], both, (((1,), (0,)), ((), ())), precision=HI, preferred_element_type=F32
                )
            )
        dm2 = jnp.concatenate(halves, axis=0)
        dm2_s[edges, :] = dm2
        dmsg = ug + nt(dm2, wt_ref[...])
        dpre_s[edges, :] = (dmsg * f_s[s].astype(F32)).astype(BF)
        drad = (dmsg * sg_s[s].astype(F32)).astype(BF)
        drad_s[edges, :] = drad
        t = (cols[:, 3:4] - centers) * inv_width
        slope = nt(drad, wr_ref[...]) * jnp.exp(-(t * t)) * (t * (-2.0 * inv_width))
        ddist = jnp.sum(jnp.transpose(slope), axis=0, keepdims=True)
        unit = geo[4:7]
        du = jnp.concatenate(turns, axis=1)[4:7]
        along = du * unit
        along = along[0:1] + along[1:2] + along[2:3]
        dv = geo[7:8] * (du - unit * along) + unit * ddist
        top = dv.astype(BF).astype(F32)
        dv_s[:, lanes] = jnp.concatenate(
            [top, dv - top, jnp.zeros((10, ES), F32)], axis=0
        ).astype(BF)
        return carry

    lax.fori_loop(0, NG, backward, 0)

    own = pl.multiple_of(me * AT, AT)
    ohs_own = oht_s[pl.ds(own, AT), :]
    ohd_own = oht_s[pl.ds(ATOMS + own, AT), :]
    dpre = dpre_s[...]
    s_src = nn(ohs_own, dpre).astype(BF)
    s_dst = nn(ohd_own, dpre).astype(BF)
    node_ref[...] = (
        cot_s[pl.ds(own, AT), 0:1] * we + nt(s_src, ws_ref[...]) + nt(s_dst, wd_ref[...])
    )
    pos = nt(dv_s[...], ohd_own) - nt(dv_s[...], ohs_own)
    pos = pos[0:3] + pos[3:6]
    for i in range(3):
        pos_out_ref[i] = pos[i : i + 1]

    group = lax.div(me, 4)
    block = pl.ds(pl.multiple_of(lax.rem(me, 4) * 128, 128), 128)
    side = pl.ds(pl.multiple_of(group * ATOMS, ATOMS), ATOMS)
    rows_t = tn(h_s[:, block], oht_s[side, :]).astype(BF)
    a_s[...] = nn(rows_t, dpre)

    @pl.when(group == 0)
    def _():
        for_trip = [msg_s[s, :, block] for s in range(NG)]
        b_s[...] = tn(jnp.concatenate(for_trip, axis=0), dm2_s[...])

    @pl.when(group == 1)
    def _():
        b_s[...] = tn(aggb_s[:, block], dzb_s[...])

    r_s[...] = nn(bt_s[pl.ds(pl.multiple_of(me * 16, 16), 16), :], drad_s[...])
    ge = ge_s[:, block]
    for u in range(4):
        for v in range(4):
            cols = slice(128 * v, 128 * v + 128)
            chunk = jnp.concatenate(
                [
                    a_s[32 * u : 32 * u + 32, cols],
                    b_s[32 * u : 32 * u + 32, cols],
                    r_s[4 * u : 4 * u + 4, cols],
                    ge,
                    jnp.zeros((CH - 69, 128), F32),
                ],
                axis=0,
            )
            pay_ref[lax.rem(u - my_u + 4, 4), lax.rem(v - my_v + 4, 4)] = chunk.astype(BF)


def batch(me, gat, ws, wd, wr, wt, wo, we, ecot):
    vm = pl.BlockSpec(memory_space=pltpu.VMEM)
    sm = pl.BlockSpec(memory_space=pltpu.SMEM)
    V = pltpu.VMEM
    return pl.pallas_call(
        main_kernel,
        out_shape=(
            jax.ShapeDtypeStruct((1, 16), F32),
            jax.ShapeDtypeStruct((3, 1, AT), F32),
            jax.ShapeDtypeStruct((AT, D), F32),
            jax.ShapeDtypeStruct((4, 4, CH, 128), BF),
        ),
        in_specs=[sm, vm] + [pl.BlockSpec(memory_space=pl.ANY)] * 5 + [vm] * 2,
        out_specs=(vm, vm, vm, vm),
        scratch_shapes=[
            V((ATOMS, D), BF),
            V((2 * ATOMS, D), BF),
            V((16, ATOMS), BF),
            V((2 * ATOMS, EDGES), BF),
            V((NG, ES, ATOMS), BF),
            V((NG, 8, ES), F32),
            V((NG, ES, D), BF),
            V((NG, ES, D), BF),
            V((NG, ES, D), BF),
            V((NG, ES, D), BF),
            V((2 * NG, BLK, BLK), F32),
            V((2 * NG, BLK, BLK), BF),
            V((EDGES, D), BF),
            V((ATOMS, D), BF),
            V((ATOMS, D), BF),
            V((ATOMS, D), BF),
            V((ATOMS, 128), F32),
            V((1, D), F32),
            V((K, EDGES), BF),
            V((EDGES, D), BF),
            V((EDGES, D), BF),
            V((EDGES, D), BF),
            V((16, EDGES), BF),
            V((BLK, D), F32),
            V((BLK, D), F32),
            V((16, D), F32),
            V((D, D), BF),
            V((D, D), BF),
            V((K, D), BF),
            V((D, D), BF),
            V((D, D), BF),
            pltpu.SemaphoreType.DMA((5,)),
        ],
        compiler_params=pltpu.CompilerParams(vmem_limit_bytes=50 * 1024 * 1024),
        name="batch",
    )(me, gat, ws, wd, wr, wt, wo, we, ecot)


def place_kernel(me_ref, own_ref, other_ref, gs_ref, gd_ref, gr_ref, gt_ref, go_ref, ge_ref, first, second, low, sems):
    x, y, zl, core = me_ref[0], me_ref[1], me_ref[2], me_ref[3]
    for c, ref in ((0, own_ref), (1, other_ref)):
        pc = core ^ c
        my_u = jnp.where(pc == 0, x, y)
        my_v = jnp.where(pc == 0, y, x)

        def body(i, carry, pc=pc, my_u=my_u, my_v=my_v, ref=ref):
            u = lax.rem(my_u - lax.div(i, 4) + 4, 4)
            v = lax.rem(my_v - lax.rem(i, 4) + 4, 4)
            cols = pl.ds(pl.multiple_of(v * 128, 128), 128)
            for kz in range(4):
                g = (zl ^ kz) * 2 + pc
                tile = ref[4 * i + kz].astype(F32)
                rows = pl.ds(pl.multiple_of(g * 128 + u * 32, 32), 32)
                first[rows, cols] = tile[0:32]
                second[rows, cols] = tile[32:64]
                low[g * 4 + u, :, cols] = tile[64:72]
            return carry

        lax.fori_loop(0, 16, body, 0)
    copies = [
        pltpu.make_async_copy(near, far, sems.at[i])
        for i, (near, far) in enumerate(
            (
                (first.at[0:D], gs_ref),
                (first.at[D : 2 * D], gd_ref),
                (second.at[0:D], gt_ref),
                (second.at[D : 2 * D], go_ref),
            )
        )
    ]
    for copy in copies:
        copy.start()
    for i in range(K // 4):
        gr_ref[4 * i : 4 * i + 4, :] = low[i, 0:4, :]
    for g in range(4):
        ge_ref[:, 128 * g : 128 * (g + 1)] = low[4 * g, 4:5, 0:128]
    for copy in copies:
        copy.wait()


def place(where, own, other):
    vm = pl.BlockSpec(memory_space=pltpu.VMEM)
    sm = pl.BlockSpec(memory_space=pltpu.SMEM)
    far = pl.BlockSpec(memory_space=pl.ANY)
    big = jax.ShapeDtypeStruct((D, D), F32)
    return pl.pallas_call(
        place_kernel,
        out_shape=(big, big, jax.ShapeDtypeStruct((K, D), F32), big, big, jax.ShapeDtypeStruct((1, D), F32)),
        in_specs=[sm, vm, vm],
        out_specs=(far, far, vm, far, far, vm),
        scratch_shapes=[
            pltpu.VMEM((2 * D, D), F32),
            pltpu.VMEM((2 * D, D), F32),
            pltpu.VMEM((K // 4, 8, D), F32),
            pltpu.SemaphoreType.DMA((4,)),
        ],
        compiler_params=pltpu.CompilerParams(vmem_limit_bytes=40 * 1024 * 1024),
        name="place",
    )(where, own, other)


def moves(fn):
    pairs = []
    for zh in range(2):
        for x in range(4):
            for y in range(4):
                for zl in range(4):
                    for c in range(2):
                        u, v = (x, y) if c == 0 else (y, x)
                        zh2, u2, v2, zl2, c2 = fn(zh, u, v, zl, c)
                        x2, y2 = (u2, v2) if c == 0 else (v2, u2)
                        here = (zh * 16 + x * 4 + y) * 8 + zl * 2 + c
                        there = (zh2 * 16 + x2 * 4 + y2) * 8 + zl2 * 2 + c2
                        pairs.append((here, there))
    return pairs


def shift(value, zh=0, u=0, v=0, zl=0, c=0):
    def fn(zh_, u_, v_, zl_, c_):
        return zh_ ^ zh, (u_ + u) % 4, (v_ + v) % 4, zl_ ^ zl, c_ ^ c

    return lax.ppermute(value, AXES, moves(fn))


def join(*parts):
    return jnp.concatenate(parts, axis=0)


ORDER = (1, 3, 2)


def total(parts):
    result = parts[0].astype(F32)
    for part in parts[1:]:
        result = result + part.astype(F32)
    return result


def per_device(
    node_feats,
    positions,
    edge_src,
    edge_dst,
    edge_count,
    trip_in,
    trip_out,
    trip_count,
    graph_ids,
    w_src,
    w_dst,
    w_radial,
    w_trip,
    w_out,
    w_energy,
    energy_cot,
):
    dp, graph = lax.axis_index("dp"), lax.axis_index("graph")
    x, y = lax.rem(lax.div(dp, 4), 4), lax.rem(dp, 4)
    zl, core = lax.div(graph, 2), lax.rem(graph, 2)
    u, v = jnp.where(core == 0, x, y), jnp.where(core == 0, y, x)
    me = jnp.stack([graph, u, v]).astype(jnp.int32)
    piece = pack(
        me,
        node_feats[0],
        jnp.swapaxes(positions, 0, 1),
        edge_src,
        edge_dst,
        edge_count,
        trip_in,
        trip_out,
        trip_count,
        graph_ids,
    )[None]
    pair = join(piece, shift(piece, c=1))
    gathered = join(pair, *[shift(pair, zl=k) for k in (1, 2, 3)])
    energy, pos_grad, node_grad, payload = batch(
        me, gathered, w_src, w_dst, w_radial, w_trip, w_out, w_energy.reshape(1, D), energy_cot
    )
    part = total([payload[0]] + [shift(payload[k], u=k) for k in ORDER]).astype(BF)
    part = total([part[0]] + [shift(part[k], v=k) for k in ORDER]).astype(BF)
    part = (part.astype(F32) + shift(part, zh=1).astype(F32)).astype(BF)[None]
    part = join(part, *[shift(part, zl=k) for k in (1, 2, 3)])
    back = [shift(part, v=k) for k in ORDER]
    part = join(part, back[0], back[2], back[1])
    back = [shift(part, u=k) for k in ORDER]
    part = join(part, back[0], back[2], back[1])
    other = shift(part, c=1)
    where = jnp.stack([x, y, zl, core]).astype(jnp.int32)
    gs, gd, gr, gt, go, ge = place(where, part, other)
    return (energy, jnp.swapaxes(pos_grad, 0, 1), node_grad[None], gs, gd, gr, gt, go, ge.reshape(D))


def solution(mesh):
    placed = (
        P("dp", "graph", None),
        P("dp", None, "graph"),
        P("dp", "graph"),
        P("dp", "graph"),
        P("dp", "graph"),
        P("dp", "graph"),
        P("dp", "graph"),
        P("dp", "graph"),
        P("dp", "graph"),
        P(),
        P(),
        P(),
        P(),
        P(),
        P(),
        P("dp", None),
    )
    return jax.shard_map(
        per_device,
        mesh=mesh,
        in_specs=placed,
        out_specs=(
            P("dp", None),
            P("dp", None, "graph"),
            P("dp", "graph", None),
            P(),
            P(),
            P(),
            P(),
            P(),
            P(),
        ),
        check_vma=False,
    )
```

```python
import jax
import jax.numpy as jnp
from jax import lax
from jax.experimental import pallas as pl
from jax.experimental.pallas import tpu as pltpu
from jax.sharding import PartitionSpec as P

BF = jnp.bfloat16
F32 = jnp.float32
NG = 8
AT = 64
ATOMS = 512
ES = 256
EDGES = 2048
D = 512
K = 128
BLK = 128
TPB = 512
PIECE = 80
CH = 80
AXES = ("dp", "graph")
HI = lax.Precision.HIGHEST


def nn(a, b):
    return lax.dot_general(a, b, (((1,), (0,)), ((), ())), preferred_element_type=F32)


def nt(a, b):
    return lax.dot_general(a, b, (((1,), (1,)), ((), ())), preferred_element_type=F32)


def tn(a, b):
    return lax.dot_general(a, b, (((0,), (0,)), ((), ())), preferred_element_type=F32)


def pack_kernel(me_ref, h_ref, pos_ref, src_ref, dst_ref, ec_ref, tin_ref, tout_ref, tc_ref, gid_ref, out_ref, meta):
    odd = lax.rem(me_ref[0], 2)
    out_ref[0:AT, :] = h_ref[...]

    def place(row):
        full = jnp.concatenate([row, jnp.zeros_like(row)], axis=1)
        return jnp.where(odd == 1, pltpu.roll(full, AT, 1), full)

    for r, ref in ((0, src_ref), (1, dst_ref)):
        v = ref[...]
        half = lax.shift_right_logical(v, 1)
        meta[r : r + 1, 0:ES] = half.astype(F32)
        meta[r : r + 1, ES : 2 * ES] = (v - 2 * half).astype(F32)
    for r, ref in ((2, tin_ref), (4, tout_ref)):
        v = ref[...].astype(F32)
        meta[r : r + 1, :] = v[:, 0:TPB]
        meta[r + 1 : r + 2, :] = v[:, TPB : 2 * TPB]
    p = jnp.concatenate([pos_ref[i] for i in range(3)], axis=0)
    p1 = p.astype(BF).astype(F32)
    p2 = (p - p1).astype(BF).astype(F32)
    p3 = (p - p1) - p2
    meta[6:16, :] = jnp.zeros((10, D), F32)
    meta[6:9, 0:128] = place(p1)
    meta[9:12, 0:128] = place(p2)
    meta[12:15, 0:128] = place(p3)
    meta[15:16, 0:128] = place(gid_ref[...].astype(F32))
    tc = tc_ref[0, 0]
    tc_half = lax.shift_right_logical(tc, 3)
    meta[15:16, 128:256] = jnp.full((1, 128), ec_ref[0, 0].astype(F32))
    meta[15:16, 256:384] = jnp.full((1, 128), tc_half.astype(F32))
    meta[15:16, 384:512] = jnp.full((1, 128), (tc - 8 * tc_half).astype(F32))
    out_ref[AT:PIECE, :] = meta[...].astype(BF)


def pack(me, h, pos, src, dst, ec, tin, tout, tc, gid):
    vm = pl.BlockSpec(memory_space=pltpu.VMEM)
    sm = pl.BlockSpec(memory_space=pltpu.SMEM)
    return pl.pallas_call(
        pack_kernel,
        out_shape=jax.ShapeDtypeStruct((PIECE, D), BF),
        in_specs=[sm, vm, vm, vm, vm, sm, vm, vm, sm, vm],
        out_specs=vm,
        scratch_shapes=[pltpu.VMEM((16, D), F32)],
        name="pack",
    )(me, h, pos, src, dst, ec, tin, tout, tc, gid)


def main_kernel(
    me_ref,
    slice_ref,
    u_ref,
    own_ref,
    other_ref,
    ws_hbm,
    wd_hbm,
    wr_hbm,
    wt_hbm,
    wo_hbm,
    we_ref,
    ecot_ref,
    energy_ref,
    pos_out_ref,
    node_ref,
    pay_ref,
    h_s,
    meta_s,
    ab_s,
    posp_s,
    oht_s,
    ohd_s,
    geo_s,
    msg_s,
    f_s,
    sg_s,
    m2_s,
    n_s,
    tt_s,
    upd_s,
    aggb_s,
    dzb_s,
    ac_s,
    cot_s,
    ge_s,
    bt_s,
    dm2_s,
    dpre_s,
    drad_s,
    dv_s,
    a_s,
    b_s,
    r_s,
    ws_ref,
    wd_ref,
    wr_ref,
    wt_ref,
    wo_ref,
    sems,
):
    loads = [
        pltpu.make_async_copy(far, near, sems.at[i])
        for i, (far, near) in enumerate(
            ((ws_hbm, ws_ref), (wd_hbm, wd_ref), (wr_hbm, wr_ref), (wt_hbm, wt_ref), (wo_hbm, wo_ref))
        )
    ]
    for load in loads:
        load.start()
    me, my_slice, my_u = me_ref[0], slice_ref[0], u_ref[0]
    for near, ref in ((0, own_ref), (1, other_ref)):
        for kz in range(4):
            shard = me ^ (2 * kz + near)
            h_s[pl.ds(pl.multiple_of(shard * AT, AT), AT), :] = ref[kz, 0:AT, :]
            meta_s[shard] = ref[kz, AT:PIECE, :].astype(F32)
    gid_rows = []
    for j in range(4):
        both = meta_s[2 * j, :, 0:128] + meta_s[2 * j + 1, :, 0:128]
        posp_s[:, 128 * j : 128 * (j + 1)] = both.astype(BF)
        gid_rows.append(both[15:16, :])
    gid_row = jnp.concatenate(gid_rows, axis=1)
    gid_col = jnp.transpose(jnp.broadcast_to(gid_row, (8, ATOMS)))[:, 0:1]

    step = 16.0 / K
    inv_width = K / 24.0
    sub_e = lax.broadcasted_iota(jnp.int32, (BLK, ES), 0).astype(F32).astype(BF)
    sub_t = lax.broadcasted_iota(jnp.int32, (BLK, TPB), 0).astype(F32).astype(BF)
    lane_a = lax.broadcasted_iota(jnp.int32, (ES, ATOMS), 1).astype(F32)
    lane_e = lax.broadcasted_iota(jnp.int32, (1, ES), 1).astype(F32)
    lane_t = lax.broadcasted_iota(jnp.int32, (1, TPB), 1).astype(F32)
    centers = lax.broadcasted_iota(jnp.int32, (1, K), 1).astype(F32) * step
    one, zero = jnp.ones((), BF), jnp.zeros((), BF)

    def onehot(cond):
        return jnp.where(cond, 1.0, 0.0).astype(BF)

    def hit(places, row):
        wide = jnp.broadcast_to(row.astype(BF), places.shape)
        return jnp.where(places == wide, one, zero)

    def geometry(s):
        meta = meta_s[s]
        src = 2.0 * meta[0:1, 0:ES] + meta[0:1, ES : 2 * ES]
        dst = 2.0 * meta[1:2, 0:ES] + meta[1:2, ES : 2 * ES]
        ec = meta[15:16, 128:256]
        live = jnp.where(lane_e < jnp.concatenate([ec, ec], axis=1), 1.0, 0.0)
        lanes = slice(s * ES, (s + 1) * ES)
        for base, row in ((0, src), (ATOMS, dst)):
            for j in range(4):
                oht_s[base + BLK * j : base + BLK * (j + 1), lanes] = hit(sub_e, row - float(BLK * j))
        posp = posp_s[...]
        ps = nn(posp, oht_s[0:ATOMS, lanes])
        pd = nn(posp, oht_s[ATOMS : 2 * ATOMS, lanes])
        ps = (ps[6:9] + ps[9:12]) + ps[12:15]
        pd = (pd[6:9] + pd[9:12]) + pd[12:15]
        vec = pd - ps
        sq = vec * vec
        dist = jnp.sqrt(sq[0:1] + sq[1:2] + sq[2:3] + 0.25)
        inv = 1.0 / dist
        geo_s[s] = jnp.concatenate([src, dst, live, dist, vec * inv, inv], axis=0)

    def forward(s):
        geo = geo_s[s]
        meta = meta_s[s]
        unit = geo[4:7]
        tc = 8.0 * meta[15:16, 256:384] + meta[15:16, 384:512]
        cols = jnp.transpose(geo)
        ohs = onehot(lane_a == cols[:, 0:1])
        ohd = onehot(lane_a == cols[:, 1:2])
        ohd_s[s] = ohd
        t = (cols[:, 3:4] - centers) * inv_width
        basis = jnp.exp(-(t * t)) * cols[:, 2:3]
        bt_s[:, s * ES : (s + 1) * ES] = jnp.transpose(basis).astype(BF)
        q = nn(ohs, ab_s[0:ATOMS, :]) + nn(ohd, ab_s[ATOMS : 2 * ATOMS, :])
        radial = nn(basis.astype(BF), wr_ref[...])
        a = 1.0 + jnp.tanh(q)
        sil = q * a
        msg = (sil * radial).astype(BF)
        msg_s[s] = msg
        f_s[s] = (radial * (a + sil * (2.0 - a))).astype(BF)
        sg_s[s] = sil.astype(BF)
        m2 = nn(msg, wt_ref[...]).astype(BF)
        m2_s[s] = m2
        for i in range(2):
            rows = slice(BLK * i, BLK * (i + 1))
            limit = jnp.concatenate([tc] * 4, axis=1) - float(TPB * i)
            tin = meta[2 + i : 3 + i, :]
            tout = jnp.where(lane_t < limit, meta[4 + i : 5 + i, :], -1.0)
            count = nt(hit(sub_t, tout), hit(sub_t, tin)) * cols[rows, 2:3]
            n_s[2 * s + i] = count
            gram = (
                cols[rows, 4:5] * unit[0:1, rows]
                + cols[rows, 5:6] * unit[1:2, rows]
                + cols[rows, 6:7] * unit[2:3, rows]
            )
            mix = count * gram
            tt_s[2 * s + i] = jnp.transpose(mix).astype(BF)
            upd = msg[rows].astype(F32) + nn(mix.astype(BF), m2[rows])
            upd_s[s * ES + BLK * i : s * ES + BLK * (i + 1), :] = upd.astype(BF)

    for s in range(NG):
        geometry(s)
    h = h_s[...]
    loads[0].wait()
    ab_s[0:ATOMS, :] = (0.5 * nn(h, ws_ref[...])).astype(BF)
    loads[1].wait()
    ab_s[ATOMS : 2 * ATOMS, :] = (0.5 * nn(h, wd_ref[...])).astype(BF)
    for load in loads[2:]:
        load.wait()
    for s in range(NG):
        forward(s)

    agg = nn(oht_s[ATOMS : 2 * ATOMS, :], upd_s[...]).astype(BF)
    aggb_s[...] = agg
    z = nn(agg, wo_ref[...])
    sig = 0.5 + 0.5 * jnp.tanh(0.5 * z)
    out = z * sig
    we = we_ref[...].astype(F32)
    x = h_s[...].astype(F32) + out
    atom_energy = jnp.sum(x * we, axis=1, keepdims=True)
    member = jnp.where(
        lax.broadcasted_iota(jnp.int32, (ATOMS, 16), 1).astype(F32) == gid_col, 1.0, 0.0
    )
    energy_ref[...] = jnp.sum(member * atom_energy, axis=0, keepdims=True)
    cot = jnp.sum(member * ecot_ref[...], axis=1, keepdims=True)
    cot_s[...] = jnp.broadcast_to(cot, (ATOMS, 128))
    ge_s[...] = jnp.sum(x * cot, axis=0, keepdims=True)
    dz = (cot * we * (sig + out * (1.0 - sig))).astype(BF)
    dzb_s[...] = dz
    ac_s[...] = nt(dz, wo_ref[...]).astype(BF)

    def backward(s):
        edges = slice(s * ES, (s + 1) * ES)
        geo = geo_s[s]
        cols = jnp.transpose(geo)
        ug = nn(ohd_s[s], ac_s[...])
        ugb = ug.astype(BF)
        m2 = m2_s[s]
        halves, turns = [], []
        for i in range(2):
            rows = slice(BLK * i, BLK * (i + 1))
            halves.append(nn(tt_s[2 * s + i], ugb[rows]).astype(BF))
            dgram = n_s[2 * s + i] * nt(ugb[rows], m2[rows])
            both = dgram + jnp.transpose(dgram)
            turns.append(
                jnp.concatenate(
                    [jnp.sum(both * cols[rows, a : a + 1], axis=0, keepdims=True) for a in (4, 5, 6)], axis=0
                )
            )
        dm2 = jnp.concatenate(halves, axis=0)
        dm2_s[edges, :] = dm2
        dmsg = ug + nt(dm2, wt_ref[...])
        dpre_s[edges, :] = (dmsg * f_s[s].astype(F32)).astype(BF)
        drad = (dmsg * sg_s[s].astype(F32)).astype(BF)
        drad_s[edges, :] = drad
        t = (cols[:, 3:4] - centers) * inv_width
        slope = nt(drad, wr_ref[...]) * (jnp.exp(-(t * t)) * (t * (-2.0 * inv_width)))
        ddist = jnp.sum(jnp.transpose(slope), axis=0, keepdims=True) * geo[2:3]
        unit = geo[4:7]
        du = jnp.concatenate(turns, axis=1)
        along = du * unit
        along = along[0:1] + along[1:2] + along[2:3]
        dv = geo[7:8] * (du - unit * along) + unit * ddist
        top = dv.astype(BF).astype(F32)
        dv_s[:, edges] = jnp.concatenate([top, dv - top, jnp.zeros((10, ES), F32)], axis=0).astype(BF)

    for s in range(NG):
        backward(s)

    own = pl.multiple_of(me * AT, AT)
    ohs_own = oht_s[pl.ds(own, AT), :]
    ohd_own = oht_s[pl.ds(ATOMS + own, AT), :]
    dpre = dpre_s[...]
    s_src = (0.5 * nn(ohs_own, dpre)).astype(BF)
    s_dst = (0.5 * nn(ohd_own, dpre)).astype(BF)
    node_ref[...] = (
        cot_s[pl.ds(own, AT), 0:1] * we + nt(s_src, ws_ref[...]) + nt(s_dst, wd_ref[...])
    )
    pos = nt(dv_s[...], ohd_own) - nt(dv_s[...], ohs_own)
    pos = pos[0:3] + pos[3:6]
    for i in range(3):
        pos_out_ref[i] = pos[i : i + 1]

    group = lax.div(my_slice, 4)
    block = pl.ds(pl.multiple_of(lax.rem(my_slice, 4) * 128, 128), 128)
    side = pl.ds(pl.multiple_of(group * ATOMS, ATOMS), ATOMS)
    rows_t = tn(h_s[:, block], oht_s[side, :]).astype(BF)
    a_s[...] = 0.5 * nn(rows_t, dpre)

    @pl.when(group == 0)
    def _():
        for_trip = [msg_s[s, :, block] for s in range(NG)]
        b_s[...] = tn(jnp.concatenate(for_trip, axis=0), dm2_s[...])

    @pl.when(group == 1)
    def _():
        b_s[...] = tn(aggb_s[:, block], dzb_s[...])

    r_s[...] = nn(bt_s[pl.ds(pl.multiple_of(my_slice * 16, 16), 16), :], drad_s[...])
    ge = ge_s[:, block]
    for u in range(4):
        for v in range(4):
            cols = slice(128 * v, 128 * v + 128)
            chunk = jnp.concatenate(
                [
                    a_s[32 * u : 32 * u + 32, cols],
                    b_s[32 * u : 32 * u + 32, cols],
                    r_s[4 * u : 4 * u + 4, cols],
                    ge,
                    jnp.zeros((CH - 69, 128), F32),
                ],
                axis=0,
            )
            pay_ref[lax.rem(u - my_u + 4, 4), v] = chunk.astype(BF)


def batch(me, part, u, own, other, ws, wd, wr, wt, wo, we, ecot):
    vm = pl.BlockSpec(memory_space=pltpu.VMEM)
    sm = pl.BlockSpec(memory_space=pltpu.SMEM)
    V = pltpu.VMEM
    return pl.pallas_call(
        main_kernel,
        out_shape=(
            jax.ShapeDtypeStruct((1, 16), F32),
            jax.ShapeDtypeStruct((3, 1, AT), F32),
            jax.ShapeDtypeStruct((AT, D), F32),
            jax.ShapeDtypeStruct((4, 4, CH, 128), BF),
        ),
        in_specs=[sm] * 3 + [vm] * 2 + [pl.BlockSpec(memory_space=pl.ANY)] * 5 + [vm] * 2,
        out_specs=(vm, vm, vm, vm),
        scratch_shapes=[
            V((ATOMS, D), BF),
            V((NG, 16, D), F32),
            V((2 * ATOMS, D), BF),
            V((16, ATOMS), BF),
            V((2 * ATOMS, EDGES), BF),
            V((NG, ES, ATOMS), BF),
            V((NG, 8, ES), F32),
            V((NG, ES, D), BF),
            V((NG, ES, D), BF),
            V((NG, ES, D), BF),
            V((NG, ES, D), BF),
            V((2 * NG, BLK, BLK), F32),
            V((2 * NG, BLK, BLK), BF),
            V((EDGES, D), BF),
            V((ATOMS, D), BF),
            V((ATOMS, D), BF),
            V((ATOMS, D), BF),
            V((ATOMS, 128), F32),
            V((1, D), F32),
            V((K, EDGES), BF),
            V((EDGES, D), BF),
            V((EDGES, D), BF),
            V((EDGES, D), BF),
            V((16, EDGES), BF),
            V((BLK, D), F32),
            V((BLK, D), F32),
            V((16, D), F32),
            V((D, D), BF),
            V((D, D), BF),
            V((K, D), BF),
            V((D, D), BF),
            V((D, D), BF),
            pltpu.SemaphoreType.DMA((5,)),
        ],
        compiler_params=pltpu.CompilerParams(vmem_limit_bytes=50 * 1024 * 1024),
        name="batch",
    )(me, part, u, own, other, ws, wd, wr, wt, wo, we, ecot)


def place_kernel(x_ref, y_ref, slice_ref, own_ref, other_ref, gs_ref, gd_ref, gr_ref, gt_ref, go_ref, ge_ref, first, second, low, sems):
    x, y, mine = x_ref[0], y_ref[0], slice_ref[0]
    core = mine & 1
    for c, ref in ((0, own_ref), (1, other_ref)):
        pc = core ^ c
        my_u = jnp.where(pc == 0, x, y)

        def body(i, carry, c=c, my_u=my_u, ref=ref):
            u = lax.rem(my_u - lax.div(i, 4) + 4, 4)
            kz = lax.rem(i, 4)
            for k in range(4):
                cols = slice(128 * k, 128 * (k + 1))
                g = lax.bitwise_xor(mine, 2 * kz + c)
                tile = ref[4 * i + k].astype(F32)
                rows = pl.ds(pl.multiple_of(g * 128 + u * 32, 32), 32)
                first[rows, cols] = tile[0:32]
                second[rows, cols] = tile[32:64]
                low[g * 4 + u, :, cols] = tile[64:72]
            return carry

        lax.fori_loop(0, 16, body, 0)
    copies = [
        pltpu.make_async_copy(near, far, sems.at[i])
        for i, (near, far) in enumerate(
            (
                (first.at[0:D], gs_ref),
                (first.at[D : 2 * D], gd_ref),
                (second.at[0:D], gt_ref),
                (second.at[D : 2 * D], go_ref),
            )
        )
    ]
    for copy in copies:
        copy.start()
    for i in range(K // 4):
        gr_ref[4 * i : 4 * i + 4, :] = low[i, 0:4, :]
    for g in range(4):
        ge_ref[:, 128 * g : 128 * (g + 1)] = low[4 * g, 4:5, 0:128]
    for copy in copies:
        copy.wait()


def place(x, y, part, own, other):
    vm = pl.BlockSpec(memory_space=pltpu.VMEM)
    sm = pl.BlockSpec(memory_space=pltpu.SMEM)
    far = pl.BlockSpec(memory_space=pl.ANY)
    big = jax.ShapeDtypeStruct((D, D), F32)
    return pl.pallas_call(
        place_kernel,
        out_shape=(big, big, jax.ShapeDtypeStruct((K, D), F32), big, big, jax.ShapeDtypeStruct((1, D), F32)),
        in_specs=[sm] * 3 + [vm] * 2,
        out_specs=(far, far, vm, far, far, vm),
        scratch_shapes=[
            pltpu.VMEM((2 * D, D), F32),
            pltpu.VMEM((2 * D, D), F32),
            pltpu.VMEM((K // 4, 8, D), F32),
            pltpu.SemaphoreType.DMA((4,)),
        ],
        compiler_params=pltpu.CompilerParams(vmem_limit_bytes=40 * 1024 * 1024),
        name="place",
    )(x, y, part, own, other)


def moves(fn):
    pairs = []
    for zh in range(2):
        for x in range(4):
            for y in range(4):
                for zl in range(4):
                    for c in range(2):
                        u, v = (x, y) if c == 0 else (y, x)
                        zh2, u2, v2, zl2, c2 = fn(zh, u, v, zl, c)
                        x2, y2 = (u2, v2) if c == 0 else (v2, u2)
                        here = (zh * 16 + x * 4 + y) * 8 + zl * 2 + c
                        there = (zh2 * 16 + x2 * 4 + y2) * 8 + zl2 * 2 + c2
                        pairs.append((here, there))
    return pairs


def shift(value, zh=0, u=0, v=0, zl=0, c=0):
    def fn(zh_, u_, v_, zl_, c_):
        return zh_ ^ zh, (u_ + u) % 4, (v_ + v) % 4, zl_ ^ zl, c_ ^ c

    return lax.ppermute(value, AXES, moves(fn))


def join(*parts):
    return jnp.concatenate(parts, axis=0)


ORDER = (1, 3, 2)


def total(a, b, c, d):
    a, b, c, d = (part.astype(F32) for part in (a, b, c, d))
    return ((a + b) + (c + d)).astype(BF)


def per_device(
    node_feats,
    positions,
    edge_src,
    edge_dst,
    edge_count,
    trip_in,
    trip_out,
    trip_count,
    graph_ids,
    w_src,
    w_dst,
    w_radial,
    w_trip,
    w_out,
    w_energy,
    energy_cot,
):
    dp, graph = lax.axis_index("dp"), lax.axis_index("graph")
    zh, x, y = lax.shift_right_logical(dp, 4), lax.shift_right_logical(dp, 2) & 3, dp & 3
    core = graph & 1
    u = jnp.where(core == 0, x, y)
    part = graph ^ (6 * zh)
    me, x, y, u, part = (a.astype(jnp.int32).reshape(1) for a in (graph, x, y, u, part))
    piece = pack(
        me,
        node_feats[0],
        jnp.swapaxes(positions, 0, 1),
        edge_src,
        edge_dst,
        edge_count,
        trip_in,
        trip_out,
        trip_count,
        graph_ids,
    )[None]
    own = join(piece, *[shift(piece, zl=k) for k in (1, 2, 3)])
    other = shift(own, c=1)
    energy, pos_grad, node_grad, payload = batch(
        me, part, u, own, other, w_src, w_dst, w_radial, w_trip, w_out, w_energy.reshape(1, D), energy_cot
    )
    one, three, two = [shift(payload[k], u=k) for k in ORDER]
    held = total(payload[0], two, one, three)
    one, three, two = [shift(held, v=k) for k in ORDER]
    held = total(held, two, one, three)
    held = (held.astype(F32) + shift(held, zh=1, zl=3).astype(F32)).astype(BF)
    held = join(held, *[shift(held, zl=k) for k in (1, 2, 3)])
    one, three, two = [shift(held, u=k) for k in ORDER]
    held = join(held, one, two, three)
    gs, gd, gr, gt, go, ge = place(x, y, part, held, shift(held, c=1))
    return (energy, jnp.swapaxes(pos_grad, 0, 1), node_grad[None], gs, gd, gr, gt, go, ge.reshape(D))


def solution(mesh):
    placed = (
        P("dp", "graph", None),
        P("dp", None, "graph"),
        P("dp", "graph"),
        P("dp", "graph"),
        P("dp", "graph"),
        P("dp", "graph"),
        P("dp", "graph"),
        P("dp", "graph"),
        P("dp", "graph"),
        P(),
        P(),
        P(),
        P(),
        P(),
        P(),
        P("dp", None),
    )
    return jax.shard_map(
        per_device,
        mesh=mesh,
        in_specs=placed,
        out_specs=(
            P("dp", None),
            P("dp", None, "graph"),
            P("dp", "graph", None),
            P(),
            P(),
            P(),
            P(),
            P(),
            P(),
        ),
        check_vma=False,
    )
```

```python
import functools

import jax
import jax.numpy as jnp
from jax import lax
from jax.experimental import pallas as pl
from jax.experimental.pallas import tpu as pltpu
from jax.sharding import PartitionSpec as P

BF = jnp.bfloat16
F32 = jnp.float32
NG = 8
AT = 64
ATOMS = 512
ES = 256
EDGES = 2048
D = 512
K = 128
BLK = 128
TPB = 512
PIECE = 80
CH = 72
AXES = ("dp", "graph")
HI = lax.Precision.HIGHEST


def nn(a, b):
    return lax.dot_general(a, b, (((1,), (0,)), ((), ())), preferred_element_type=F32)


def nt(a, b):
    return lax.dot_general(a, b, (((1,), (1,)), ((), ())), preferred_element_type=F32)


def tn(a, b):
    return lax.dot_general(a, b, (((0,), (0,)), ((), ())), preferred_element_type=F32)


def pack_kernel(me_ref, h_ref, pos_ref, src_ref, dst_ref, ec_ref, tin_ref, tout_ref, tc_ref, gid_ref, out_ref, meta):
    odd = lax.rem(me_ref[0], 2)
    out_ref[0:AT, :] = h_ref[...]

    def place(row):
        full = jnp.concatenate([row, jnp.zeros_like(row)], axis=1)
        return jnp.where(odd == 1, pltpu.roll(full, AT, 1), full)

    for r, ref in ((0, src_ref), (1, dst_ref)):
        v = ref[...]
        half = lax.shift_right_logical(v, 1)
        meta[r : r + 1, 0:ES] = half.astype(F32)
        meta[r : r + 1, ES : 2 * ES] = (v - 2 * half).astype(F32)
    for r, ref in ((2, tin_ref), (4, tout_ref)):
        v = ref[...].astype(F32)
        meta[r : r + 1, :] = v[:, 0:TPB]
        meta[r + 1 : r + 2, :] = v[:, TPB : 2 * TPB]
    p = jnp.concatenate([pos_ref[i] for i in range(3)], axis=0)
    p1 = p.astype(BF).astype(F32)
    p2 = (p - p1).astype(BF).astype(F32)
    p3 = (p - p1) - p2
    meta[6:16, :] = jnp.zeros((10, D), F32)
    meta[6:9, 0:128] = place(p1)
    meta[9:12, 0:128] = place(p2)
    meta[12:15, 0:128] = place(p3)
    meta[15:16, 0:128] = place(gid_ref[...].astype(F32))
    tc = tc_ref[0, 0]
    tc_half = lax.shift_right_logical(tc, 3)
    meta[15:16, 128:256] = jnp.full((1, 128), ec_ref[0, 0].astype(F32))
    meta[15:16, 256:384] = jnp.full((1, 128), tc_half.astype(F32))
    meta[15:16, 384:512] = jnp.full((1, 128), (tc - 8 * tc_half).astype(F32))
    out_ref[AT:PIECE, :] = meta[...].astype(BF)


def pack(me, h, pos, src, dst, ec, tin, tout, tc, gid):
    vm = pl.BlockSpec(memory_space=pltpu.VMEM)
    sm = pl.BlockSpec(memory_space=pltpu.SMEM)
    return pl.pallas_call(
        pack_kernel,
        out_shape=jax.ShapeDtypeStruct((PIECE, D), BF),
        in_specs=[sm, vm, vm, vm, vm, sm, vm, vm, sm, vm],
        out_specs=vm,
        scratch_shapes=[pltpu.VMEM((16, D), F32)],
        name="pack",
    )(me, h, pos, src, dst, ec, tin, tout, tc, gid)


def main_kernel(
    me_ref,
    slice_ref,
    u_ref,
    own_ref,
    other_ref,
    ws_hbm,
    wd_hbm,
    wr_hbm,
    wt_hbm,
    wo_hbm,
    we_ref,
    ecot_ref,
    energy_ref,
    pos_out_ref,
    own_s_ref,
    cot_ref,
    pay_ref,
    h_s,
    meta_s,
    ab_s,
    posp_s,
    oht_s,
    ohd_s,
    geo_s,
    msg_s,
    f_s,
    sg_s,
    m2_s,
    n_s,
    tt_s,
    upd_s,
    aggb_s,
    dzb_s,
    ac_s,
    cot_s,
    ge_s,
    bt_s,
    dm2_s,
    dpre_s,
    drad_s,
    dv_s,
    a_s,
    b_s,
    r_s,
    ws_ref,
    wd_ref,
    wr_ref,
    wt_ref,
    wo_ref,
    sems,
    wtt_s,
):
    loads = [
        pltpu.make_async_copy(far, near, sems.at[i])
        for i, (far, near) in enumerate(
            ((ws_hbm, ws_ref), (wd_hbm, wd_ref), (wr_hbm, wr_ref), (wt_hbm, wt_ref), (wo_hbm, wo_ref))
        )
    ]
    for load in loads:
        load.start()
    me, my_slice, my_u = me_ref[0], slice_ref[0], u_ref[0]
    for near, ref in ((0, own_ref), (1, other_ref)):
        for kz in range(4):
            shard = me ^ (2 * kz + near)
            h_s[pl.ds(pl.multiple_of(shard * AT, AT), AT), :] = ref[kz, 0:AT, :]
            meta_s[shard] = ref[kz, AT:PIECE, :].astype(F32)
    gid_rows = []
    for j in range(4):
        both = meta_s[2 * j, :, 0:128] + meta_s[2 * j + 1, :, 0:128]
        posp_s[:, 128 * j : 128 * (j + 1)] = both.astype(BF)
        gid_rows.append(both[15:16, :])
    gid_row = jnp.concatenate(gid_rows, axis=1)
    gid_col = jnp.transpose(jnp.broadcast_to(gid_row, (8, ATOMS)))[:, 0:1]

    step = 16.0 / K
    inv_width = K / 24.0
    sub_e = lax.broadcasted_iota(jnp.int32, (BLK, ES), 0).astype(F32).astype(BF)
    sub_t = lax.broadcasted_iota(jnp.int32, (BLK, TPB), 0).astype(F32).astype(BF)
    lane_a = lax.broadcasted_iota(jnp.int32, (ES, ATOMS), 1).astype(F32)
    lane_e = lax.broadcasted_iota(jnp.int32, (1, ES), 1).astype(F32)
    lane_t = lax.broadcasted_iota(jnp.int32, (1, TPB), 1).astype(F32)
    centers = lax.broadcasted_iota(jnp.int32, (1, K), 1).astype(F32) * step
    one, zero = jnp.ones((), BF), jnp.zeros((), BF)

    def onehot(cond):
        return jnp.where(cond, 1.0, 0.0).astype(BF)

    def hit(places, row):
        wide = jnp.broadcast_to(row.astype(BF), places.shape)
        return jnp.where(places == wide, one, zero)

    def geometry(s):
        meta = meta_s[s]
        src = 2.0 * meta[0:1, 0:ES] + meta[0:1, ES : 2 * ES]
        dst = 2.0 * meta[1:2, 0:ES] + meta[1:2, ES : 2 * ES]
        ec = meta[15:16, 128:256]
        live = jnp.where(lane_e < jnp.concatenate([ec, ec], axis=1), 1.0, 0.0)
        lanes = slice(s * ES, (s + 1) * ES)
        for base, row in ((0, src), (ATOMS, dst)):
            for j in range(4):
                oht_s[base + BLK * j : base + BLK * (j + 1), lanes] = hit(sub_e, row - float(BLK * j))
        posp = posp_s[...]
        ps = nn(posp, oht_s[0:ATOMS, lanes])
        pd = nn(posp, oht_s[ATOMS : 2 * ATOMS, lanes])
        ps = (ps[6:9] + ps[9:12]) + ps[12:15]
        pd = (pd[6:9] + pd[9:12]) + pd[12:15]
        vec = pd - ps
        sq = vec * vec
        dist = jnp.sqrt(sq[0:1] + sq[1:2] + sq[2:3] + 0.25)
        inv = 1.0 / dist
        geo_s[s] = jnp.concatenate([src, dst, live, dist, vec * inv, inv], axis=0)

    def forward(s):
        geo = geo_s[s]
        meta = meta_s[s]
        unit = geo[4:7]
        tc = 8.0 * meta[15:16, 256:384] + meta[15:16, 384:512]
        cols = jnp.transpose(geo)
        ohs = onehot(lane_a == cols[:, 0:1])
        ohd = onehot(lane_a == cols[:, 1:2])
        ohd_s[s] = ohd
        t = (cols[:, 3:4] - centers) * inv_width
        basis = jnp.exp(-(t * t)) * cols[:, 2:3]
        bt_s[:, s * ES : (s + 1) * ES] = jnp.transpose(basis).astype(BF)
        q = nn(ohs, ab_s[0:ATOMS, :]) + nn(ohd, ab_s[ATOMS : 2 * ATOMS, :])
        radial = nn(basis.astype(BF), wr_ref[...])
        a = 1.0 + jnp.tanh(q)
        sil = q * a
        msg = (sil * radial).astype(BF)
        msg_s[s] = msg
        f_s[s] = (radial * (a + sil * (2.0 - a))).astype(BF)
        sg_s[s] = sil.astype(BF)
        m2 = nn(msg, wt_ref[...]).astype(BF)
        m2_s[s] = m2
        for i in range(2):
            rows = slice(BLK * i, BLK * (i + 1))
            limit = jnp.concatenate([tc] * 4, axis=1) - float(TPB * i)
            tin = meta[2 + i : 3 + i, :]
            tout = jnp.where(lane_t < limit, meta[4 + i : 5 + i, :], -1.0)
            count = nt(hit(sub_t, tout), hit(sub_t, tin)) * cols[rows, 2:3]
            n_s[2 * s + i] = count
            gram = (
                cols[rows, 4:5] * unit[0:1, rows]
                + cols[rows, 5:6] * unit[1:2, rows]
                + cols[rows, 6:7] * unit[2:3, rows]
            )
            mix = count * gram
            tt_s[2 * s + i] = jnp.transpose(mix).astype(BF)
            upd = msg[rows].astype(F32) + nn(mix.astype(BF), m2[rows])
            upd_s[s * ES + BLK * i : s * ES + BLK * (i + 1), :] = upd.astype(BF)

    for s in range(NG):
        geometry(s)
    h = h_s[...]
    loads[0].wait()
    ab_s[0:ATOMS, :] = (0.5 * nn(h, ws_ref[...])).astype(BF)
    loads[1].wait()
    ab_s[ATOMS : 2 * ATOMS, :] = (0.5 * nn(h, wd_ref[...])).astype(BF)
    for load in loads[2:]:
        load.wait()
    for s in range(NG):
        forward(s)

    agg = nn(oht_s[ATOMS : 2 * ATOMS, :], upd_s[...]).astype(BF)
    aggb_s[...] = agg
    z = nn(agg, wo_ref[...])
    sig = 0.5 + 0.5 * jnp.tanh(0.5 * z)
    out = z * sig
    we = we_ref[...].astype(F32)
    x = h_s[...].astype(F32) + out
    atom_energy = jnp.sum(x * we, axis=1, keepdims=True)
    member = jnp.where(
        lax.broadcasted_iota(jnp.int32, (ATOMS, 16), 1).astype(F32) == gid_col, 1.0, 0.0
    )
    energy_ref[...] = jnp.sum(member * atom_energy, axis=0, keepdims=True)
    cot = jnp.sum(member * ecot_ref[...], axis=1, keepdims=True)
    cot_s[...] = jnp.broadcast_to(cot, (ATOMS, 128))
    ge_s[...] = jnp.sum(x * cot, axis=0, keepdims=True)
    dz = (cot * we * (sig + out * (1.0 - sig))).astype(BF)
    dzb_s[...] = dz
    ac_s[...] = nt(dz, wo_ref[...]).astype(BF)

    def backward(s):
        edges = slice(s * ES, (s + 1) * ES)
        geo = geo_s[s]
        cols = jnp.transpose(geo)
        ug = nn(ohd_s[s], ac_s[...])
        ugb = ug.astype(BF)
        m2 = m2_s[s]
        halves, turns = [], []
        for i in range(2):
            rows = slice(BLK * i, BLK * (i + 1))
            halves.append(nn(tt_s[2 * s + i], ugb[rows]).astype(BF))
            dgram = n_s[2 * s + i] * nt(ugb[rows], m2[rows])
            both = dgram + jnp.transpose(dgram)
            turns.append(
                jnp.concatenate(
                    [jnp.sum(both * cols[rows, a : a + 1], axis=0, keepdims=True) for a in (4, 5, 6)], axis=0
                )
            )
        dm2 = jnp.concatenate(halves, axis=0)
        dm2_s[edges, :] = dm2
        dmsg = ug + nn(dm2, wtt_s[...])
        dpre_s[edges, :] = (dmsg * f_s[s].astype(F32)).astype(BF)
        drad = (dmsg * sg_s[s].astype(F32)).astype(BF)
        drad_s[edges, :] = drad
        t = (cols[:, 3:4] - centers) * inv_width
        slope = nt(drad, wr_ref[...]) * (jnp.exp(-(t * t)) * (t * (-2.0 * inv_width)))
        ddist = jnp.sum(jnp.transpose(slope), axis=0, keepdims=True) * geo[2:3]
        unit = geo[4:7]
        du = jnp.concatenate(turns, axis=1)
        along = du * unit
        along = along[0:1] + along[1:2] + along[2:3]
        dv = geo[7:8] * (du - unit * along) + unit * ddist
        top = dv.astype(BF).astype(F32)
        dv_s[:, edges] = jnp.concatenate([top, dv - top, jnp.zeros((10, ES), F32)], axis=0).astype(BF)

    wtt_s[...] = jnp.transpose(wt_ref[...])
    for s in range(NG):
        backward(s)

    own = pl.multiple_of(me * AT, AT)
    ohs_own = oht_s[pl.ds(own, AT), :]
    ohd_own = oht_s[pl.ds(ATOMS + own, AT), :]
    group = lax.div(my_slice, 4)
    block = pl.ds(pl.multiple_of(lax.rem(my_slice, 4) * 128, 128), 128)
    side = pl.ds(pl.multiple_of(group * ATOMS, ATOMS), ATOMS)
    rows_t = tn(h_s[:, block], oht_s[side, :]).astype(BF)
    sums = nn(jnp.concatenate([rows_t, ohs_own, ohd_own], axis=0), dpre_s[...])
    a_s[...] = 0.5 * sums[0:BLK]
    own_s_ref[...] = (0.5 * sums[BLK : 2 * BLK]).astype(BF)
    cot_ref[...] = cot_s[pl.ds(own, AT), :]
    pos = nt(dv_s[...], ohd_own - ohs_own)
    pos = pos[0:3] + pos[3:6]
    for i in range(3):
        pos_out_ref[i] = pos[i : i + 1]

    @pl.when(group == 0)
    def _():
        for_trip = [msg_s[s, :, block] for s in range(NG)]
        b_s[...] = tn(jnp.concatenate(for_trip, axis=0), dm2_s[...])

    @pl.when(group == 1)
    def _():
        b_s[...] = tn(aggb_s[:, block], dzb_s[...])

    r_s[...] = nn(bt_s[pl.ds(pl.multiple_of(my_slice * 16, 16), 16), :], drad_s[...])
    ge = ge_s[:, block]
    for u in range(4):
        for v in range(4):
            cols = slice(128 * v, 128 * v + 128)
            chunk = jnp.concatenate(
                [
                    a_s[32 * u : 32 * u + 32, cols],
                    b_s[32 * u : 32 * u + 32, cols],
                    r_s[4 * u : 4 * u + 4, cols],
                    ge,
                    jnp.zeros((CH - 69, 128), F32),
                ],
                axis=0,
            )
            pay_ref[lax.rem(u - my_u + 4, 4), v] = chunk.astype(BF)


def batch(me, part, u, own, other, ws, wd, wr, wt, wo, we, ecot):
    vm = pl.BlockSpec(memory_space=pltpu.VMEM)
    sm = pl.BlockSpec(memory_space=pltpu.SMEM)
    V = pltpu.VMEM
    return pl.pallas_call(
        main_kernel,
        out_shape=(
            jax.ShapeDtypeStruct((1, 16), F32),
            jax.ShapeDtypeStruct((3, 1, AT), F32),
            jax.ShapeDtypeStruct((2 * AT, D), BF),
            jax.ShapeDtypeStruct((AT, 128), F32),
            jax.ShapeDtypeStruct((4, 4, CH, 128), BF),
        ),
        in_specs=[sm] * 3 + [vm] * 2 + [pl.BlockSpec(memory_space=pltpu.HBM)] * 5 + [vm] * 2,
        out_specs=(vm,) * 5,
        scratch_shapes=[
            V((ATOMS, D), BF),
            V((NG, 16, D), F32),
            V((2 * ATOMS, D), BF),
            V((16, ATOMS), BF),
            V((2 * ATOMS, EDGES), BF),
            V((NG, ES, ATOMS), BF),
            V((NG, 8, ES), F32),
            V((NG, ES, D), BF),
            V((NG, ES, D), BF),
            V((NG, ES, D), BF),
            V((NG, ES, D), BF),
            V((2 * NG, BLK, BLK), F32),
            V((2 * NG, BLK, BLK), BF),
            V((EDGES, D), BF),
            V((ATOMS, D), BF),
            V((ATOMS, D), BF),
            V((ATOMS, D), BF),
            V((ATOMS, 128), F32),
            V((1, D), F32),
            V((K, EDGES), BF),
            V((EDGES, D), BF),
            V((EDGES, D), BF),
            V((EDGES, D), BF),
            V((16, EDGES), BF),
            V((BLK, D), F32),
            V((BLK, D), F32),
            V((16, D), F32),
            V((D, D), BF),
            V((D, D), BF),
            V((K, D), BF),
            V((D, D), BF),
            V((D, D), BF),
            pltpu.SemaphoreType.DMA((5,)),
            V((D, D), BF),
        ],
        compiler_params=pltpu.CompilerParams(vmem_limit_bytes=53760 * 1024),
        name="batch",
    )(me, part, u, own, other, ws, wd, wr, wt, wo, we, ecot)


def node_kernel(sums_ref, cot_ref, ws_ref, wd_ref, we_ref, out_ref):
    out_ref[...] = (
        cot_ref[:, 0:1] * we_ref[...].astype(F32)
        + nt(sums_ref[0:AT, :], ws_ref[...])
        + nt(sums_ref[AT : 2 * AT, :], wd_ref[...])
    )


def node(sums, cot, ws, wd, we):
    vm = pl.BlockSpec(memory_space=pltpu.VMEM)
    return pl.pallas_call(
        node_kernel,
        out_shape=jax.ShapeDtypeStruct((AT, D), F32),
        in_specs=[vm] * 5,
        out_specs=vm,
        name="node",
    )(sums, cot, ws, wd, we)


def place_kernel(c, x_ref, y_ref, slice_ref, ref, *rest):
    gs_ref, gd_ref, gr_ref, gt_ref, go_ref, ge_ref, first, second, low, radial, energy, sems = rest[-12:]
    x, y, mine = x_ref[0], y_ref[0], slice_ref[0]
    pc = (mine & 1) ^ c
    my_u = jnp.where(pc == 0, x, y)

    for kz in range(4):

        def body(ku, carry, kz=kz):
            u = lax.rem(my_u - ku + 4, 4)
            rows = pl.ds(pl.multiple_of(u * 32, 32), 32)
            for v in range(4):
                cols = slice(128 * v, 128 * (v + 1))
                tile = ref[16 * ku + 4 * kz + v].astype(F32)
                first[kz, rows, cols] = tile[0:32]
                second[kz, rows, cols] = tile[32:64]
                low[4 * kz + u, :, cols] = tile[64:72]
            return carry

        lax.fori_loop(0, 4, body, 0, unroll=True)
        g = lax.bitwise_xor(mine, 2 * kz + c)
        block = pl.ds(pl.multiple_of((g & 3) * 128, 128), 128)

        def send(near, far, sem):
            pltpu.make_async_copy(near, far, sem).start()

        @pl.when(g < 4)
        def _():
            send(first.at[kz], gs_ref.at[block], sems.at[0, kz])
            send(second.at[kz], gt_ref.at[block], sems.at[1, kz])

        @pl.when(g >= 4)
        def _():
            send(first.at[kz], gd_ref.at[block], sems.at[0, kz])
            send(second.at[kz], go_ref.at[block], sems.at[1, kz])

        for u in range(4):
            radial[kz, 4 * u : 4 * u + 4, :] = low[4 * kz + u, 0:4, :]
        send(radial.at[kz], gr_ref.at[pl.ds(pl.multiple_of(g * 16, 16), 16)], sems.at[2, kz])

        @pl.when(g < 4)
        def _():
            energy[kz] = low[4 * kz, 4:5, 0:128]
            copy = pltpu.make_async_copy(energy.at[kz], ge_ref.at[:, block], sems.at[3, kz])
            copy.start()
            copy.wait()

    for kz in range(4):
        pltpu.make_async_copy(first.at[kz], gs_ref.at[0:128], sems.at[0, kz]).wait()
        pltpu.make_async_copy(second.at[kz], gt_ref.at[0:128], sems.at[1, kz]).wait()
        pltpu.make_async_copy(radial.at[kz], gr_ref.at[0:16], sems.at[2, kz]).wait()


def place(c, x, y, part, pieces, *before):
    vm = pl.BlockSpec(memory_space=pltpu.VMEM)
    sm = pl.BlockSpec(memory_space=pltpu.SMEM)
    far = pl.BlockSpec(memory_space=pl.ANY)
    big = jax.ShapeDtypeStruct((D, D), F32)
    return pl.pallas_call(
        functools.partial(place_kernel, c),
        out_shape=(big, big, jax.ShapeDtypeStruct((K, D), F32), big, big, jax.ShapeDtypeStruct((1, D), F32)),
        in_specs=[sm] * 3 + [vm] + [far] * len(before),
        out_specs=(far,) * 6,
        scratch_shapes=[
            pltpu.VMEM((4, 128, D), F32),
            pltpu.VMEM((4, 128, D), F32),
            pltpu.VMEM((16, 8, D), F32),
            pltpu.VMEM((4, 16, D), F32),
            pltpu.VMEM((4, 1, 128), F32),
            pltpu.SemaphoreType.DMA((4, 4)),
        ],
        input_output_aliases={4 + i: i for i in range(len(before))},
        compiler_params=pltpu.CompilerParams(vmem_limit_bytes=30 * 1024 * 1024),
        name="place",
    )(x, y, part, pieces, *before)


def moves(fn):
    pairs = []
    for zh in range(2):
        for x in range(4):
            for y in range(4):
                for zl in range(4):
                    for c in range(2):
                        u, v = (x, y) if c == 0 else (y, x)
                        zh2, u2, v2, zl2, c2 = fn(zh, u, v, zl, c)
                        x2, y2 = (u2, v2) if c == 0 else (v2, u2)
                        here = (zh * 16 + x * 4 + y) * 8 + zl * 2 + c
                        there = (zh2 * 16 + x2 * 4 + y2) * 8 + zl2 * 2 + c2
                        pairs.append((here, there))
    return pairs


def shift(value, zh=0, u=0, v=0, zl=0, c=0):
    def fn(zh_, u_, v_, zl_, c_):
        return zh_ ^ zh, (u_ + u) % 4, (v_ + v) % 4, zl_ ^ zl, c_ ^ c

    return lax.ppermute(value, AXES, moves(fn))


def join(*parts):
    return jnp.concatenate(parts, axis=0)


ORDER = (1, 3, 2)


def total(a, b, c, d):
    a, b, c, d = (part.astype(F32) for part in (a, b, c, d))
    return ((a + b) + (c + d)).astype(BF)


def per_device(
    node_feats,
    positions,
    edge_src,
    edge_dst,
    edge_count,
    trip_in,
    trip_out,
    trip_count,
    graph_ids,
    w_src,
    w_dst,
    w_radial,
    w_trip,
    w_out,
    w_energy,
    energy_cot,
):
    dp, graph = lax.axis_index("dp"), lax.axis_index("graph")
    zh, x, y = lax.shift_right_logical(dp, 4), lax.shift_right_logical(dp, 2) & 3, dp & 3
    core = graph & 1
    u = jnp.where(core == 0, x, y)
    part = graph ^ (6 * zh)
    me, x, y, u, part = (a.astype(jnp.int32).reshape(1) for a in (graph, x, y, u, part))
    piece = pack(
        me,
        node_feats[0],
        jnp.swapaxes(positions, 0, 1),
        edge_src,
        edge_dst,
        edge_count,
        trip_in,
        trip_out,
        trip_count,
        graph_ids,
    )[None]
    own = join(piece, *[shift(piece, zl=k) for k in (1, 2, 3)])
    other = shift(own, c=1)
    we = w_energy.reshape(1, D)
    energy, pos_grad, sums, cot, payload = batch(
        me, part, u, own, other, w_src, w_dst, w_radial, w_trip, w_out, we, energy_cot
    )
    node_grad = node(sums, cot, w_src, w_dst, we)
    one, three, two = [shift(payload[k], u=k) for k in ORDER]
    held = total(payload[0], two, one, three)
    one, three, two = [shift(held, v=k) for k in ORDER]
    held = total(held, two, one, three)
    held = (held.astype(F32) + shift(held, zh=1, zl=3).astype(F32)).astype(BF)
    held = join(held, *[shift(held, zl=k) for k in (1, 2, 3)])
    one, three, two = [shift(held, u=k) for k in ORDER]
    held = join(held, one, two, three)
    other = shift(held, c=1)
    gs, gd, gr, gt, go, ge = place(1, x, y, part, other, *place(0, x, y, part, held))
    return (energy, jnp.swapaxes(pos_grad, 0, 1), node_grad[None], gs, gd, gr, gt, go, ge.reshape(D))


def solution(mesh):
    placed = (
        P("dp", "graph", None),
        P("dp", None, "graph"),
        P("dp", "graph"),
        P("dp", "graph"),
        P("dp", "graph"),
        P("dp", "graph"),
        P("dp", "graph"),
        P("dp", "graph"),
        P("dp", "graph"),
        P(),
        P(),
        P(),
        P(),
        P(),
        P(),
        P("dp", None),
    )
    return jax.shard_map(
        per_device,
        mesh=mesh,
        in_specs=placed,
        out_specs=(
            P("dp", None),
            P("dp", None, "graph"),
            P("dp", "graph", None),
            P(),
            P(),
            P(),
            P(),
            P(),
            P(),
        ),
        check_vma=False,
    )
```

```python
import functools

import jax
import jax.numpy as jnp
from jax import lax
from jax.experimental import pallas as pl
from jax.experimental.pallas import tpu as pltpu
from jax.sharding import PartitionSpec as P

BF = jnp.bfloat16
F32 = jnp.float32
NG = 8
AT = 64
ATOMS = 512
ES = 256
EDGES = 2048
D = 512
K = 128
BLK = 128
TPB = 512
PIECE = 80
CH = 72
AXES = ("dp", "graph")
HI = lax.Precision.HIGHEST


def nn(a, b):
    return lax.dot_general(a, b, (((1,), (0,)), ((), ())), preferred_element_type=F32)


def nt(a, b):
    return lax.dot_general(a, b, (((1,), (1,)), ((), ())), preferred_element_type=F32)


def tn(a, b):
    return lax.dot_general(a, b, (((0,), (0,)), ((), ())), preferred_element_type=F32)


def pack_kernel(me_ref, h_ref, pos_ref, src_ref, dst_ref, ec_ref, tin_ref, tout_ref, tc_ref, gid_ref, ecot_ref, wr_ref, out_ref, cot_ref, wr_out, meta):
    cot_ref[...] = ecot_ref[...]
    wr_out[...] = wr_ref[...]
    odd = lax.rem(me_ref[0], 2)
    out_ref[0:AT, :] = h_ref[...]

    def place(row):
        full = jnp.concatenate([row, jnp.zeros_like(row)], axis=1)
        return jnp.where(odd == 1, pltpu.roll(full, AT, 1), full)

    for r, ref in ((0, src_ref), (1, dst_ref)):
        v = ref[...]
        half = lax.shift_right_logical(v, 1)
        meta[r : r + 1, 0:ES] = half.astype(F32)
        meta[r : r + 1, ES : 2 * ES] = (v - 2 * half).astype(F32)
    for r, ref in ((2, tin_ref), (4, tout_ref)):
        v = ref[...].astype(F32)
        meta[r : r + 1, :] = v[:, 0:TPB]
        meta[r + 1 : r + 2, :] = v[:, TPB : 2 * TPB]
    p = jnp.concatenate([pos_ref[i] for i in range(3)], axis=0)
    p1 = p.astype(BF).astype(F32)
    p2 = (p - p1).astype(BF).astype(F32)
    p3 = (p - p1) - p2
    meta[6:16, :] = jnp.zeros((10, D), F32)
    meta[6:9, 0:128] = place(p1)
    meta[9:12, 0:128] = place(p2)
    meta[12:15, 0:128] = place(p3)
    meta[15:16, 0:128] = place(gid_ref[...].astype(F32))
    tc = tc_ref[0, 0]
    tc_half = lax.shift_right_logical(tc, 3)
    meta[15:16, 128:256] = jnp.full((1, 128), ec_ref[0, 0].astype(F32))
    meta[15:16, 256:384] = jnp.full((1, 128), tc_half.astype(F32))
    meta[15:16, 384:512] = jnp.full((1, 128), (tc - 8 * tc_half).astype(F32))
    out_ref[AT:PIECE, :] = meta[...].astype(BF)


def pack(me, h, pos, src, dst, ec, tin, tout, tc, gid, ecot, wr):
    vm = pl.BlockSpec(memory_space=pltpu.VMEM)
    sm = pl.BlockSpec(memory_space=pltpu.SMEM)
    return pl.pallas_call(
        pack_kernel,
        out_shape=(jax.ShapeDtypeStruct((PIECE, D), BF), jax.ShapeDtypeStruct((1, 16), F32), jax.ShapeDtypeStruct((K, D), BF)),
        in_specs=[sm, vm, vm, vm, vm, sm, vm, vm, sm, vm, vm, vm],
        out_specs=(vm,) * 3,
        scratch_shapes=[pltpu.VMEM((16, D), F32)],
        name="pack",
    )(me, h, pos, src, dst, ec, tin, tout, tc, gid, ecot, wr)


def main_kernel(
    me_ref,
    slice_ref,
    u_ref,
    own_ref,
    other_ref,
    ws_hbm,
    wd_hbm,
    wr_ref,
    wt_hbm,
    wo_hbm,
    we_ref,
    ecot_ref,
    energy_ref,
    pos_out_ref,
    own_s_ref,
    cot_ref,
    pay_ref,
    h_s,
    meta_s,
    ab_s,
    posp_s,
    oht_s,
    ohd_s,
    geo_s,
    msg_s,
    f_s,
    sg_s,
    m2_s,
    n_s,
    tt_s,
    upd_s,
    aggb_s,
    dzb_s,
    ac_s,
    cot_s,
    ge_s,
    bt_s,
    dm2_s,
    dpre_s,
    drad_s,
    dv_s,
    a_s,
    b_s,
    r_s,
    ws_ref,
    wd_ref,
    wt_ref,
    wo_ref,
    sems,
    wtt_s,
):
    loads = [
        pltpu.make_async_copy(far, near, sems.at[i])
        for i, (far, near) in enumerate(
            ((ws_hbm, ws_ref), (wd_hbm, wd_ref), (wt_hbm, wt_ref), (wo_hbm, wo_ref))
        )
    ]
    for load in loads:
        load.start()
    me, my_slice, my_u = me_ref[0], slice_ref[0], u_ref[0]
    for near, ref in ((0, own_ref), (1, other_ref)):
        for kz in range(4):
            shard = me ^ (2 * kz + near)
            h_s[pl.ds(pl.multiple_of(shard * AT, AT), AT), :] = ref[kz, 0:AT, :]
            meta_s[shard] = ref[kz, AT:PIECE, :].astype(F32)
    gid_rows = []
    for j in range(4):
        both = meta_s[2 * j, :, 0:128] + meta_s[2 * j + 1, :, 0:128]
        posp_s[:, 128 * j : 128 * (j + 1)] = both.astype(BF)
        gid_rows.append(both[15:16, :])
    gid_row = jnp.concatenate(gid_rows, axis=1)
    gid_col = jnp.transpose(jnp.broadcast_to(gid_row, (8, ATOMS)))[:, 0:1]

    step = 16.0 / K
    inv_width = K / 24.0
    sub_e = lax.broadcasted_iota(jnp.int32, (BLK, ES), 0).astype(F32).astype(BF)
    sub_t = lax.broadcasted_iota(jnp.int32, (BLK, TPB), 0).astype(F32).astype(BF)
    lane_a = lax.broadcasted_iota(jnp.int32, (ES, ATOMS), 1).astype(F32)
    lane_e = lax.broadcasted_iota(jnp.int32, (1, ES), 1).astype(F32)
    lane_t = lax.broadcasted_iota(jnp.int32, (1, TPB), 1).astype(F32)
    centers = lax.broadcasted_iota(jnp.int32, (1, K), 1).astype(F32) * step
    one, zero = jnp.ones((), BF), jnp.zeros((), BF)

    def onehot(cond):
        return jnp.where(cond, 1.0, 0.0).astype(BF)

    def hit(places, row):
        wide = jnp.broadcast_to(row.astype(BF), places.shape)
        return jnp.where(places == wide, one, zero)

    def geometry(s):
        meta = meta_s[s]
        src = 2.0 * meta[0:1, 0:ES] + meta[0:1, ES : 2 * ES]
        dst = 2.0 * meta[1:2, 0:ES] + meta[1:2, ES : 2 * ES]
        ec = meta[15:16, 128:256]
        live = jnp.where(lane_e < jnp.concatenate([ec, ec], axis=1), 1.0, 0.0)
        lanes = slice(s * ES, (s + 1) * ES)
        for base, row in ((0, src), (ATOMS, dst)):
            for j in range(4):
                oht_s[base + BLK * j : base + BLK * (j + 1), lanes] = hit(sub_e, row - float(BLK * j))
        posp = posp_s[...]
        ps = nn(posp, oht_s[0:ATOMS, lanes])
        pd = nn(posp, oht_s[ATOMS : 2 * ATOMS, lanes])
        ps = (ps[6:9] + ps[9:12]) + ps[12:15]
        pd = (pd[6:9] + pd[9:12]) + pd[12:15]
        vec = pd - ps
        sq = vec * vec
        dist = jnp.sqrt(sq[0:1] + sq[1:2] + sq[2:3] + 0.25)
        inv = 1.0 / dist
        geo_s[s] = jnp.concatenate([src, dst, live, dist, vec * inv, inv], axis=0)

    def gather(s):
        cols = jnp.transpose(geo_s[s])
        ohs = onehot(lane_a == cols[:, 0:1])
        ohd = onehot(lane_a == cols[:, 1:2])
        ohd_s[s] = ohd
        t = (cols[:, 3:4] - centers) * inv_width
        basis = jnp.exp(-(t * t)) * cols[:, 2:3]
        bt_s[:, s * ES : (s + 1) * ES] = jnp.transpose(basis).astype(BF)
        q = nn(ohs, ab_s[0:ATOMS, :]) + nn(ohd, ab_s[ATOMS : 2 * ATOMS, :])
        return s, cols, q, nn(basis.astype(BF), wr_ref[...])

    def message(s, cols, q, radial):
        a = 1.0 + jnp.tanh(q)
        sil = q * a
        msg = (sil * radial).astype(BF)
        msg_s[s] = msg
        f_s[s] = (radial * (a + sil * (2.0 - a))).astype(BF)
        sg_s[s] = sil.astype(BF)
        m2 = nn(msg, wt_ref[...]).astype(BF)
        m2_s[s] = m2
        meta = meta_s[s]
        unit = geo_s[s][4:7]
        tc = 8.0 * meta[15:16, 256:384] + meta[15:16, 384:512]
        mixes = []
        for i in range(2):
            rows = slice(BLK * i, BLK * (i + 1))
            limit = jnp.concatenate([tc] * 4, axis=1) - float(TPB * i)
            tin = meta[2 + i : 3 + i, :]
            tout = jnp.where(lane_t < limit, meta[4 + i : 5 + i, :], -1.0)
            count = nt(hit(sub_t, tout), hit(sub_t, tin)) * cols[rows, 2:3]
            n_s[2 * s + i] = count
            gram = (
                cols[rows, 4:5] * unit[0:1, rows]
                + cols[rows, 5:6] * unit[1:2, rows]
                + cols[rows, 6:7] * unit[2:3, rows]
            )
            mix = count * gram
            tt_s[2 * s + i] = jnp.transpose(mix).astype(BF)
            mixes.append(mix.astype(BF))
        return s, msg, m2, mixes

    def update(s, msg, m2, mixes):
        for i in range(2):
            rows = slice(BLK * i, BLK * (i + 1))
            upd = msg[rows].astype(F32) + nn(mixes[i], m2[rows])
            upd_s[s * ES + BLK * i : s * ES + BLK * (i + 1), :] = upd.astype(BF)

    def staged(*stages):
        waiting = [None] * len(stages)
        for turn in range(NG + len(stages) - 1):
            for k in reversed(range(len(stages))):
                if k == 0:
                    given = (turn,) if turn < NG else None
                else:
                    given = waiting[k - 1]
                waiting[k] = None if given is None else stages[k](*given)

    for s in range(NG):
        geometry(s)
    h = h_s[...]
    loads[0].wait()
    ab_s[0:ATOMS, :] = (0.5 * nn(h, ws_ref[...])).astype(BF)
    loads[1].wait()
    ab_s[ATOMS : 2 * ATOMS, :] = (0.5 * nn(h, wd_ref[...])).astype(BF)
    for load in loads[2:]:
        load.wait()
    staged(gather, message, update)

    agg = nn(oht_s[ATOMS : 2 * ATOMS, :], upd_s[...]).astype(BF)
    aggb_s[...] = agg
    z = nn(agg, wo_ref[...])
    sig = 0.5 + 0.5 * jnp.tanh(0.5 * z)
    out = z * sig
    we = we_ref[...].astype(F32)
    x = h_s[...].astype(F32) + out
    atom_energy = jnp.sum(x * we, axis=1, keepdims=True)
    member = jnp.where(
        lax.broadcasted_iota(jnp.int32, (ATOMS, 16), 1).astype(F32) == gid_col, 1.0, 0.0
    )
    energy_ref[...] = jnp.sum(member * atom_energy, axis=0, keepdims=True)
    cot = jnp.sum(member * ecot_ref[...], axis=1, keepdims=True)
    cot_s[...] = jnp.broadcast_to(cot, (ATOMS, 128))
    ge_s[...] = jnp.sum(x * cot, axis=0, keepdims=True)
    dz = (cot * we * (sig + out * (1.0 - sig))).astype(BF)
    dzb_s[...] = dz
    ac_s[...] = nt(dz, wo_ref[...]).astype(BF)

    def fetch(s):
        return s, nn(ohd_s[s], ac_s[...])

    def mixed(s, ug):
        geo = geo_s[s]
        cols = jnp.transpose(geo)
        ugb = ug.astype(BF)
        m2 = m2_s[s]
        halves, grams = [], []
        for i in range(2):
            rows = slice(BLK * i, BLK * (i + 1))
            halves.append(nn(tt_s[2 * s + i], ugb[rows]).astype(BF))
            grams.append(n_s[2 * s + i] * nt(ugb[rows], m2[rows]))
        dm2 = jnp.concatenate(halves, axis=0)
        dm2_s[s * ES : (s + 1) * ES, :] = dm2
        return s, geo, cols, ug, dm2, grams

    def spread(s, geo, cols, ug, dm2, grams):
        edges = slice(s * ES, (s + 1) * ES)
        dmsg = ug + nn(dm2, wtt_s[...])
        dpre_s[edges, :] = (dmsg * f_s[s].astype(F32)).astype(BF)
        drad = (dmsg * sg_s[s].astype(F32)).astype(BF)
        drad_s[edges, :] = drad
        return s, geo, cols, drad, grams

    def turn_back(s, geo, cols, drad, grams):
        edges = slice(s * ES, (s + 1) * ES)
        turns = []
        for i in range(2):
            rows = slice(BLK * i, BLK * (i + 1))
            both = grams[i] + jnp.transpose(grams[i])
            turns.append(
                jnp.concatenate(
                    [jnp.sum(both * cols[rows, a : a + 1], axis=0, keepdims=True) for a in (4, 5, 6)], axis=0
                )
            )
        t = (cols[:, 3:4] - centers) * inv_width
        slope = nt(drad, wr_ref[...]) * (jnp.exp(-(t * t)) * (t * (-2.0 * inv_width)))
        ddist = jnp.sum(jnp.transpose(slope), axis=0, keepdims=True) * geo[2:3]
        unit = geo[4:7]
        du = jnp.concatenate(turns, axis=1)
        along = du * unit
        along = along[0:1] + along[1:2] + along[2:3]
        dv = geo[7:8] * (du - unit * along) + unit * ddist
        top = dv.astype(BF).astype(F32)
        dv_s[:, edges] = jnp.concatenate([top, dv - top, jnp.zeros((10, ES), F32)], axis=0).astype(BF)

    wtt_s[...] = jnp.transpose(wt_ref[...])
    staged(fetch, mixed, spread, turn_back)

    own = pl.multiple_of(me * AT, AT)
    ohs_own = oht_s[pl.ds(own, AT), :]
    ohd_own = oht_s[pl.ds(ATOMS + own, AT), :]
    group = lax.div(my_slice, 4)
    block = pl.ds(pl.multiple_of(lax.rem(my_slice, 4) * 128, 128), 128)
    side = pl.ds(pl.multiple_of(group * ATOMS, ATOMS), ATOMS)
    rows_t = tn(h_s[:, block], oht_s[side, :]).astype(BF)
    sums = nn(jnp.concatenate([rows_t, ohs_own, ohd_own], axis=0), dpre_s[...])
    a_s[...] = 0.5 * sums[0:BLK]
    own_s_ref[...] = (0.5 * sums[BLK : 2 * BLK]).astype(BF)
    cot_ref[...] = cot_s[pl.ds(own, AT), :]
    pos = nt(dv_s[...], ohd_own - ohs_own)
    pos = pos[0:3] + pos[3:6]
    for i in range(3):
        pos_out_ref[i] = pos[i : i + 1]

    @pl.when(group == 0)
    def _():
        for_trip = [msg_s[s, :, block] for s in range(NG)]
        b_s[...] = tn(jnp.concatenate(for_trip, axis=0), dm2_s[...])

    @pl.when(group == 1)
    def _():
        b_s[...] = tn(aggb_s[:, block], dzb_s[...])

    r_s[...] = nn(bt_s[pl.ds(pl.multiple_of(my_slice * 16, 16), 16), :], drad_s[...])
    ge = ge_s[:, block]
    for u in range(4):
        for v in range(4):
            cols = slice(128 * v, 128 * v + 128)
            chunk = jnp.concatenate(
                [
                    a_s[32 * u : 32 * u + 32, cols],
                    b_s[32 * u : 32 * u + 32, cols],
                    r_s[4 * u : 4 * u + 4, cols],
                    ge,
                    jnp.zeros((CH - 69, 128), F32),
                ],
                axis=0,
            )
            pay_ref[lax.rem(u - my_u + 4, 4), v] = chunk.astype(BF)


def batch(me, part, u, own, other, ws, wd, wr, wt, wo, we, ecot):
    vm = pl.BlockSpec(memory_space=pltpu.VMEM)
    sm = pl.BlockSpec(memory_space=pltpu.SMEM)
    far = pl.BlockSpec(memory_space=pltpu.HBM)
    V = pltpu.VMEM
    return pl.pallas_call(
        main_kernel,
        out_shape=(
            jax.ShapeDtypeStruct((1, 16), F32),
            jax.ShapeDtypeStruct((3, 1, AT), F32),
            jax.ShapeDtypeStruct((2 * AT, D), BF),
            jax.ShapeDtypeStruct((AT, 128), F32),
            jax.ShapeDtypeStruct((4, 4, CH, 128), BF),
        ),
        in_specs=[sm] * 3 + [vm] * 2 + [far] * 2 + [vm] + [far] * 2 + [vm] * 2,
        out_specs=(vm,) * 5,
        scratch_shapes=[
            V((ATOMS, D), BF),
            V((NG, 16, D), F32),
            V((2 * ATOMS, D), BF),
            V((16, ATOMS), BF),
            V((2 * ATOMS, EDGES), BF),
            V((NG, ES, ATOMS), BF),
            V((NG, 8, ES), F32),
            V((NG, ES, D), BF),
            V((NG, ES, D), BF),
            V((NG, ES, D), BF),
            V((NG, ES, D), BF),
            V((2 * NG, BLK, BLK), F32),
            V((2 * NG, BLK, BLK), BF),
            V((EDGES, D), BF),
            V((ATOMS, D), BF),
            V((ATOMS, D), BF),
            V((ATOMS, D), BF),
            V((ATOMS, 128), F32),
            V((1, D), F32),
            V((K, EDGES), BF),
            V((EDGES, D), BF),
            V((EDGES, D), BF),
            V((EDGES, D), BF),
            V((16, EDGES), BF),
            V((BLK, D), F32),
            V((BLK, D), F32),
            V((16, D), F32),
            V((D, D), BF),
            V((D, D), BF),
            V((D, D), BF),
            V((D, D), BF),
            pltpu.SemaphoreType.DMA((4,)),
            V((D, D), BF),
        ],
        compiler_params=pltpu.CompilerParams(vmem_limit_bytes=53760 * 1024),
        name="batch",
    )(me, part, u, own, other, ws, wd, wr, wt, wo, we, ecot)


def node_kernel(sums_ref, cot_ref, ws_ref, wd_ref, we_ref, out_ref):
    out_ref[...] = (
        cot_ref[:, 0:1] * we_ref[...].astype(F32)
        + nt(sums_ref[0:AT, :], ws_ref[...])
        + nt(sums_ref[AT : 2 * AT, :], wd_ref[...])
    )


def node(sums, cot, ws, wd, we):
    vm = pl.BlockSpec(memory_space=pltpu.VMEM)
    return pl.pallas_call(
        node_kernel,
        out_shape=jax.ShapeDtypeStruct((AT, D), F32),
        in_specs=[vm] * 5,
        out_specs=vm,
        name="node",
    )(sums, cot, ws, wd, we)


def place_kernel(c, x_ref, y_ref, slice_ref, ref, *rest):
    gs_ref, gd_ref, gr_ref, gt_ref, go_ref, ge_ref, first, second, low, radial, energy, sems = rest[-12:]
    x, y, mine = x_ref[0], y_ref[0], slice_ref[0]
    pc = (mine & 1) ^ c
    my_u = jnp.where(pc == 0, x, y)

    for kz in range(4):

        def body(ku, carry, kz=kz):
            u = lax.rem(my_u - ku + 4, 4)
            rows = pl.ds(pl.multiple_of(u * 32, 32), 32)
            for v in range(4):
                cols = slice(128 * v, 128 * (v + 1))
                tile = ref[16 * ku + 4 * kz + v].astype(F32)
                first[kz, rows, cols] = tile[0:32]
                second[kz, rows, cols] = tile[32:64]
                low[4 * kz + u, :, cols] = tile[64:72]
            return carry

        lax.fori_loop(0, 4, body, 0, unroll=True)
        g = lax.bitwise_xor(mine, 2 * kz + c)
        block = pl.ds(pl.multiple_of((g & 3) * 128, 128), 128)

        def send(near, far, sem):
            pltpu.make_async_copy(near, far, sem).start()

        @pl.when(g < 4)
        def _():
            send(first.at[kz], gs_ref.at[block], sems.at[0, kz])
            send(second.at[kz], gt_ref.at[block], sems.at[1, kz])

        @pl.when(g >= 4)
        def _():
            send(first.at[kz], gd_ref.at[block], sems.at[0, kz])
            send(second.at[kz], go_ref.at[block], sems.at[1, kz])

        for u in range(4):
            radial[kz, 4 * u : 4 * u + 4, :] = low[4 * kz + u, 0:4, :]
        send(radial.at[kz], gr_ref.at[pl.ds(pl.multiple_of(g * 16, 16), 16)], sems.at[2, kz])

        @pl.when(g < 4)
        def _():
            energy[kz] = low[4 * kz, 4:5, 0:128]
            copy = pltpu.make_async_copy(energy.at[kz], ge_ref.at[:, block], sems.at[3, kz])
            copy.start()
            copy.wait()

    for kz in range(4):
        pltpu.make_async_copy(first.at[kz], gs_ref.at[0:128], sems.at[0, kz]).wait()
        pltpu.make_async_copy(second.at[kz], gt_ref.at[0:128], sems.at[1, kz]).wait()
        pltpu.make_async_copy(radial.at[kz], gr_ref.at[0:16], sems.at[2, kz]).wait()


def place(c, x, y, part, pieces, *before):
    vm = pl.BlockSpec(memory_space=pltpu.VMEM)
    sm = pl.BlockSpec(memory_space=pltpu.SMEM)
    far = pl.BlockSpec(memory_space=pl.ANY)
    big = jax.ShapeDtypeStruct((D, D), F32)
    return pl.pallas_call(
        functools.partial(place_kernel, c),
        out_shape=(big, big, jax.ShapeDtypeStruct((K, D), F32), big, big, jax.ShapeDtypeStruct((1, D), F32)),
        in_specs=[sm] * 3 + [vm] + [far] * len(before),
        out_specs=(far,) * 6,
        scratch_shapes=[
            pltpu.VMEM((4, 128, D), F32),
            pltpu.VMEM((4, 128, D), F32),
            pltpu.VMEM((16, 8, D), F32),
            pltpu.VMEM((4, 16, D), F32),
            pltpu.VMEM((4, 1, 128), F32),
            pltpu.SemaphoreType.DMA((4, 4)),
        ],
        input_output_aliases={4 + i: i for i in range(len(before))},
        compiler_params=pltpu.CompilerParams(vmem_limit_bytes=30 * 1024 * 1024),
        name="place",
    )(x, y, part, pieces, *before)


def moves(fn):
    pairs = []
    for zh in range(2):
        for x in range(4):
            for y in range(4):
                for zl in range(4):
                    for c in range(2):
                        u, v = (x, y) if c == 0 else (y, x)
                        zh2, u2, v2, zl2, c2 = fn(zh, u, v, zl, c)
                        x2, y2 = (u2, v2) if c == 0 else (v2, u2)
                        here = (zh * 16 + x * 4 + y) * 8 + zl * 2 + c
                        there = (zh2 * 16 + x2 * 4 + y2) * 8 + zl2 * 2 + c2
                        pairs.append((here, there))
    return pairs


def shift(value, zh=0, u=0, v=0, zl=0, c=0):
    def fn(zh_, u_, v_, zl_, c_):
        return zh_ ^ zh, (u_ + u) % 4, (v_ + v) % 4, zl_ ^ zl, c_ ^ c

    return lax.ppermute(value, AXES, moves(fn))


def join(*parts):
    return jnp.concatenate(parts, axis=0)


ORDER = (1, 3, 2)


def total(a, b, c, d):
    a, b, c, d = (part.astype(F32) for part in (a, b, c, d))
    return ((a + b) + (c + d)).astype(BF)


def per_device(
    node_feats,
    positions,
    edge_src,
    edge_dst,
    edge_count,
    trip_in,
    trip_out,
    trip_count,
    graph_ids,
    w_src,
    w_dst,
    w_radial,
    w_trip,
    w_out,
    w_energy,
    energy_cot,
):
    dp, graph = lax.axis_index("dp"), lax.axis_index("graph")
    zh, x, y = lax.shift_right_logical(dp, 4), lax.shift_right_logical(dp, 2) & 3, dp & 3
    core = graph & 1
    u = jnp.where(core == 0, x, y)
    part = graph ^ (6 * zh)
    me, x, y, u, part = (a.astype(jnp.int32).reshape(1) for a in (graph, x, y, u, part))
    piece, ecot, wr = pack(
        me,
        node_feats[0],
        jnp.swapaxes(positions, 0, 1),
        edge_src,
        edge_dst,
        edge_count,
        trip_in,
        trip_out,
        trip_count,
        graph_ids,
        energy_cot,
        w_radial,
    )
    piece = piece[None]
    own = join(piece, *[shift(piece, zl=k) for k in (1, 2, 3)])
    other = shift(own, c=1)
    we = w_energy.reshape(1, D)
    energy, pos_grad, sums, cot, payload = batch(
        me, part, u, own, other, w_src, w_dst, wr, w_trip, w_out, we, ecot
    )
    node_grad = node(sums, cot, w_src, w_dst, we)
    one, three, two = [shift(payload[k], u=k) for k in ORDER]
    held = total(payload[0], two, one, three)
    one, three, two = [shift(held, v=k) for k in ORDER]
    held = total(held, two, one, three)
    held = (held.astype(F32) + shift(held, zh=1, zl=3).astype(F32)).astype(BF)
    held = join(held, *[shift(held, zl=k) for k in (1, 2, 3)])
    one, three, two = [shift(held, u=k) for k in ORDER]
    one, three, two, node_grad = lax.optimization_barrier((one, three, two, node_grad))
    held = join(held, one, two, three)
    other = shift(held, c=1)
    gs, gd, gr, gt, go, ge = place(1, x, y, part, other, *place(0, x, y, part, held))
    return (energy, jnp.swapaxes(pos_grad, 0, 1), node_grad[None], gs, gd, gr, gt, go, ge.reshape(D))


def solution(mesh):
    placed = (
        P("dp", "graph", None),
        P("dp", None, "graph"),
        P("dp", "graph"),
        P("dp", "graph"),
        P("dp", "graph"),
        P("dp", "graph"),
        P("dp", "graph"),
        P("dp", "graph"),
        P("dp", "graph"),
        P(),
        P(),
        P(),
        P(),
        P(),
        P(),
        P("dp", None),
    )
    return jax.shard_map(
        per_device,
        mesh=mesh,
        in_specs=placed,
        out_specs=(
            P("dp", None),
            P("dp", None, "graph"),
            P("dp", "graph", None),
            P(),
            P(),
            P(),
            P(),
            P(),
            P(),
        ),
        check_vma=False,
    )
```

```python
import functools

import jax
import jax.numpy as jnp
from jax import lax
from jax.experimental import pallas as pl
from jax.experimental.pallas import tpu as pltpu
from jax.sharding import PartitionSpec as P

BF = jnp.bfloat16
F32 = jnp.float32
NG = 8
AT = 64
ATOMS = 512
ES = 256
EDGES = 2048
D = 512
K = 128
BLK = 128
TPB = 512
PIECE = 80
CH = 72
AXES = ("dp", "graph")
HI = lax.Precision.HIGHEST


def nn(a, b):
    return lax.dot_general(a, b, (((1,), (0,)), ((), ())), preferred_element_type=F32)


def nt(a, b):
    return lax.dot_general(a, b, (((1,), (1,)), ((), ())), preferred_element_type=F32)


def tn(a, b):
    return lax.dot_general(a, b, (((0,), (0,)), ((), ())), preferred_element_type=F32)


def pack_kernel(me_ref, h_ref, pos_ref, src_ref, dst_ref, ec_ref, tin_ref, tout_ref, tc_ref, gid_ref, ecot_ref, out_ref, meta):
    odd = lax.rem(me_ref[0], 2)
    out_ref[0:AT, :] = h_ref[...]

    def place(row):
        full = jnp.concatenate([row, jnp.zeros_like(row)], axis=1)
        return jnp.where(odd == 1, pltpu.roll(full, AT, 1), full)

    for r, ref in ((0, src_ref), (1, dst_ref)):
        v = ref[...]
        half = lax.shift_right_logical(v, 1)
        meta[r : r + 1, 0:ES] = half.astype(F32)
        meta[r : r + 1, ES : 2 * ES] = (v - 2 * half).astype(F32)
    for r, ref in ((2, tin_ref), (4, tout_ref)):
        v = ref[...].astype(F32)
        meta[r : r + 1, :] = v[:, 0:TPB]
        meta[r + 1 : r + 2, :] = v[:, TPB : 2 * TPB]
    p = jnp.concatenate([pos_ref[i] for i in range(3)], axis=0)
    p1 = p.astype(BF).astype(F32)
    p2 = (p - p1).astype(BF).astype(F32)
    p3 = (p - p1) - p2
    meta[6:16, :] = jnp.zeros((10, D), F32)
    meta[6:9, 0:128] = place(p1)
    meta[9:12, 0:128] = place(p2)
    meta[12:15, 0:128] = place(p3)
    e = jnp.concatenate([ecot_ref[...], jnp.zeros((1, 112), F32)], axis=1)
    e1 = e.astype(BF).astype(F32)
    e2 = (e - e1).astype(BF).astype(F32)
    meta[6:7, 128:256] = e1
    meta[7:8, 128:256] = e2
    meta[8:9, 128:256] = (e - e1) - e2
    meta[15:16, 0:128] = place(gid_ref[...].astype(F32))
    tc = tc_ref[0, 0]
    tc_half = lax.shift_right_logical(tc, 3)
    meta[15:16, 128:256] = jnp.full((1, 128), ec_ref[0, 0].astype(F32))
    meta[15:16, 256:384] = jnp.full((1, 128), tc_half.astype(F32))
    meta[15:16, 384:512] = jnp.full((1, 128), (tc - 8 * tc_half).astype(F32))
    out_ref[AT:PIECE, :] = meta[...].astype(BF)


def pack(me, h, pos, src, dst, ec, tin, tout, tc, gid, ecot):
    vm = pl.BlockSpec(memory_space=pltpu.VMEM)
    sm = pl.BlockSpec(memory_space=pltpu.SMEM)
    return pl.pallas_call(
        pack_kernel,
        out_shape=jax.ShapeDtypeStruct((PIECE, D), BF),
        in_specs=[sm, vm, vm, vm, vm, sm, vm, vm, sm, vm, vm],
        out_specs=vm,
        scratch_shapes=[pltpu.VMEM((16, D), F32)],
        name="pack",
    )(me, h, pos, src, dst, ec, tin, tout, tc, gid, ecot)


def main_kernel(
    me_ref,
    slice_ref,
    u_ref,
    own_ref,
    other_ref,
    ws_hbm,
    wd_hbm,
    wide_ref,
    wt_hbm,
    wo_hbm,
    energy_ref,
    pos_out_ref,
    own_s_ref,
    cot_ref,
    pay_ref,
    h_s,
    meta_s,
    ab_s,
    posp_s,
    oht_s,
    ohd_s,
    geo_s,
    msg_s,
    f_s,
    sg_s,
    m2_s,
    n_s,
    tt_s,
    upd_s,
    aggb_s,
    dzb_s,
    ac_s,
    cot_s,
    ge_s,
    bt_s,
    dm2_s,
    dpre_s,
    drad_s,
    dv_s,
    a_s,
    b_s,
    r_s,
    ws_ref,
    wd_ref,
    wt_ref,
    wo_ref,
    sems,
    wtt_s,
):
    loads = [
        pltpu.make_async_copy(far, near, sems.at[i])
        for i, (far, near) in enumerate(
            ((ws_hbm, ws_ref), (wd_hbm, wd_ref), (wt_hbm, wt_ref), (wo_hbm, wo_ref))
        )
    ]
    for load in loads:
        load.start()
    wr_ref, we_ref = wide_ref.at[0:K], wide_ref.at[K : K + 16]
    me, my_slice, my_u = me_ref[0], slice_ref[0], u_ref[0]
    for near, ref in ((0, own_ref), (1, other_ref)):
        for kz in range(4):
            shard = me ^ (2 * kz + near)
            h_s[pl.ds(pl.multiple_of(shard * AT, AT), AT), :] = ref[kz, 0:AT, :]
            meta_s[shard] = ref[kz, AT:PIECE, :].astype(F32)
    gid_rows = []
    for j in range(4):
        both = meta_s[2 * j, :, 0:128] + meta_s[2 * j + 1, :, 0:128]
        posp_s[:, 128 * j : 128 * (j + 1)] = both.astype(BF)
        gid_rows.append(both[15:16, :])
    gid_row = jnp.concatenate(gid_rows, axis=1)
    gid_col = jnp.transpose(jnp.broadcast_to(gid_row, (8, ATOMS)))[:, 0:1]

    step = 16.0 / K
    inv_width = K / 24.0
    sub_e = lax.broadcasted_iota(jnp.int32, (BLK, ES), 0).astype(F32).astype(BF)
    sub_t = lax.broadcasted_iota(jnp.int32, (BLK, TPB), 0).astype(F32).astype(BF)
    lane_a = lax.broadcasted_iota(jnp.int32, (ES, ATOMS), 1).astype(F32)
    lane_e = lax.broadcasted_iota(jnp.int32, (1, ES), 1).astype(F32)
    lane_t = lax.broadcasted_iota(jnp.int32, (1, TPB), 1).astype(F32)
    centers = lax.broadcasted_iota(jnp.int32, (1, K), 1).astype(F32) * step
    one, zero = jnp.ones((), BF), jnp.zeros((), BF)

    def onehot(cond):
        return jnp.where(cond, 1.0, 0.0).astype(BF)

    def hit(places, row):
        wide = jnp.broadcast_to(row.astype(BF), places.shape)
        return jnp.where(places == wide, one, zero)

    def geometry(s):
        meta = meta_s[s]
        src = 2.0 * meta[0:1, 0:ES] + meta[0:1, ES : 2 * ES]
        dst = 2.0 * meta[1:2, 0:ES] + meta[1:2, ES : 2 * ES]
        ec = meta[15:16, 128:256]
        live = jnp.where(lane_e < jnp.concatenate([ec, ec], axis=1), 1.0, 0.0)
        lanes = slice(s * ES, (s + 1) * ES)
        for base, row in ((0, src), (ATOMS, dst)):
            for j in range(4):
                oht_s[base + BLK * j : base + BLK * (j + 1), lanes] = hit(sub_e, row - float(BLK * j))
        posp = posp_s[...]
        ps = nn(posp, oht_s[0:ATOMS, lanes])
        pd = nn(posp, oht_s[ATOMS : 2 * ATOMS, lanes])
        ps = (ps[6:9] + ps[9:12]) + ps[12:15]
        pd = (pd[6:9] + pd[9:12]) + pd[12:15]
        vec = pd - ps
        sq = vec * vec
        dist = jnp.sqrt(sq[0:1] + sq[1:2] + sq[2:3] + 0.25)
        inv = 1.0 / dist
        geo_s[s] = jnp.concatenate([src, dst, live, dist, vec * inv, inv], axis=0)

    def gather(s):
        cols = jnp.transpose(geo_s[s])
        ohs = onehot(lane_a == cols[:, 0:1])
        ohd = onehot(lane_a == cols[:, 1:2])
        ohd_s[s] = ohd
        t = (cols[:, 3:4] - centers) * inv_width
        basis = jnp.exp(-(t * t)) * cols[:, 2:3]
        bt_s[:, s * ES : (s + 1) * ES] = jnp.transpose(basis).astype(BF)
        q = nn(ohs, ab_s[0:ATOMS, :]) + nn(ohd, ab_s[ATOMS : 2 * ATOMS, :])
        return s, cols, q, nn(basis.astype(BF), wr_ref[...])

    def message(s, cols, q, radial):
        a = 1.0 + jnp.tanh(q)
        sil = q * a
        msg = (sil * radial).astype(BF)
        msg_s[s] = msg
        f_s[s] = (radial * (a + sil * (2.0 - a))).astype(BF)
        sg_s[s] = sil.astype(BF)
        m2 = nn(msg, wt_ref[...]).astype(BF)
        m2_s[s] = m2
        meta = meta_s[s]
        unit = geo_s[s][4:7]
        tc = 8.0 * meta[15:16, 256:384] + meta[15:16, 384:512]
        mixes = []
        for i in range(2):
            rows = slice(BLK * i, BLK * (i + 1))
            limit = jnp.concatenate([tc] * 4, axis=1) - float(TPB * i)
            tin = meta[2 + i : 3 + i, :]
            tout = jnp.where(lane_t < limit, meta[4 + i : 5 + i, :], -1.0)
            count = nt(hit(sub_t, tout), hit(sub_t, tin)) * cols[rows, 2:3]
            n_s[2 * s + i] = count
            gram = (
                cols[rows, 4:5] * unit[0:1, rows]
                + cols[rows, 5:6] * unit[1:2, rows]
                + cols[rows, 6:7] * unit[2:3, rows]
            )
            mix = count * gram
            tt_s[2 * s + i] = jnp.transpose(mix).astype(BF)
            mixes.append(mix.astype(BF))
        return s, msg, m2, mixes

    def update(s, msg, m2, mixes):
        for i in range(2):
            rows = slice(BLK * i, BLK * (i + 1))
            upd = msg[rows].astype(F32) + nn(mixes[i], m2[rows])
            upd_s[s * ES + BLK * i : s * ES + BLK * (i + 1), :] = upd.astype(BF)

    def staged(count, *stages):
        waiting = [None] * len(stages)
        for turn in range(count + len(stages) - 1):
            for k in reversed(range(len(stages))):
                if k == 0:
                    given = (turn,) if turn < count else None
                else:
                    given = waiting[k - 1]
                waiting[k] = None if given is None else stages[k](*given)

    for s in range(NG):
        geometry(s)
    h = h_s[...]
    loads[0].wait()
    ab_s[0:ATOMS, :] = (0.5 * nn(h, ws_ref[...])).astype(BF)
    loads[1].wait()
    ab_s[ATOMS : 2 * ATOMS, :] = (0.5 * nn(h, wd_ref[...])).astype(BF)
    for load in loads[2:]:
        load.wait()
    staged(NG, gather, message, update)

    we = we_ref[...].astype(F32)[0:1]
    ecot = (meta_s[0, 6:7, 128:144] + meta_s[0, 7:8, 128:144]) + meta_s[0, 8:9, 128:144]
    energies, slopes = [], []

    def collect(b):
        agg = nn(oht_s[ATOMS + 512 * b : ATOMS + 512 * (b + 1), :], upd_s[...]).astype(BF)
        aggb_s[512 * b : 512 * (b + 1), :] = agg
        return b, nn(agg, wo_ref[...])

    def settle(b, z):
        rows = slice(512 * b, 512 * (b + 1))
        sig = 0.5 + 0.5 * jnp.tanh(0.5 * z)
        out = z * sig
        x = h_s[rows, :].astype(F32) + out
        atom_energy = jnp.sum(x * we, axis=1, keepdims=True)
        places = lax.broadcasted_iota(jnp.int32, (512, 16), 1).astype(F32)
        member = jnp.where(places == gid_col[rows], 1.0, 0.0)
        energies.append(jnp.sum(member * atom_energy, axis=0, keepdims=True))
        cot = jnp.sum(member * ecot, axis=1, keepdims=True)
        cot_s[rows, :] = jnp.broadcast_to(cot, (512, 128))
        slopes.append(jnp.sum(x * cot, axis=0, keepdims=True))
        dz = (cot * we * (sig + out * (1.0 - sig))).astype(BF)
        dzb_s[rows, :] = dz
        ac_s[rows, :] = nt(dz, wo_ref[...]).astype(BF)
        return (b,)

    staged(1, collect, settle)
    energy_ref[...] = sum(energies[1:], energies[0])
    ge_s[...] = sum(slopes[1:], slopes[0])

    def fetch(s):
        return s, nn(ohd_s[s], ac_s[...])

    def mixed(s, ug):
        geo = geo_s[s]
        cols = jnp.transpose(geo)
        ugb = ug.astype(BF)
        m2 = m2_s[s]
        halves, grams = [], []
        for i in range(2):
            rows = slice(BLK * i, BLK * (i + 1))
            halves.append(nn(tt_s[2 * s + i], ugb[rows]).astype(BF))
            grams.append(n_s[2 * s + i] * nt(ugb[rows], m2[rows]))
        dm2 = jnp.concatenate(halves, axis=0)
        dm2_s[s * ES : (s + 1) * ES, :] = dm2
        return s, geo, cols, ug, dm2, grams

    def spread(s, geo, cols, ug, dm2, grams):
        edges = slice(s * ES, (s + 1) * ES)
        dmsg = ug + nn(dm2, wtt_s[...])
        dpre_s[edges, :] = (dmsg * f_s[s].astype(F32)).astype(BF)
        drad = (dmsg * sg_s[s].astype(F32)).astype(BF)
        drad_s[edges, :] = drad
        return s, geo, cols, drad, grams

    def turn_back(s, geo, cols, drad, grams):
        edges = slice(s * ES, (s + 1) * ES)
        turns = []
        for i in range(2):
            rows = slice(BLK * i, BLK * (i + 1))
            both = grams[i] + jnp.transpose(grams[i])
            turns.append(
                jnp.concatenate(
                    [jnp.sum(both * cols[rows, a : a + 1], axis=0, keepdims=True) for a in (4, 5, 6)], axis=0
                )
            )
        t = (cols[:, 3:4] - centers) * inv_width
        slope = nt(drad, wr_ref[...]) * (jnp.exp(-(t * t)) * (t * (-2.0 * inv_width)))
        ddist = jnp.sum(jnp.transpose(slope), axis=0, keepdims=True) * geo[2:3]
        unit = geo[4:7]
        du = jnp.concatenate(turns, axis=1)
        along = du * unit
        along = along[0:1] + along[1:2] + along[2:3]
        dv = geo[7:8] * (du - unit * along) + unit * ddist
        top = dv.astype(BF).astype(F32)
        dv_s[:, edges] = jnp.concatenate([top, dv - top, jnp.zeros((10, ES), F32)], axis=0).astype(BF)

    wtt_s[...] = jnp.transpose(wt_ref[...])
    staged(NG, fetch, mixed, spread, turn_back)

    own = pl.multiple_of(me * AT, AT)
    ohs_own = oht_s[pl.ds(own, AT), :]
    ohd_own = oht_s[pl.ds(ATOMS + own, AT), :]
    group = lax.div(my_slice, 4)
    block = pl.ds(pl.multiple_of(lax.rem(my_slice, 4) * 128, 128), 128)
    side = pl.ds(pl.multiple_of(group * ATOMS, ATOMS), ATOMS)
    rows_t = tn(h_s[:, block], oht_s[side, :]).astype(BF)
    sums = nn(jnp.concatenate([rows_t, ohs_own, ohd_own], axis=0), dpre_s[...])
    a_s[...] = 0.5 * sums[0:BLK]
    own_s_ref[...] = (0.5 * sums[BLK : 2 * BLK]).astype(BF)
    cot_ref[...] = cot_s[pl.ds(own, AT), :]
    pos = nt(dv_s[...], ohd_own - ohs_own)
    pos = pos[0:3] + pos[3:6]
    for i in range(3):
        pos_out_ref[i] = pos[i : i + 1]

    @pl.when(group == 0)
    def _():
        for_trip = [msg_s[s, :, block] for s in range(NG)]
        b_s[...] = tn(jnp.concatenate(for_trip, axis=0), dm2_s[...])

    @pl.when(group == 1)
    def _():
        b_s[...] = tn(aggb_s[:, block], dzb_s[...])

    r_s[...] = nn(bt_s[pl.ds(pl.multiple_of(my_slice * 16, 16), 16), :], drad_s[...])
    ge = ge_s[:, block]
    for u in range(4):
        for v in range(4):
            cols = slice(128 * v, 128 * v + 128)
            chunk = jnp.concatenate(
                [
                    a_s[32 * u : 32 * u + 32, cols],
                    b_s[32 * u : 32 * u + 32, cols],
                    r_s[4 * u : 4 * u + 4, cols],
                    ge,
                    jnp.zeros((CH - 69, 128), F32),
                ],
                axis=0,
            )
            pay_ref[lax.rem(u - my_u + 4, 4), v] = chunk.astype(BF)


def batch(me, part, u, own, other, ws, wd, wide, wt, wo):
    vm = pl.BlockSpec(memory_space=pltpu.VMEM)
    sm = pl.BlockSpec(memory_space=pltpu.SMEM)
    far = pl.BlockSpec(memory_space=pltpu.HBM)
    V = pltpu.VMEM
    return pl.pallas_call(
        main_kernel,
        out_shape=(
            jax.ShapeDtypeStruct((1, 16), F32),
            jax.ShapeDtypeStruct((3, 1, AT), F32),
            jax.ShapeDtypeStruct((2 * AT, D), BF),
            jax.ShapeDtypeStruct((AT, 128), F32),
            jax.ShapeDtypeStruct((4, 4, CH, 128), BF),
        ),
        in_specs=[sm] * 3 + [vm] * 2 + [far] * 2 + [vm] + [far] * 2,
        out_specs=(vm,) * 5,
        scratch_shapes=[
            V((ATOMS, D), BF),
            V((NG, 16, D), F32),
            V((2 * ATOMS, D), BF),
            V((16, ATOMS), BF),
            V((2 * ATOMS, EDGES), BF),
            V((NG, ES, ATOMS), BF),
            V((NG, 8, ES), F32),
            V((NG, ES, D), BF),
            V((NG, ES, D), BF),
            V((NG, ES, D), BF),
            V((NG, ES, D), BF),
            V((2 * NG, BLK, BLK), F32),
            V((2 * NG, BLK, BLK), BF),
            V((EDGES, D), BF),
            V((ATOMS, D), BF),
            V((ATOMS, D), BF),
            V((ATOMS, D), BF),
            V((ATOMS, 128), F32),
            V((1, D), F32),
            V((K, EDGES), BF),
            V((EDGES, D), BF),
            V((EDGES, D), BF),
            V((EDGES, D), BF),
            V((16, EDGES), BF),
            V((BLK, D), F32),
            V((BLK, D), F32),
            V((16, D), F32),
            V((D, D), BF),
            V((D, D), BF),
            V((D, D), BF),
            V((D, D), BF),
            pltpu.SemaphoreType.DMA((4,)),
            V((D, D), BF),
        ],
        compiler_params=pltpu.CompilerParams(vmem_limit_bytes=53760 * 1024),
        name="batch",
    )(me, part, u, own, other, ws, wd, wide, wt, wo)


def node_kernel(sums_ref, cot_ref, ws_ref, wd_ref, wide_ref, out_ref):
    out_ref[...] = (
        cot_ref[:, 0:1] * wide_ref[K : K + 16, :].astype(F32)[0:1]
        + nt(sums_ref[0:AT, :], ws_ref[...])
        + nt(sums_ref[AT : 2 * AT, :], wd_ref[...])
    )


def node(sums, cot, ws, wd, we):
    vm = pl.BlockSpec(memory_space=pltpu.VMEM)
    return pl.pallas_call(
        node_kernel,
        out_shape=jax.ShapeDtypeStruct((AT, D), F32),
        in_specs=[vm] * 5,
        out_specs=vm,
        compiler_params=pltpu.CompilerParams(vmem_limit_bytes=24 * 1024 * 1024),
        name="node",
    )(sums, cot, ws, wd, we)


def place_kernel(c, x_ref, y_ref, slice_ref, ref, *rest):
    gs_ref, gd_ref, gr_ref, gt_ref, go_ref, ge_ref, first, second, low, radial, energy, sems = rest[-12:]
    x, y, mine = x_ref[0], y_ref[0], slice_ref[0]
    pc = (mine & 1) ^ c
    my_u = jnp.where(pc == 0, x, y)

    for kz in range(4):

        def body(ku, carry, kz=kz):
            u = lax.rem(my_u - ku + 4, 4)
            rows = pl.ds(pl.multiple_of(u * 32, 32), 32)
            for v in range(4):
                cols = slice(128 * v, 128 * (v + 1))
                tile = ref[16 * ku + 4 * kz + v].astype(F32)
                first[kz, rows, cols] = tile[0:32]
                second[kz, rows, cols] = tile[32:64]
                low[4 * kz + u, :, cols] = tile[64:72]
            return carry

        lax.fori_loop(0, 4, body, 0, unroll=True)
        g = lax.bitwise_xor(mine, 2 * kz + c)
        block = pl.ds(pl.multiple_of((g & 3) * 128, 128), 128)

        def send(near, far, sem):
            pltpu.make_async_copy(near, far, sem).start()

        @pl.when(g < 4)
        def _():
            send(first.at[kz], gs_ref.at[block], sems.at[0, kz])
            send(second.at[kz], gt_ref.at[block], sems.at[1, kz])

        @pl.when(g >= 4)
        def _():
            send(first.at[kz], gd_ref.at[block], sems.at[0, kz])
            send(second.at[kz], go_ref.at[block], sems.at[1, kz])

        for u in range(4):
            radial[kz, 4 * u : 4 * u + 4, :] = low[4 * kz + u, 0:4, :]
        send(radial.at[kz], gr_ref.at[pl.ds(pl.multiple_of(g * 16, 16), 16)], sems.at[2, kz])

        @pl.when(g < 4)
        def _():
            energy[kz] = low[4 * kz, 4:5, 0:128]
            copy = pltpu.make_async_copy(energy.at[kz], ge_ref.at[:, block], sems.at[3, kz])
            copy.start()
            copy.wait()

    for kz in range(4):
        pltpu.make_async_copy(first.at[kz], gs_ref.at[0:128], sems.at[0, kz]).wait()
        pltpu.make_async_copy(second.at[kz], gt_ref.at[0:128], sems.at[1, kz]).wait()
        pltpu.make_async_copy(radial.at[kz], gr_ref.at[0:16], sems.at[2, kz]).wait()


def place(c, x, y, part, pieces, *before):
    vm = pl.BlockSpec(memory_space=pltpu.VMEM)
    sm = pl.BlockSpec(memory_space=pltpu.SMEM)
    far = pl.BlockSpec(memory_space=pl.ANY)
    big = jax.ShapeDtypeStruct((D, D), F32)
    return pl.pallas_call(
        functools.partial(place_kernel, c),
        out_shape=(big, big, jax.ShapeDtypeStruct((K, D), F32), big, big, jax.ShapeDtypeStruct((1, D), F32)),
        in_specs=[sm] * 3 + [vm] + [far] * len(before),
        out_specs=(far,) * 6,
        scratch_shapes=[
            pltpu.VMEM((4, 128, D), F32),
            pltpu.VMEM((4, 128, D), F32),
            pltpu.VMEM((16, 8, D), F32),
            pltpu.VMEM((4, 16, D), F32),
            pltpu.VMEM((4, 1, 128), F32),
            pltpu.SemaphoreType.DMA((4, 4)),
        ],
        input_output_aliases={4 + i: i for i in range(len(before))},
        compiler_params=pltpu.CompilerParams(vmem_limit_bytes=30 * 1024 * 1024),
        name="place",
    )(x, y, part, pieces, *before)


def moves(fn):
    pairs = []
    for zh in range(2):
        for x in range(4):
            for y in range(4):
                for zl in range(4):
                    for c in range(2):
                        u, v = (x, y) if c == 0 else (y, x)
                        zh2, u2, v2, zl2, c2 = fn(zh, u, v, zl, c)
                        x2, y2 = (u2, v2) if c == 0 else (v2, u2)
                        here = (zh * 16 + x * 4 + y) * 8 + zl * 2 + c
                        there = (zh2 * 16 + x2 * 4 + y2) * 8 + zl2 * 2 + c2
                        pairs.append((here, there))
    return pairs


def shift(value, zh=0, u=0, v=0, zl=0, c=0):
    def fn(zh_, u_, v_, zl_, c_):
        return zh_ ^ zh, (u_ + u) % 4, (v_ + v) % 4, zl_ ^ zl, c_ ^ c

    return lax.ppermute(value, AXES, moves(fn))


def join(*parts):
    return jnp.concatenate(parts, axis=0)


ORDER = (1, 3, 2)


def total(a, b, c, d):
    a, b, c, d = (part.astype(F32) for part in (a, b, c, d))
    return ((a + b) + (c + d)).astype(BF)


def per_device(
    node_feats,
    positions,
    edge_src,
    edge_dst,
    edge_count,
    trip_in,
    trip_out,
    trip_count,
    graph_ids,
    w_src,
    w_dst,
    w_radial,
    w_trip,
    w_out,
    w_energy,
    energy_cot,
):
    dp, graph = lax.axis_index("dp"), lax.axis_index("graph")
    zh, x, y = lax.shift_right_logical(dp, 4), lax.shift_right_logical(dp, 2) & 3, dp & 3
    core = graph & 1
    u = jnp.where(core == 0, x, y)
    part = graph ^ (6 * zh)
    me, x, y, u, part = (a.astype(jnp.int32).reshape(1) for a in (graph, x, y, u, part))
    piece = pack(
        me,
        node_feats[0],
        jnp.swapaxes(positions, 0, 1),
        edge_src,
        edge_dst,
        edge_count,
        trip_in,
        trip_out,
        trip_count,
        graph_ids,
        energy_cot,
    )[None]
    own = join(piece, *[shift(piece, zl=k) for k in (1, 2, 3)])
    other = shift(own, c=1)
    wide = jnp.concatenate([w_radial, w_energy.reshape(1, D), jnp.zeros((15, D), BF)], axis=0)
    energy, pos_grad, sums, cot, payload = batch(
        me, part, u, own, other, w_src, w_dst, wide, w_trip, w_out
    )
    node_grad = node(sums, cot, w_src, w_dst, wide)
    one, three, two = [shift(payload[k], u=k) for k in ORDER]
    held = total(payload[0], two, one, three)
    one, three, two = [shift(held, v=k) for k in ORDER]
    held = total(held, two, one, three)
    held = (held.astype(F32) + shift(held, zh=1, zl=3).astype(F32)).astype(BF)
    held = join(held, *[shift(held, zl=k) for k in (1, 2, 3)])
    one, three, two = [shift(held, u=k) for k in ORDER]
    one, three, two, node_grad = lax.optimization_barrier((one, three, two, node_grad))
    held = join(held, one, two, three)
    other = shift(held, c=1)
    gs, gd, gr, gt, go, ge = place(1, x, y, part, other, *place(0, x, y, part, held))
    return (energy, jnp.swapaxes(pos_grad, 0, 1), node_grad[None], gs, gd, gr, gt, go, ge.reshape(D))


def solution(mesh):
    placed = (
        P("dp", "graph", None),
        P("dp", None, "graph"),
        P("dp", "graph"),
        P("dp", "graph"),
        P("dp", "graph"),
        P("dp", "graph"),
        P("dp", "graph"),
        P("dp", "graph"),
        P("dp", "graph"),
        P(),
        P(),
        P(),
        P(),
        P(),
        P(),
        P("dp", None),
    )
    return jax.shard_map(
        per_device,
        mesh=mesh,
        in_specs=placed,
        out_specs=(
            P("dp", None),
            P("dp", None, "graph"),
            P("dp", "graph", None),
            P(),
            P(),
            P(),
            P(),
            P(),
            P(),
        ),
        check_vma=False,
    )
```

```python
import functools

import jax
import jax.numpy as jnp
from jax import lax
from jax.experimental import pallas as pl
from jax.experimental.pallas import tpu as pltpu
from jax.sharding import PartitionSpec as P

BF = jnp.bfloat16
F32 = jnp.float32
NG = 8
AT = 64
ATOMS = 512
ES = 256
EDGES = 2048
D = 512
K = 128
BLK = 128
TPB = 512
PIECE = 80
CH = 72
AXES = ("dp", "graph")
HI = lax.Precision.HIGHEST


def nn(a, b):
    return lax.dot_general(a, b, (((1,), (0,)), ((), ())), preferred_element_type=F32)


def nt(a, b):
    return lax.dot_general(a, b, (((1,), (1,)), ((), ())), preferred_element_type=F32)


def tn(a, b):
    return lax.dot_general(a, b, (((0,), (0,)), ((), ())), preferred_element_type=F32)


def pack_kernel(me_ref, h_ref, pos_ref, src_ref, dst_ref, ec_ref, tin_ref, tout_ref, tc_ref, gid_ref, ecot_ref, out_ref, meta):
    odd = lax.rem(me_ref[0], 2)
    out_ref[0:AT, :] = h_ref[...]

    def place(row):
        full = jnp.concatenate([row, jnp.zeros_like(row)], axis=1)
        return jnp.where(odd == 1, pltpu.roll(full, AT, 1), full)

    for r, ref in ((0, src_ref), (1, dst_ref)):
        v = ref[...]
        half = lax.shift_right_logical(v, 1)
        meta[r : r + 1, 0:ES] = half.astype(F32)
        meta[r : r + 1, ES : 2 * ES] = (v - 2 * half).astype(F32)
    for r, ref in ((2, tin_ref), (4, tout_ref)):
        v = ref[...].astype(F32)
        meta[r : r + 1, :] = v[:, 0:TPB]
        meta[r + 1 : r + 2, :] = v[:, TPB : 2 * TPB]
    p = jnp.concatenate([pos_ref[i] for i in range(3)], axis=0)
    p1 = p.astype(BF).astype(F32)
    p2 = (p - p1).astype(BF).astype(F32)
    p3 = (p - p1) - p2
    meta[6:16, :] = jnp.zeros((10, D), F32)
    meta[6:9, 0:128] = place(p1)
    meta[9:12, 0:128] = place(p2)
    meta[12:15, 0:128] = place(p3)
    e = jnp.concatenate([ecot_ref[...], jnp.zeros((1, 112), F32)], axis=1)
    e1 = e.astype(BF).astype(F32)
    e2 = (e - e1).astype(BF).astype(F32)
    meta[6:7, 128:256] = e1
    meta[7:8, 128:256] = e2
    meta[8:9, 128:256] = (e - e1) - e2
    meta[15:16, 0:128] = place(gid_ref[...].astype(F32))
    tc = tc_ref[0, 0]
    tc_half = lax.shift_right_logical(tc, 3)
    meta[15:16, 128:256] = jnp.full((1, 128), ec_ref[0, 0].astype(F32))
    meta[15:16, 256:384] = jnp.full((1, 128), tc_half.astype(F32))
    meta[15:16, 384:512] = jnp.full((1, 128), (tc - 8 * tc_half).astype(F32))
    out_ref[AT:PIECE, :] = meta[...].astype(BF)


def pack(me, h, pos, src, dst, ec, tin, tout, tc, gid, ecot):
    vm = pl.BlockSpec(memory_space=pltpu.VMEM)
    sm = pl.BlockSpec(memory_space=pltpu.SMEM)
    return pl.pallas_call(
        pack_kernel,
        out_shape=jax.ShapeDtypeStruct((PIECE, D), BF),
        in_specs=[sm, vm, vm, vm, vm, sm, vm, vm, sm, vm, vm],
        out_specs=vm,
        scratch_shapes=[pltpu.VMEM((16, D), F32)],
        name="pack",
    )(me, h, pos, src, dst, ec, tin, tout, tc, gid, ecot)


def main_kernel(
    me_ref,
    slice_ref,
    u_ref,
    own_ref,
    other_ref,
    ws_hbm,
    wd_hbm,
    wide_ref,
    wt_hbm,
    wo_hbm,
    energy_ref,
    pos_out_ref,
    own_s_ref,
    cot_ref,
    pay_ref,
    h_s,
    meta_s,
    ab_s,
    posp_s,
    oht_s,
    ohd_s,
    geo_s,
    msg_s,
    f_s,
    sg_s,
    m2_s,
    n_s,
    tt_s,
    upd_s,
    aggb_s,
    dzb_s,
    ac_s,
    cot_s,
    ge_s,
    bt_s,
    dm2_s,
    dpre_s,
    drad_s,
    dv_s,
    a_s,
    b_s,
    r_s,
    ws_ref,
    wd_ref,
    wt_ref,
    wo_ref,
    sems,
    wtt_s,
):
    loads = [
        pltpu.make_async_copy(far, near, sems.at[i])
        for i, (far, near) in enumerate(
            ((ws_hbm, ws_ref), (wd_hbm, wd_ref), (wt_hbm, wt_ref), (wo_hbm, wo_ref))
        )
    ]
    for load in loads:
        load.start()
    wr_ref, we_ref = wide_ref.at[0:K], wide_ref.at[K : K + 16]
    me, my_slice, my_u = me_ref[0], slice_ref[0], u_ref[0]
    for near, ref in ((0, own_ref), (1, other_ref)):
        for kz in range(4):
            shard = me ^ (2 * kz + near)
            h_s[pl.ds(pl.multiple_of(shard * AT, AT), AT), :] = ref[kz, 0:AT, :]
            meta_s[shard] = ref[kz, AT:PIECE, :].astype(F32)
    gid_rows = []
    for j in range(4):
        both = meta_s[2 * j, :, 0:128] + meta_s[2 * j + 1, :, 0:128]
        posp_s[:, 128 * j : 128 * (j + 1)] = both.astype(BF)
        gid_rows.append(both[15:16, :])
    gid_row = jnp.concatenate(gid_rows, axis=1)
    gid_col = jnp.transpose(jnp.broadcast_to(gid_row, (8, ATOMS)))[:, 0:1]

    step = 16.0 / K
    inv_width = K / 24.0
    sub_e = lax.broadcasted_iota(jnp.int32, (BLK, ES), 0).astype(F32).astype(BF)
    sub_t = lax.broadcasted_iota(jnp.int32, (BLK, TPB), 0).astype(F32).astype(BF)
    lane_a = lax.broadcasted_iota(jnp.int32, (ES, ATOMS), 1).astype(F32)
    lane_e = lax.broadcasted_iota(jnp.int32, (1, ES), 1).astype(F32)
    lane_t = lax.broadcasted_iota(jnp.int32, (1, TPB), 1).astype(F32)
    centers = lax.broadcasted_iota(jnp.int32, (1, K), 1).astype(F32) * step
    one, zero = jnp.ones((), BF), jnp.zeros((), BF)

    def onehot(cond):
        return jnp.where(cond, 1.0, 0.0).astype(BF)

    def hit(places, row):
        wide = jnp.broadcast_to(row.astype(BF), places.shape)
        return jnp.where(places == wide, one, zero)

    def geometry(s):
        meta = meta_s[s]
        src = 2.0 * meta[0:1, 0:ES] + meta[0:1, ES : 2 * ES]
        dst = 2.0 * meta[1:2, 0:ES] + meta[1:2, ES : 2 * ES]
        ec = meta[15:16, 128:256]
        live = jnp.where(lane_e < jnp.concatenate([ec, ec], axis=1), 1.0, 0.0)
        lanes = slice(s * ES, (s + 1) * ES)
        for base, row in ((0, src), (ATOMS, dst)):
            for j in range(4):
                oht_s[base + BLK * j : base + BLK * (j + 1), lanes] = hit(sub_e, row - float(BLK * j))
        posp = posp_s[...]
        ps = nn(posp, oht_s[0:ATOMS, lanes])
        pd = nn(posp, oht_s[ATOMS : 2 * ATOMS, lanes])
        ps = (ps[6:9] + ps[9:12]) + ps[12:15]
        pd = (pd[6:9] + pd[9:12]) + pd[12:15]
        vec = pd - ps
        sq = vec * vec
        dist = jnp.sqrt(sq[0:1] + sq[1:2] + sq[2:3] + 0.25)
        inv = 1.0 / dist
        geo_s[s] = jnp.concatenate([src, dst, live, dist, vec * inv, inv], axis=0)

    def gather(s):
        cols = jnp.transpose(geo_s[s])
        ohs = onehot(lane_a == cols[:, 0:1])
        ohd = onehot(lane_a == cols[:, 1:2])
        ohd_s[s] = ohd
        t = (cols[:, 3:4] - centers) * inv_width
        basis = jnp.exp(-(t * t)) * cols[:, 2:3]
        bt_s[:, s * ES : (s + 1) * ES] = jnp.transpose(basis).astype(BF)
        q = nn(ohs, ab_s[0:ATOMS, :]) + nn(ohd, ab_s[ATOMS : 2 * ATOMS, :])
        return s, cols, q, nn(basis.astype(BF), wr_ref[...])

    def message(s, cols, q, radial):
        a = 1.0 + jnp.tanh(q)
        sil = q * a
        msg = (sil * radial).astype(BF)
        msg_s[s] = msg
        f_s[s] = (radial * (a + sil * (2.0 - a))).astype(BF)
        sg_s[s] = sil.astype(BF)
        m2 = nn(msg, wt_ref[...]).astype(BF)
        m2_s[s] = m2
        meta = meta_s[s]
        unit = geo_s[s][4:7]
        tc = 8.0 * meta[15:16, 256:384] + meta[15:16, 384:512]
        mixes = []
        for i in range(2):
            rows = slice(BLK * i, BLK * (i + 1))
            limit = jnp.concatenate([tc] * 4, axis=1) - float(TPB * i)
            tin = meta[2 + i : 3 + i, :]
            tout = jnp.where(lane_t < limit, meta[4 + i : 5 + i, :], -1.0)
            count = nt(hit(sub_t, tout), hit(sub_t, tin)) * cols[rows, 2:3]
            n_s[2 * s + i] = count
            gram = (
                cols[rows, 4:5] * unit[0:1, rows]
                + cols[rows, 5:6] * unit[1:2, rows]
                + cols[rows, 6:7] * unit[2:3, rows]
            )
            mix = count * gram
            tt_s[2 * s + i] = jnp.transpose(mix).astype(BF)
            mixes.append(mix.astype(BF))
        return s, msg, m2, mixes

    def update(s, msg, m2, mixes):
        for i in range(2):
            rows = slice(BLK * i, BLK * (i + 1))
            upd = msg[rows].astype(F32) + nn(mixes[i], m2[rows])
            upd_s[s * ES + BLK * i : s * ES + BLK * (i + 1), :] = upd.astype(BF)

    def staged(count, *stages):
        waiting = [None] * len(stages)
        for turn in range(count + len(stages) - 1):
            for k in reversed(range(len(stages))):
                if k == 0:
                    given = (turn,) if turn < count else None
                else:
                    given = waiting[k - 1]
                waiting[k] = None if given is None else stages[k](*given)

    for s in range(NG):
        geometry(s)
    h = h_s[...]
    loads[0].wait()
    ab_s[0:ATOMS, :] = (0.5 * nn(h, ws_ref[...])).astype(BF)
    loads[1].wait()
    ab_s[ATOMS : 2 * ATOMS, :] = (0.5 * nn(h, wd_ref[...])).astype(BF)
    for load in loads[2:]:
        load.wait()
    staged(NG, gather, message, update)

    we = we_ref[...].astype(F32)[0:1]
    ecot = (meta_s[0, 6:7, 128:144] + meta_s[0, 7:8, 128:144]) + meta_s[0, 8:9, 128:144]
    energies, slopes = [], []

    def collect(b):
        agg = nn(oht_s[ATOMS + 512 * b : ATOMS + 512 * (b + 1), :], upd_s[...]).astype(BF)
        aggb_s[512 * b : 512 * (b + 1), :] = agg
        return b, nn(agg, wo_ref[...])

    def settle(b, z):
        rows = slice(512 * b, 512 * (b + 1))
        sig = 0.5 + 0.5 * jnp.tanh(0.5 * z)
        out = z * sig
        x = h_s[rows, :].astype(F32) + out
        atom_energy = jnp.sum(x * we, axis=1, keepdims=True)
        places = lax.broadcasted_iota(jnp.int32, (512, 16), 1).astype(F32)
        member = jnp.where(places == gid_col[rows], 1.0, 0.0)
        energies.append(jnp.sum(member * atom_energy, axis=0, keepdims=True))
        cot = jnp.sum(member * ecot, axis=1, keepdims=True)
        cot_s[rows, :] = jnp.broadcast_to(cot, (512, 128))
        slopes.append(jnp.sum(x * cot, axis=0, keepdims=True))
        dz = (cot * we * (sig + out * (1.0 - sig))).astype(BF)
        dzb_s[rows, :] = dz
        ac_s[rows, :] = nt(dz, wo_ref[...]).astype(BF)
        return (b,)

    staged(1, collect, settle)
    energy_ref[...] = sum(energies[1:], energies[0])
    ge_s[...] = sum(slopes[1:], slopes[0])

    def fetch(s):
        return s, nn(ohd_s[s], ac_s[...])

    def mixed(s, ug):
        geo = geo_s[s]
        cols = jnp.transpose(geo)
        ugb = ug.astype(BF)
        m2 = m2_s[s]
        halves, grams = [], []
        for i in range(2):
            rows = slice(BLK * i, BLK * (i + 1))
            halves.append(nn(tt_s[2 * s + i], ugb[rows]).astype(BF))
            grams.append(n_s[2 * s + i] * nt(ugb[rows], m2[rows]))
        dm2 = jnp.concatenate(halves, axis=0)
        dm2_s[s * ES : (s + 1) * ES, :] = dm2
        return s, geo, cols, ug, dm2, grams

    def spread(s, geo, cols, ug, dm2, grams):
        edges = slice(s * ES, (s + 1) * ES)
        dmsg = ug + nn(dm2, wtt_s[...])
        dpre_s[edges, :] = (dmsg * f_s[s].astype(F32)).astype(BF)
        drad = (dmsg * sg_s[s].astype(F32)).astype(BF)
        drad_s[edges, :] = drad
        return s, geo, cols, drad, grams

    def turn_back(s, geo, cols, drad, grams):
        edges = slice(s * ES, (s + 1) * ES)
        turns = []
        for i in range(2):
            rows = slice(BLK * i, BLK * (i + 1))
            both = grams[i] + jnp.transpose(grams[i])
            turns.append(
                jnp.concatenate(
                    [jnp.sum(both * cols[rows, a : a + 1], axis=0, keepdims=True) for a in (4, 5, 6)], axis=0
                )
            )
        t = (cols[:, 3:4] - centers) * inv_width
        slope = nt(drad, wr_ref[...]) * (jnp.exp(-(t * t)) * (t * (-2.0 * inv_width)))
        ddist = jnp.sum(jnp.transpose(slope), axis=0, keepdims=True) * geo[2:3]
        unit = geo[4:7]
        du = jnp.concatenate(turns, axis=1)
        along = du * unit
        along = along[0:1] + along[1:2] + along[2:3]
        dv = geo[7:8] * (du - unit * along) + unit * ddist
        top = dv.astype(BF).astype(F32)
        dv_s[:, edges] = jnp.concatenate([top, dv - top, jnp.zeros((10, ES), F32)], axis=0).astype(BF)

    wtt_s[...] = jnp.transpose(wt_ref[...])
    staged(NG, fetch, mixed, spread, turn_back)

    own = pl.multiple_of(me * AT, AT)
    ohs_own = oht_s[pl.ds(own, AT), :]
    ohd_own = oht_s[pl.ds(ATOMS + own, AT), :]
    group = lax.div(my_slice, 4)
    block = pl.ds(pl.multiple_of(lax.rem(my_slice, 4) * 128, 128), 128)
    side = pl.ds(pl.multiple_of(group * ATOMS, ATOMS), ATOMS)
    rows_t = tn(h_s[:, block], oht_s[side, :]).astype(BF)
    sums = nn(jnp.concatenate([rows_t, ohs_own, ohd_own], axis=0), dpre_s[...])
    a_s[...] = 0.5 * sums[0:BLK]
    own_s_ref[...] = (0.5 * sums[BLK : 2 * BLK]).astype(BF)
    cot_ref[...] = cot_s[pl.ds(own, AT), :]
    pos = nt(dv_s[...], ohd_own - ohs_own)
    pos = pos[0:3] + pos[3:6]
    for i in range(3):
        pos_out_ref[i] = pos[i : i + 1]

    @pl.when(group == 0)
    def _():
        for_trip = [msg_s[s, :, block] for s in range(NG)]
        b_s[...] = tn(jnp.concatenate(for_trip, axis=0), dm2_s[...])

    @pl.when(group == 1)
    def _():
        b_s[...] = tn(aggb_s[:, block], dzb_s[...])

    r_s[...] = nn(bt_s[pl.ds(pl.multiple_of(my_slice * 16, 16), 16), :], drad_s[...])
    ge = ge_s[:, block]
    for u in range(4):
        for v in range(4):
            cols = slice(128 * v, 128 * v + 128)
            chunk = jnp.concatenate(
                [
                    a_s[32 * u : 32 * u + 32, cols],
                    b_s[32 * u : 32 * u + 32, cols],
                    r_s[4 * u : 4 * u + 4, cols],
                    ge,
                    jnp.zeros((CH - 69, 128), F32),
                ],
                axis=0,
            )
            pay_ref[lax.rem(u - my_u + 4, 4), v] = chunk.astype(BF)


def batch(me, part, u, own, other, ws, wd, wide, wt, wo):
    vm = pl.BlockSpec(memory_space=pltpu.VMEM)
    sm = pl.BlockSpec(memory_space=pltpu.SMEM)
    far = pl.BlockSpec(memory_space=pltpu.HBM)
    V = pltpu.VMEM
    return pl.pallas_call(
        main_kernel,
        out_shape=(
            jax.ShapeDtypeStruct((1, 16), F32),
            jax.ShapeDtypeStruct((3, 1, AT), F32),
            jax.ShapeDtypeStruct((2 * AT, D), BF),
            jax.ShapeDtypeStruct((AT, 128), F32),
            jax.ShapeDtypeStruct((4, 4, CH, 128), BF),
        ),
        in_specs=[sm] * 3 + [vm] * 2 + [far] * 2 + [vm] + [far] * 2,
        out_specs=(vm,) * 5,
        scratch_shapes=[
            V((ATOMS, D), BF),
            V((NG, 16, D), F32),
            V((2 * ATOMS, D), BF),
            V((16, ATOMS), BF),
            V((2 * ATOMS, EDGES), BF),
            V((NG, ES, ATOMS), BF),
            V((NG, 8, ES), F32),
            V((NG, ES, D), BF),
            V((NG, ES, D), BF),
            V((NG, ES, D), BF),
            V((NG, ES, D), BF),
            V((2 * NG, BLK, BLK), F32),
            V((2 * NG, BLK, BLK), BF),
            V((EDGES, D), BF),
            V((ATOMS, D), BF),
            V((ATOMS, D), BF),
            V((ATOMS, D), BF),
            V((ATOMS, 128), F32),
            V((1, D), F32),
            V((K, EDGES), BF),
            V((EDGES, D), BF),
            V((EDGES, D), BF),
            V((EDGES, D), BF),
            V((16, EDGES), BF),
            V((BLK, D), F32),
            V((BLK, D), F32),
            V((16, D), F32),
            V((D, D), BF),
            V((D, D), BF),
            V((D, D), BF),
            V((D, D), BF),
            pltpu.SemaphoreType.DMA((4,)),
            V((D, D), BF),
        ],
        compiler_params=pltpu.CompilerParams(vmem_limit_bytes=53760 * 1024),
        name="batch",
    )(me, part, u, own, other, ws, wd, wide, wt, wo)


def node_kernel(sums_ref, cot_ref, ws_ref, wd_ref, wide_ref, out_ref):
    out_ref[...] = (
        cot_ref[:, 0:1] * wide_ref[K : K + 16, :].astype(F32)[0:1]
        + nt(sums_ref[0:AT, :], ws_ref[...])
        + nt(sums_ref[AT : 2 * AT, :], wd_ref[...])
    )


def node(sums, cot, ws, wd, we):
    vm = pl.BlockSpec(memory_space=pltpu.VMEM)
    return pl.pallas_call(
        node_kernel,
        out_shape=jax.ShapeDtypeStruct((AT, D), F32),
        in_specs=[vm] * 5,
        out_specs=vm,
        compiler_params=pltpu.CompilerParams(vmem_limit_bytes=24 * 1024 * 1024),
        name="node",
    )(sums, cot, ws, wd, we)


def place_kernel(c, x_ref, y_ref, slice_ref, ref, *rest):
    gs_ref, gd_ref, gr_ref, gt_ref, go_ref, ge_ref, first, second, low, radial, energy, sems = rest[-12:]
    x, y, mine = x_ref[0], y_ref[0], slice_ref[0]
    pc = (mine & 1) ^ c
    my_u = jnp.where(pc == 0, x, y)

    for kz in range(4):

        def body(ku, carry, kz=kz):
            u = lax.rem(my_u - ku + 4, 4)
            rows = pl.ds(pl.multiple_of(u * 32, 32), 32)
            for v in range(4):
                cols = slice(128 * v, 128 * (v + 1))
                tile = ref[16 * ku + 4 * kz + v].astype(F32)
                first[kz, rows, cols] = tile[0:32]
                second[kz, rows, cols] = tile[32:64]
                low[4 * kz + u, :, cols] = tile[64:72]
            return carry

        lax.fori_loop(0, 4, body, 0, unroll=True)
        g = lax.bitwise_xor(mine, 2 * kz + c)
        block = pl.ds(pl.multiple_of((g & 3) * 128, 128), 128)

        def send(near, far, sem):
            pltpu.make_async_copy(near, far, sem).start()

        @pl.when(g < 4)
        def _():
            send(first.at[kz], gs_ref.at[block], sems.at[0, kz])
            send(second.at[kz], gt_ref.at[block], sems.at[1, kz])

        @pl.when(g >= 4)
        def _():
            send(first.at[kz], gd_ref.at[block], sems.at[0, kz])
            send(second.at[kz], go_ref.at[block], sems.at[1, kz])

        for u in range(4):
            radial[kz, 4 * u : 4 * u + 4, :] = low[4 * kz + u, 0:4, :]
        send(radial.at[kz], gr_ref.at[pl.ds(pl.multiple_of(g * 16, 16), 16)], sems.at[2, kz])

        @pl.when(g < 4)
        def _():
            energy[kz] = low[4 * kz, 4:5, 0:128]
            copy = pltpu.make_async_copy(energy.at[kz], ge_ref.at[:, block], sems.at[3, kz])
            copy.start()
            copy.wait()

    for kz in range(4):
        pltpu.make_async_copy(first.at[kz], gs_ref.at[0:128], sems.at[0, kz]).wait()
        pltpu.make_async_copy(second.at[kz], gt_ref.at[0:128], sems.at[1, kz]).wait()
        pltpu.make_async_copy(radial.at[kz], gr_ref.at[0:16], sems.at[2, kz]).wait()


def place(c, x, y, part, pieces, *before):
    vm = pl.BlockSpec(memory_space=pltpu.VMEM)
    sm = pl.BlockSpec(memory_space=pltpu.SMEM)
    far = pl.BlockSpec(memory_space=pl.ANY)
    big = jax.ShapeDtypeStruct((D, D), F32)
    return pl.pallas_call(
        functools.partial(place_kernel, c),
        out_shape=(big, big, jax.ShapeDtypeStruct((K, D), F32), big, big, jax.ShapeDtypeStruct((1, D), F32)),
        in_specs=[sm] * 3 + [vm] + [far] * len(before),
        out_specs=(far,) * 6,
        scratch_shapes=[
            pltpu.VMEM((4, 128, D), F32),
            pltpu.VMEM((4, 128, D), F32),
            pltpu.VMEM((16, 8, D), F32),
            pltpu.VMEM((4, 16, D), F32),
            pltpu.VMEM((4, 1, 128), F32),
            pltpu.SemaphoreType.DMA((4, 4)),
        ],
        input_output_aliases={4 + i: i for i in range(len(before))},
        compiler_params=pltpu.CompilerParams(vmem_limit_bytes=30 * 1024 * 1024),
        name="place",
    )(x, y, part, pieces, *before)


def moves(fn):
    pairs = []
    for zh in range(2):
        for x in range(4):
            for y in range(4):
                for zl in range(4):
                    for c in range(2):
                        u, v = (x, y) if c == 0 else (y, x)
                        zh2, u2, v2, zl2, c2 = fn(zh, u, v, zl, c)
                        x2, y2 = (u2, v2) if c == 0 else (v2, u2)
                        here = (zh * 16 + x * 4 + y) * 8 + zl * 2 + c
                        there = (zh2 * 16 + x2 * 4 + y2) * 8 + zl2 * 2 + c2
                        pairs.append((here, there))
    return pairs


def shift(value, zh=0, u=0, v=0, zl=0, c=0):
    def fn(zh_, u_, v_, zl_, c_):
        return zh_ ^ zh, (u_ + u) % 4, (v_ + v) % 4, zl_ ^ zl, c_ ^ c

    return lax.ppermute(value, AXES, moves(fn))


def join(*parts):
    return jnp.concatenate(parts, axis=0)


ORDER = (1, 3, 2)


def total(a, b, c, d):
    a, b, c, d = (part.astype(F32) for part in (a, b, c, d))
    return ((a + b) + (c + d)).astype(BF)


def per_device(
    node_feats,
    positions,
    edge_src,
    edge_dst,
    edge_count,
    trip_in,
    trip_out,
    trip_count,
    graph_ids,
    w_src,
    w_dst,
    w_radial,
    w_trip,
    w_out,
    w_energy,
    energy_cot,
):
    dp, graph = lax.axis_index("dp"), lax.axis_index("graph")
    zh, x, y = lax.shift_right_logical(dp, 4), lax.shift_right_logical(dp, 2) & 3, dp & 3
    core = graph & 1
    u = jnp.where(core == 0, x, y)
    part = graph ^ (6 * zh)
    me, x, y, u, part = (a.astype(jnp.int32).reshape(1) for a in (graph, x, y, u, part))
    piece = pack(
        me,
        node_feats[0],
        jnp.swapaxes(positions, 0, 1),
        edge_src,
        edge_dst,
        edge_count,
        trip_in,
        trip_out,
        trip_count,
        graph_ids,
        energy_cot,
    )[None]
    wide = jnp.concatenate([w_radial, w_energy.reshape(1, D), jnp.zeros((15, D), BF)], axis=0)
    near = [shift(piece, zl=k) for k in (1, 2, 3)]
    *near, wide = lax.optimization_barrier((*near, wide))
    own = join(piece, *near)
    other = shift(own, c=1)
    energy, pos_grad, sums, cot, payload = batch(
        me, part, u, own, other, w_src, w_dst, wide, w_trip, w_out
    )
    node_grad = node(sums, cot, w_src, w_dst, wide)
    one, three, two = [shift(payload[k], u=k) for k in ORDER]
    held = total(payload[0], two, one, three)
    one, three, two = [shift(held, v=k) for k in ORDER]
    held = total(held, two, one, three)
    held = (held.astype(F32) + shift(held, zh=1, zl=3).astype(F32)).astype(BF)
    held = join(held, *[shift(held, zl=k) for k in (1, 2, 3)])
    one, three, two = [shift(held, u=k) for k in ORDER]
    one, three, two, node_grad = lax.optimization_barrier((one, three, two, node_grad))
    held = join(held, one, two, three)
    other = shift(held, c=1)
    gs, gd, gr, gt, go, ge = place(1, x, y, part, other, *place(0, x, y, part, held))
    return (energy, jnp.swapaxes(pos_grad, 0, 1), node_grad[None], gs, gd, gr, gt, go, ge.reshape(D))


def solution(mesh):
    placed = (
        P("dp", "graph", None),
        P("dp", None, "graph"),
        P("dp", "graph"),
        P("dp", "graph"),
        P("dp", "graph"),
        P("dp", "graph"),
        P("dp", "graph"),
        P("dp", "graph"),
        P("dp", "graph"),
        P(),
        P(),
        P(),
        P(),
        P(),
        P(),
        P("dp", None),
    )
    return jax.shard_map(
        per_device,
        mesh=mesh,
        in_specs=placed,
        out_specs=(
            P("dp", None),
            P("dp", None, "graph"),
            P("dp", "graph", None),
            P(),
            P(),
            P(),
            P(),
            P(),
            P(),
        ),
        check_vma=False,
    )
```

```python
import functools

import jax
import jax.numpy as jnp
from jax import lax
from jax.experimental import pallas as pl
from jax.experimental.pallas import tpu as pltpu
from jax.sharding import PartitionSpec as P

BF = jnp.bfloat16
F32 = jnp.float32
NG = 8
AT = 64
ATOMS = 512
ES = 256
EDGES = 2048
D = 512
K = 128
BLK = 128
TPB = 512
PIECE = 80
CH = 72
AXES = ("dp", "graph")
HI = lax.Precision.HIGHEST


def nn(a, b):
    return lax.dot_general(a, b, (((1,), (0,)), ((), ())), preferred_element_type=F32)


def nt(a, b):
    return lax.dot_general(a, b, (((1,), (1,)), ((), ())), preferred_element_type=F32)


def tn(a, b):
    return lax.dot_general(a, b, (((0,), (0,)), ((), ())), preferred_element_type=F32)


def pack_kernel(me_ref, h_ref, pos_ref, src_ref, dst_ref, ec_ref, tin_ref, tout_ref, tc_ref, gid_ref, ecot_ref, out_ref, meta):
    odd = lax.rem(me_ref[0], 2)
    out_ref[0:AT, :] = h_ref[...]

    def place(row):
        full = jnp.concatenate([row, jnp.zeros_like(row)], axis=1)
        return jnp.where(odd == 1, pltpu.roll(full, AT, 1), full)

    for r, ref in ((0, src_ref), (1, dst_ref)):
        v = ref[...]
        half = lax.shift_right_logical(v, 1)
        meta[r : r + 1, 0:ES] = half.astype(F32)
        meta[r : r + 1, ES : 2 * ES] = (v - 2 * half).astype(F32)
    for r, ref in ((2, tin_ref), (4, tout_ref)):
        v = ref[...].astype(F32)
        meta[r : r + 1, :] = v[:, 0:TPB]
        meta[r + 1 : r + 2, :] = v[:, TPB : 2 * TPB]
    p = jnp.concatenate([pos_ref[i] for i in range(3)], axis=0)
    p1 = p.astype(BF).astype(F32)
    p2 = (p - p1).astype(BF).astype(F32)
    p3 = (p - p1) - p2
    meta[6:16, :] = jnp.zeros((10, D), F32)
    meta[6:9, 0:128] = place(p1)
    meta[9:12, 0:128] = place(p2)
    meta[12:15, 0:128] = place(p3)
    e = jnp.concatenate([ecot_ref[...], jnp.zeros((1, 112), F32)], axis=1)
    e1 = e.astype(BF).astype(F32)
    e2 = (e - e1).astype(BF).astype(F32)
    meta[6:7, 128:256] = e1
    meta[7:8, 128:256] = e2
    meta[8:9, 128:256] = (e - e1) - e2
    meta[15:16, 0:128] = place(gid_ref[...].astype(F32))
    tc = tc_ref[0, 0]
    tc_half = lax.shift_right_logical(tc, 3)
    meta[15:16, 128:256] = jnp.full((1, 128), ec_ref[0, 0].astype(F32))
    meta[15:16, 256:384] = jnp.full((1, 128), tc_half.astype(F32))
    meta[15:16, 384:512] = jnp.full((1, 128), (tc - 8 * tc_half).astype(F32))
    out_ref[AT:PIECE, :] = meta[...].astype(BF)


def pack(me, h, pos, src, dst, ec, tin, tout, tc, gid, ecot):
    vm = pl.BlockSpec(memory_space=pltpu.VMEM)
    sm = pl.BlockSpec(memory_space=pltpu.SMEM)
    return pl.pallas_call(
        pack_kernel,
        out_shape=jax.ShapeDtypeStruct((PIECE, D), BF),
        in_specs=[sm, vm, vm, vm, vm, sm, vm, vm, sm, vm, vm],
        out_specs=vm,
        scratch_shapes=[pltpu.VMEM((16, D), F32)],
        name="pack",
    )(me, h, pos, src, dst, ec, tin, tout, tc, gid, ecot)


def main_kernel(
    me_ref,
    slice_ref,
    u_ref,
    own_0,
    own_1,
    own_2,
    own_3,
    other_0,
    other_1,
    other_2,
    other_3,
    ws_hbm,
    wd_hbm,
    wide_ref,
    wt_hbm,
    wo_hbm,
    energy_ref,
    pos_out_ref,
    own_s_ref,
    cot_ref,
    pay_ref,
    h_s,
    meta_s,
    ab_s,
    posp_s,
    oht_s,
    ohd_s,
    geo_s,
    msg_s,
    f_s,
    sg_s,
    m2_s,
    n_s,
    tt_s,
    upd_s,
    aggb_s,
    dzb_s,
    ac_s,
    cot_s,
    ge_s,
    bt_s,
    dm2_s,
    dpre_s,
    drad_s,
    dv_s,
    a_s,
    b_s,
    r_s,
    ws_ref,
    wd_ref,
    wt_ref,
    wo_ref,
    sems,
    wtt_s,
):
    loads = [
        pltpu.make_async_copy(far, near, sems.at[i])
        for i, (far, near) in enumerate(
            ((ws_hbm, ws_ref), (wd_hbm, wd_ref), (wt_hbm, wt_ref), (wo_hbm, wo_ref))
        )
    ]
    for load in loads:
        load.start()
    wr_ref, we_ref = wide_ref.at[0:K], wide_ref.at[K : K + 16]
    me, my_slice, my_u = me_ref[0], slice_ref[0], u_ref[0]
    for near, refs in ((0, (own_0, own_1, own_2, own_3)), (1, (other_0, other_1, other_2, other_3))):
        for kz, ref in enumerate(refs):
            shard = me ^ (2 * kz + near)
            h_s[pl.ds(pl.multiple_of(shard * AT, AT), AT), :] = ref[0:AT, :]
            meta_s[shard] = ref[AT:PIECE, :].astype(F32)
    gid_rows = []
    for j in range(4):
        both = meta_s[2 * j, :, 0:128] + meta_s[2 * j + 1, :, 0:128]
        posp_s[:, 128 * j : 128 * (j + 1)] = both.astype(BF)
        gid_rows.append(both[15:16, :])
    gid_row = jnp.concatenate(gid_rows, axis=1)
    gid_col = jnp.transpose(jnp.broadcast_to(gid_row, (8, ATOMS)))[:, 0:1]

    step = 16.0 / K
    inv_width = K / 24.0
    sub_e = lax.broadcasted_iota(jnp.int32, (BLK, ES), 0).astype(F32).astype(BF)
    sub_t = lax.broadcasted_iota(jnp.int32, (BLK, TPB), 0).astype(F32).astype(BF)
    lane_a = lax.broadcasted_iota(jnp.int32, (ES, ATOMS), 1).astype(F32)
    lane_e = lax.broadcasted_iota(jnp.int32, (1, ES), 1).astype(F32)
    lane_t = lax.broadcasted_iota(jnp.int32, (1, TPB), 1).astype(F32)
    centers = lax.broadcasted_iota(jnp.int32, (1, K), 1).astype(F32) * step
    one, zero = jnp.ones((), BF), jnp.zeros((), BF)

    def onehot(cond):
        return jnp.where(cond, 1.0, 0.0).astype(BF)

    def hit(places, row):
        wide = jnp.broadcast_to(row.astype(BF), places.shape)
        return jnp.where(places == wide, one, zero)

    def geometry(s):
        meta = meta_s[s]
        src = 2.0 * meta[0:1, 0:ES] + meta[0:1, ES : 2 * ES]
        dst = 2.0 * meta[1:2, 0:ES] + meta[1:2, ES : 2 * ES]
        ec = meta[15:16, 128:256]
        live = jnp.where(lane_e < jnp.concatenate([ec, ec], axis=1), 1.0, 0.0)
        lanes = slice(s * ES, (s + 1) * ES)
        for base, row in ((0, src), (ATOMS, dst)):
            for j in range(4):
                oht_s[base + BLK * j : base + BLK * (j + 1), lanes] = hit(sub_e, row - float(BLK * j))
        posp = posp_s[...]
        ps = nn(posp, oht_s[0:ATOMS, lanes])
        pd = nn(posp, oht_s[ATOMS : 2 * ATOMS, lanes])
        ps = (ps[6:9] + ps[9:12]) + ps[12:15]
        pd = (pd[6:9] + pd[9:12]) + pd[12:15]
        vec = pd - ps
        sq = vec * vec
        dist = jnp.sqrt(sq[0:1] + sq[1:2] + sq[2:3] + 0.25)
        inv = 1.0 / dist
        geo_s[s] = jnp.concatenate([src, dst, live, dist, vec * inv, inv], axis=0)

    def gather(s):
        cols = jnp.transpose(geo_s[s])
        ohs = onehot(lane_a == cols[:, 0:1])
        ohd = onehot(lane_a == cols[:, 1:2])
        ohd_s[s] = ohd
        t = (cols[:, 3:4] - centers) * inv_width
        basis = jnp.exp(-(t * t)) * cols[:, 2:3]
        bt_s[:, s * ES : (s + 1) * ES] = jnp.transpose(basis).astype(BF)
        q = nn(ohs, ab_s[0:ATOMS, :]) + nn(ohd, ab_s[ATOMS : 2 * ATOMS, :])
        return s, cols, q, nn(basis.astype(BF), wr_ref[...])

    def message(s, cols, q, radial):
        a = 1.0 + jnp.tanh(q)
        sil = q * a
        msg = (sil * radial).astype(BF)
        msg_s[s] = msg
        f_s[s] = (radial * (a + sil * (2.0 - a))).astype(BF)
        sg_s[s] = sil.astype(BF)
        m2 = nn(msg, wt_ref[...]).astype(BF)
        m2_s[s] = m2
        meta = meta_s[s]
        unit = geo_s[s][4:7]
        tc = 8.0 * meta[15:16, 256:384] + meta[15:16, 384:512]
        mixes = []
        for i in range(2):
            rows = slice(BLK * i, BLK * (i + 1))
            limit = jnp.concatenate([tc] * 4, axis=1) - float(TPB * i)
            tin = meta[2 + i : 3 + i, :]
            tout = jnp.where(lane_t < limit, meta[4 + i : 5 + i, :], -1.0)
            count = nt(hit(sub_t, tout), hit(sub_t, tin)) * cols[rows, 2:3]
            n_s[2 * s + i] = count
            gram = (
                cols[rows, 4:5] * unit[0:1, rows]
                + cols[rows, 5:6] * unit[1:2, rows]
                + cols[rows, 6:7] * unit[2:3, rows]
            )
            mix = count * gram
            tt_s[2 * s + i] = jnp.transpose(mix).astype(BF)
            mixes.append(mix.astype(BF))
        return s, msg, m2, mixes

    def update(s, msg, m2, mixes):
        for i in range(2):
            rows = slice(BLK * i, BLK * (i + 1))
            upd = msg[rows].astype(F32) + nn(mixes[i], m2[rows])
            upd_s[s * ES + BLK * i : s * ES + BLK * (i + 1), :] = upd.astype(BF)

    def staged(count, *stages):
        waiting = [None] * len(stages)
        for turn in range(count + len(stages) - 1):
            for k in reversed(range(len(stages))):
                if k == 0:
                    given = (turn,) if turn < count else None
                else:
                    given = waiting[k - 1]
                waiting[k] = None if given is None else stages[k](*given)

    for s in range(NG):
        geometry(s)
    h = h_s[...]
    loads[0].wait()
    ab_s[0:ATOMS, :] = (0.5 * nn(h, ws_ref[...])).astype(BF)
    loads[1].wait()
    ab_s[ATOMS : 2 * ATOMS, :] = (0.5 * nn(h, wd_ref[...])).astype(BF)
    for load in loads[2:]:
        load.wait()
    staged(NG, gather, message, update)

    we = we_ref[...].astype(F32)[0:1]
    ecot = (meta_s[0, 6:7, 128:144] + meta_s[0, 7:8, 128:144]) + meta_s[0, 8:9, 128:144]
    energies, slopes = [], []

    def collect(b):
        agg = nn(oht_s[ATOMS + 512 * b : ATOMS + 512 * (b + 1), :], upd_s[...]).astype(BF)
        aggb_s[512 * b : 512 * (b + 1), :] = agg
        return b, nn(agg, wo_ref[...])

    def settle(b, z):
        rows = slice(512 * b, 512 * (b + 1))
        sig = 0.5 + 0.5 * jnp.tanh(0.5 * z)
        out = z * sig
        x = h_s[rows, :].astype(F32) + out
        atom_energy = jnp.sum(x * we, axis=1, keepdims=True)
        places = lax.broadcasted_iota(jnp.int32, (512, 16), 1).astype(F32)
        member = jnp.where(places == gid_col[rows], 1.0, 0.0)
        energies.append(jnp.sum(member * atom_energy, axis=0, keepdims=True))
        cot = jnp.sum(member * ecot, axis=1, keepdims=True)
        cot_s[rows, :] = jnp.broadcast_to(cot, (512, 128))
        slopes.append(jnp.sum(x * cot, axis=0, keepdims=True))
        dz = (cot * we * (sig + out * (1.0 - sig))).astype(BF)
        dzb_s[rows, :] = dz
        ac_s[rows, :] = nt(dz, wo_ref[...]).astype(BF)
        return (b,)

    staged(1, collect, settle)
    energy_ref[...] = sum(energies[1:], energies[0])
    ge_s[...] = sum(slopes[1:], slopes[0])

    def fetch(s):
        return s, nn(ohd_s[s], ac_s[...])

    def mixed(s, ug):
        geo = geo_s[s]
        cols = jnp.transpose(geo)
        ugb = ug.astype(BF)
        m2 = m2_s[s]
        halves, grams = [], []
        for i in range(2):
            rows = slice(BLK * i, BLK * (i + 1))
            halves.append(nn(tt_s[2 * s + i], ugb[rows]).astype(BF))
            grams.append(n_s[2 * s + i] * nt(ugb[rows], m2[rows]))
        dm2 = jnp.concatenate(halves, axis=0)
        dm2_s[s * ES : (s + 1) * ES, :] = dm2
        return s, geo, cols, ug, dm2, grams

    def spread(s, geo, cols, ug, dm2, grams):
        edges = slice(s * ES, (s + 1) * ES)
        dmsg = ug + nn(dm2, wtt_s[...])
        dpre_s[edges, :] = (dmsg * f_s[s].astype(F32)).astype(BF)
        drad = (dmsg * sg_s[s].astype(F32)).astype(BF)
        drad_s[edges, :] = drad
        return s, geo, cols, drad, grams

    def turn_back(s, geo, cols, drad, grams):
        edges = slice(s * ES, (s + 1) * ES)
        turns = []
        for i in range(2):
            rows = slice(BLK * i, BLK * (i + 1))
            both = grams[i] + jnp.transpose(grams[i])
            turns.append(
                jnp.concatenate(
                    [jnp.sum(both * cols[rows, a : a + 1], axis=0, keepdims=True) for a in (4, 5, 6)], axis=0
                )
            )
        t = (cols[:, 3:4] - centers) * inv_width
        slope = nt(drad, wr_ref[...]) * (jnp.exp(-(t * t)) * (t * (-2.0 * inv_width)))
        ddist = jnp.sum(jnp.transpose(slope), axis=0, keepdims=True) * geo[2:3]
        unit = geo[4:7]
        du = jnp.concatenate(turns, axis=1)
        along = du * unit
        along = along[0:1] + along[1:2] + along[2:3]
        dv = geo[7:8] * (du - unit * along) + unit * ddist
        top = dv.astype(BF).astype(F32)
        dv_s[:, edges] = jnp.concatenate([top, dv - top, jnp.zeros((10, ES), F32)], axis=0).astype(BF)

    wtt_s[...] = jnp.transpose(wt_ref[...])
    staged(NG, fetch, mixed, spread, turn_back)

    own = pl.multiple_of(me * AT, AT)
    ohs_own = oht_s[pl.ds(own, AT), :]
    ohd_own = oht_s[pl.ds(ATOMS + own, AT), :]
    group = lax.div(my_slice, 4)
    block = pl.ds(pl.multiple_of(lax.rem(my_slice, 4) * 128, 128), 128)
    side = pl.ds(pl.multiple_of(group * ATOMS, ATOMS), ATOMS)
    rows_t = tn(h_s[:, block], oht_s[side, :]).astype(BF)
    sums = nn(jnp.concatenate([rows_t, ohs_own, ohd_own], axis=0), dpre_s[...])
    a_s[...] = 0.5 * sums[0:BLK]
    own_s_ref[...] = (0.5 * sums[BLK : 2 * BLK]).astype(BF)
    cot_ref[...] = cot_s[pl.ds(own, AT), :]
    pos = nt(dv_s[...], ohd_own - ohs_own)
    pos = pos[0:3] + pos[3:6]
    for i in range(3):
        pos_out_ref[i] = pos[i : i + 1]

    @pl.when(group == 0)
    def _():
        for_trip = [msg_s[s, :, block] for s in range(NG)]
        b_s[...] = tn(jnp.concatenate(for_trip, axis=0), dm2_s[...])

    @pl.when(group == 1)
    def _():
        b_s[...] = tn(aggb_s[:, block], dzb_s[...])

    r_s[...] = nn(bt_s[pl.ds(pl.multiple_of(my_slice * 16, 16), 16), :], drad_s[...])
    ge = ge_s[:, block]
    for u in range(4):
        for v in range(4):
            cols = slice(128 * v, 128 * v + 128)
            chunk = jnp.concatenate(
                [
                    a_s[32 * u : 32 * u + 32, cols],
                    b_s[32 * u : 32 * u + 32, cols],
                    r_s[4 * u : 4 * u + 4, cols],
                    ge,
                    jnp.zeros((CH - 69, 128), F32),
                ],
                axis=0,
            )
            pay_ref[lax.rem(u - my_u + 4, 4), v] = chunk.astype(BF)


def batch(me, part, u, own, other, ws, wd, wide, wt, wo):
    vm = pl.BlockSpec(memory_space=pltpu.VMEM)
    sm = pl.BlockSpec(memory_space=pltpu.SMEM)
    far = pl.BlockSpec(memory_space=pltpu.HBM)
    V = pltpu.VMEM
    return pl.pallas_call(
        main_kernel,
        out_shape=(
            jax.ShapeDtypeStruct((1, 16), F32),
            jax.ShapeDtypeStruct((3, 1, AT), F32),
            jax.ShapeDtypeStruct((2 * AT, D), BF),
            jax.ShapeDtypeStruct((AT, 128), F32),
            jax.ShapeDtypeStruct((4, 4, CH, 128), BF),
        ),
        in_specs=[sm] * 3 + [vm] * 8 + [far] * 2 + [vm] + [far] * 2,
        out_specs=(vm,) * 5,
        scratch_shapes=[
            V((ATOMS, D), BF),
            V((NG, 16, D), F32),
            V((2 * ATOMS, D), BF),
            V((16, ATOMS), BF),
            V((2 * ATOMS, EDGES), BF),
            V((NG, ES, ATOMS), BF),
            V((NG, 8, ES), F32),
            V((NG, ES, D), BF),
            V((NG, ES, D), BF),
            V((NG, ES, D), BF),
            V((NG, ES, D), BF),
            V((2 * NG, BLK, BLK), F32),
            V((2 * NG, BLK, BLK), BF),
            V((EDGES, D), BF),
            V((ATOMS, D), BF),
            V((ATOMS, D), BF),
            V((ATOMS, D), BF),
            V((ATOMS, 128), F32),
            V((1, D), F32),
            V((K, EDGES), BF),
            V((EDGES, D), BF),
            V((EDGES, D), BF),
            V((EDGES, D), BF),
            V((16, EDGES), BF),
            V((BLK, D), F32),
            V((BLK, D), F32),
            V((16, D), F32),
            V((D, D), BF),
            V((D, D), BF),
            V((D, D), BF),
            V((D, D), BF),
            pltpu.SemaphoreType.DMA((4,)),
            V((D, D), BF),
        ],
        compiler_params=pltpu.CompilerParams(vmem_limit_bytes=53760 * 1024),
        name="batch",
    )(me, part, u, *own, *other, ws, wd, wide, wt, wo)


def node_kernel(sums_ref, cot_ref, ws_ref, wd_ref, wide_ref, out_ref):
    out_ref[...] = (
        cot_ref[:, 0:1] * wide_ref[K : K + 16, :].astype(F32)[0:1]
        + nt(sums_ref[0:AT, :], ws_ref[...])
        + nt(sums_ref[AT : 2 * AT, :], wd_ref[...])
    )


def node(sums, cot, ws, wd, we):
    vm = pl.BlockSpec(memory_space=pltpu.VMEM)
    return pl.pallas_call(
        node_kernel,
        out_shape=jax.ShapeDtypeStruct((AT, D), F32),
        in_specs=[vm] * 5,
        out_specs=vm,
        compiler_params=pltpu.CompilerParams(vmem_limit_bytes=24 * 1024 * 1024),
        name="node",
    )(sums, cot, ws, wd, we)


def place_kernel(c, x_ref, y_ref, slice_ref, ref, *rest):
    gs_ref, gd_ref, gr_ref, gt_ref, go_ref, ge_ref, first, second, low, radial, energy, sems = rest[-12:]
    x, y, mine = x_ref[0], y_ref[0], slice_ref[0]
    pc = (mine & 1) ^ c
    my_u = jnp.where(pc == 0, x, y)

    for kz in range(4):

        def body(ku, carry, kz=kz):
            u = lax.rem(my_u - ku + 4, 4)
            rows = pl.ds(pl.multiple_of(u * 32, 32), 32)
            for v in range(4):
                cols = slice(128 * v, 128 * (v + 1))
                tile = ref[16 * ku + 4 * kz + v].astype(F32)
                first[kz, rows, cols] = tile[0:32]
                second[kz, rows, cols] = tile[32:64]
                low[4 * kz + u, :, cols] = tile[64:72]
            return carry

        lax.fori_loop(0, 4, body, 0, unroll=True)
        g = lax.bitwise_xor(mine, 2 * kz + c)
        block = pl.ds(pl.multiple_of((g & 3) * 128, 128), 128)

        def send(near, far, sem):
            pltpu.make_async_copy(near, far, sem).start()

        @pl.when(g < 4)
        def _():
            send(first.at[kz], gs_ref.at[block], sems.at[0, kz])
            send(second.at[kz], gt_ref.at[block], sems.at[1, kz])

        @pl.when(g >= 4)
        def _():
            send(first.at[kz], gd_ref.at[block], sems.at[0, kz])
            send(second.at[kz], go_ref.at[block], sems.at[1, kz])

        for u in range(4):
            radial[kz, 4 * u : 4 * u + 4, :] = low[4 * kz + u, 0:4, :]
        send(radial.at[kz], gr_ref.at[pl.ds(pl.multiple_of(g * 16, 16), 16)], sems.at[2, kz])

        @pl.when(g < 4)
        def _():
            energy[kz] = low[4 * kz, 4:5, 0:128]
            copy = pltpu.make_async_copy(energy.at[kz], ge_ref.at[:, block], sems.at[3, kz])
            copy.start()
            copy.wait()

    for kz in range(4):
        pltpu.make_async_copy(first.at[kz], gs_ref.at[0:128], sems.at[0, kz]).wait()
        pltpu.make_async_copy(second.at[kz], gt_ref.at[0:128], sems.at[1, kz]).wait()
        pltpu.make_async_copy(radial.at[kz], gr_ref.at[0:16], sems.at[2, kz]).wait()


def place(c, x, y, part, pieces, *before):
    vm = pl.BlockSpec(memory_space=pltpu.VMEM)
    sm = pl.BlockSpec(memory_space=pltpu.SMEM)
    far = pl.BlockSpec(memory_space=pl.ANY)
    big = jax.ShapeDtypeStruct((D, D), F32)
    return pl.pallas_call(
        functools.partial(place_kernel, c),
        out_shape=(big, big, jax.ShapeDtypeStruct((K, D), F32), big, big, jax.ShapeDtypeStruct((1, D), F32)),
        in_specs=[sm] * 3 + [vm] + [far] * len(before),
        out_specs=(far,) * 6,
        scratch_shapes=[
            pltpu.VMEM((4, 128, D), F32),
            pltpu.VMEM((4, 128, D), F32),
            pltpu.VMEM((16, 8, D), F32),
            pltpu.VMEM((4, 16, D), F32),
            pltpu.VMEM((4, 1, 128), F32),
            pltpu.SemaphoreType.DMA((4, 4)),
        ],
        input_output_aliases={4 + i: i for i in range(len(before))},
        compiler_params=pltpu.CompilerParams(vmem_limit_bytes=30 * 1024 * 1024),
        name="place",
    )(x, y, part, pieces, *before)


def moves(fn):
    pairs = []
    for zh in range(2):
        for x in range(4):
            for y in range(4):
                for zl in range(4):
                    for c in range(2):
                        u, v = (x, y) if c == 0 else (y, x)
                        zh2, u2, v2, zl2, c2 = fn(zh, u, v, zl, c)
                        x2, y2 = (u2, v2) if c == 0 else (v2, u2)
                        here = (zh * 16 + x * 4 + y) * 8 + zl * 2 + c
                        there = (zh2 * 16 + x2 * 4 + y2) * 8 + zl2 * 2 + c2
                        pairs.append((here, there))
    return pairs


def shift(value, zh=0, u=0, v=0, zl=0, c=0):
    def fn(zh_, u_, v_, zl_, c_):
        return zh_ ^ zh, (u_ + u) % 4, (v_ + v) % 4, zl_ ^ zl, c_ ^ c

    return lax.ppermute(value, AXES, moves(fn))


def join(*parts):
    return jnp.concatenate(parts, axis=0)


ORDER = (1, 3, 2)


def total(a, b, c, d):
    a, b, c, d = (part.astype(F32) for part in (a, b, c, d))
    return ((a + b) + (c + d)).astype(BF)


def per_device(
    node_feats,
    positions,
    edge_src,
    edge_dst,
    edge_count,
    trip_in,
    trip_out,
    trip_count,
    graph_ids,
    w_src,
    w_dst,
    w_radial,
    w_trip,
    w_out,
    w_energy,
    energy_cot,
):
    dp, graph = lax.axis_index("dp"), lax.axis_index("graph")
    zh, x, y = lax.shift_right_logical(dp, 4), lax.shift_right_logical(dp, 2) & 3, dp & 3
    core = graph & 1
    u = jnp.where(core == 0, x, y)
    part = graph ^ (6 * zh)
    me, x, y, u, part = (a.astype(jnp.int32).reshape(1) for a in (graph, x, y, u, part))
    piece = pack(
        me,
        node_feats[0],
        jnp.swapaxes(positions, 0, 1),
        edge_src,
        edge_dst,
        edge_count,
        trip_in,
        trip_out,
        trip_count,
        graph_ids,
        energy_cot,
    )
    wide = jnp.concatenate([w_radial, w_energy.reshape(1, D), jnp.zeros((15, D), BF)], axis=0)
    own = [piece] + [shift(piece, zl=k) for k in (1, 2, 3)]
    other = [shift(p, c=1) for p in own]
    energy, pos_grad, sums, cot, payload = batch(
        me, part, u, own, other, w_src, w_dst, wide, w_trip, w_out
    )
    node_grad = node(sums, cot, w_src, w_dst, wide)
    one, three, two = [shift(payload[k], u=k) for k in ORDER]
    held = total(payload[0], two, one, three)
    one, three, two = [shift(held, v=k) for k in ORDER]
    held = total(held, two, one, three)
    held = (held.astype(F32) + shift(held, zh=1, zl=3).astype(F32)).astype(BF)
    held = join(held, *[shift(held, zl=k) for k in (1, 2, 3)])
    one, three, two = [shift(held, u=k) for k in ORDER]
    one, three, two, node_grad = lax.optimization_barrier((one, three, two, node_grad))
    held = join(held, one, two, three)
    other = shift(held, c=1)
    gs, gd, gr, gt, go, ge = place(1, x, y, part, other, *place(0, x, y, part, held))
    return (energy, jnp.swapaxes(pos_grad, 0, 1), node_grad[None], gs, gd, gr, gt, go, ge.reshape(D))


def solution(mesh):
    placed = (
        P("dp", "graph", None),
        P("dp", None, "graph"),
        P("dp", "graph"),
        P("dp", "graph"),
        P("dp", "graph"),
        P("dp", "graph"),
        P("dp", "graph"),
        P("dp", "graph"),
        P("dp", "graph"),
        P(),
        P(),
        P(),
        P(),
        P(),
        P(),
        P("dp", None),
    )
    return jax.shard_map(
        per_device,
        mesh=mesh,
        in_specs=placed,
        out_specs=(
            P("dp", None),
            P("dp", None, "graph"),
            P("dp", "graph", None),
            P(),
            P(),
            P(),
            P(),
            P(),
            P(),
        ),
        check_vma=False,
    )
```
